32 devices in a mesh: dp: 4 (over y, x), seq: 8 (over z, core).
Axes of the slice: x: 2, y: 2, z: 4, core: 2. Of those that a mesh axis runs over, the one named last changes fastest.
Arguments:
- inputs: bfloat16 [32, 1024, 1024], P('dp', 'seq'), may hold values from -6 to 6
- cotangent: bfloat16 [32, 1024, 1024], P('dp', 'seq'), may hold values from -6 to 6
- lengths: int32 [32], P('dp'), may hold values from 64 to 1024, as said below
- norm_gain: bfloat16 [2, 1024], replicated, may hold values from 0.5 to 1.5
- norm_shift: bfloat16 [2, 1024], replicated, may hold values from -3 to 3
- query_key_value_weight: bfloat16 [1024, 3072], replicated, may hold values from -0.1875 to 0.1875
- output_projection_weight: bfloat16 [1024, 1024], replicated, may hold values from -0.75 to 0.75
- first_feedforward_weight: bfloat16 [1024, 4096], replicated, may hold values from -0.1875 to 0.1875
- second_feedforward_weight: bfloat16 [4096, 1024], replicated, may hold values from -0.09375 to 0.09375
- biases: bfloat16 [8192], replicated, may hold values from -3 to 3
- down_model: float32 [3, 1024, 4], replicated, may hold values from -0.1875 to 0.1875
- down_hidden: float32 [4096, 4], replicated, may hold values from -0.09375 to 0.09375
- query_key_value_upward: float32 [4, 3072], replicated, may hold values from -0.12 to 0.12
- hidden_adapter_upward: float32 [4, 4096], replicated, may hold values from -0.12 to 0.12
- model_adapter_upward: float32 [2, 4, 1024], replicated, may hold values from -0.12 to 0.12
- row_down_model: float32 [3, 1024], replicated, may hold values from 98304 to 1572864
- col_down_model: float32 [3, 4], replicated, may hold values from 98304 to 1572864
- row_down_hidden: float32 [4096], replicated, may hold values from 98304 to 1572864
- col_down_hidden: float32 [4], replicated, may hold values from 98304 to 1572864
- row_up_qkv: float32 [4], replicated, may hold values from 98304 to 1572864
- col_up_qkv: float32 [3072], replicated, may hold values from 98304 to 1572864
- row_up_hidden: float32 [4], replicated, may hold values from 98304 to 1572864
- col_up_hidden: float32 [4096], replicated, may hold values from 98304 to 1572864
- row_up_model: float32 [2, 4], replicated, may hold values from 98304 to 1572864
- col_up_model: float32 [2, 1024], replicated, may hold values from 98304 to 1572864
Outputs:
- output: bfloat16 [32, 1024, 1024], P('dp', 'seq')
- input_grad: bfloat16 [32, 1024, 1024], P('dp', 'seq')
- grad_down_model: float32 [3, 1024, 4], replicated
- grad_down_hidden: float32 [4096, 4], replicated
- grad_up_qkv: float32 [4, 3072], replicated
- grad_up_hidden: float32 [4, 4096], replicated
- grad_up_model: float32 [2, 4, 1024], replicated
- new_down_model: float32 [3, 1024, 4], replicated
- new_down_hidden: float32 [4096, 4], replicated
- new_up_qkv: float32 [4, 3072], replicated
- new_up_hidden: float32 [4, 4096], replicated
- new_up_model: float32 [2, 4, 1024], replicated
- new_row_down_model: float32 [3, 1024], replicated
- new_row_down_hidden: float32 [4096], replicated
- new_row_up_qkv: float32 [4], replicated
- new_row_up_hidden: float32 [4], replicated
- new_row_up_model: float32 [2, 4], replicated
- new_col_down_model: float32 [3, 4], replicated
- new_col_down_hidden: float32 [4], replicated
- new_col_up_qkv: float32 [3072], replicated
- new_col_up_hidden: float32 [4096], replicated
- new_col_up_model: float32 [2, 1024], replicated
The draws below stay inside these ranges and needn't reach their ends.
Inputs may be any that keep to these rules, and one draw needn't show every extreme that they name: `lengths`: in each aligned block of 8 rows (the rows of one index of dp) one row has length exactly 1024.
All inputs are finite; a program needn't handle non-finite values.
Results may differ from the reference program's by a relative error of at most 0.012.
Values may be sent and summed in bfloat16 or wider, within the bound.
A program may use at most 192 MiB of HBM per device.

```python
import math
from functools import partial
import jax
import jax.numpy as jnp
from jax import lax

D = 1024
HEADS = 16
HEAD_DIM = 64
FF = 4096
RANK = 4
ROW_LEN = 1024
ROWS = 8
STEP = 10
BATCH = 32


def draw_lengths(key, part):
    key = jax.random.fold_in(key, 11)
    base_key, pick_key = jax.random.split(key)
    groups = BATCH // ROWS
    base = jax.random.randint(base_key, (BATCH,), ROW_LEN // 16, ROW_LEN + 1)
    pick = jax.random.randint(pick_key, (groups,), 0, ROWS)
    index = jnp.arange(BATCH)
    full = index % ROWS == pick[index // ROWS]
    return jnp.where(full, ROW_LEN, base).astype(jnp.int32)


def levels(own_key, extent, pieces, least, high):
    def one(dim, blocks):
        draws = jax.random.uniform(jax.random.fold_in(jax.random.fold_in(own_key, 6), dim), (blocks,), jnp.float32, least / len(pieces), high / len(pieces))
        return jnp.repeat(jnp.exp(draws), extent[dim] // blocks).reshape((-1,) + (1,) * (len(extent) - dim - 1))

    level = one(*pieces[0])
    for cut in pieces[1:]:
        level = level * one(*cut)
    return level


def bell_draw(key, shape, scale, bound, cuts=(), kind=jnp.bfloat16):
    drawn = scale * jax.random.normal(key, shape, jnp.float32)
    if cuts:
        drawn = drawn * levels(key, shape, cuts, -0.22, 0.18)
    return jnp.clip(drawn, -bound, bound).astype(kind)


def setup_inputs(seed: int = 0) -> dict:
    streams_of = jax.random.split(jax.random.key(seed), 26)
    inputs = bell_draw(streams_of[0], (BATCH, ROW_LEN, D), 1.0, 6.0, ((0, 4), (1, 8)))
    cotangent = bell_draw(streams_of[1], (BATCH, ROW_LEN, D), 1.0, 6.0, ((0, 4), (1, 8)))
    lengths = draw_lengths(jax.random.fold_in(streams_of[25], 71), 0)
    norm_gain = jnp.clip(1.0 + 0.1 * jax.random.normal(streams_of[3], (2, D), jnp.float32), 0.5, 1.5).astype(jnp.bfloat16)
    norm_shift = bell_draw(streams_of[4], (2, D), 0.5, 3.0)
    query_key_value_weight = bell_draw(streams_of[5], (D, 3 * D), D ** -0.5, 0.1875)
    output_projection_weight = bell_draw(streams_of[6], (D, D), (D // 16) ** -0.5, 0.75)
    first_feedforward_weight = bell_draw(streams_of[7], (D, FF), D ** -0.5, 0.1875)
    second_feedforward_weight = bell_draw(streams_of[8], (FF, D), FF ** -0.5, 0.09375)
    biases = bell_draw(streams_of[9], (4 * D + FF,), 0.5, 3.0)
    down_model = bell_draw(streams_of[10], (3, D, RANK), D ** -0.5, 0.1875, (), jnp.float32)
    down_hidden = bell_draw(streams_of[11], (FF, RANK), FF ** -0.5, 0.09375, (), jnp.float32)
    query_key_value_upward = bell_draw(streams_of[12], (RANK, 3 * D), 0.02, 0.12, (), jnp.float32)
    hidden_adapter_upward = bell_draw(streams_of[13], (RANK, FF), 0.02, 0.12, (), jnp.float32)
    model_adapter_upward = bell_draw(streams_of[14], (2, RANK, D), 0.02, 0.12, (), jnp.float32)
    row_down_model = jnp.clip(jnp.exp(jax.random.uniform(streams_of[15], (3, D), jnp.float32, math.log(98304.0), math.log(1572864))), 98304.0, 1572864)
    col_down_model = jnp.clip(jnp.exp(jax.random.uniform(streams_of[16], (3, RANK), jnp.float32, math.log(98304.0), math.log(1572864))), 98304.0, 1572864)
    row_down_hidden = jnp.clip(jnp.exp(jax.random.uniform(streams_of[17], (FF,), jnp.float32, math.log(98304.0), math.log(1572864))), 98304.0, 1572864)
    col_down_hidden = jnp.clip(jnp.exp(jax.random.uniform(streams_of[18], (RANK,), jnp.float32, math.log(98304.0), math.log(1572864))), 98304.0, 1572864)
    row_up_qkv = jnp.clip(jnp.exp(jax.random.uniform(streams_of[19], (RANK,), jnp.float32, math.log(98304.0), math.log(1572864))), 98304.0, 1572864)
    col_up_qkv = jnp.clip(jnp.exp(jax.random.uniform(streams_of[20], (3 * D,), jnp.float32, math.log(98304.0), math.log(1572864))), 98304.0, 1572864)
    row_up_hidden = jnp.clip(jnp.exp(jax.random.uniform(streams_of[21], (RANK,), jnp.float32, math.log(98304.0), math.log(1572864))), 98304.0, 1572864)
    col_up_hidden = jnp.clip(jnp.exp(jax.random.uniform(streams_of[22], (FF,), jnp.float32, math.log(98304.0), math.log(1572864))), 98304.0, 1572864)
    row_up_model = jnp.clip(jnp.exp(jax.random.uniform(streams_of[23], (2, RANK), jnp.float32, math.log(98304.0), math.log(1572864))), 98304.0, 1572864)
    col_up_model = jnp.clip(jnp.exp(jax.random.uniform(streams_of[24], (2, D), jnp.float32, math.log(98304.0), math.log(1572864))), 98304.0, 1572864)
    return dict(inputs=inputs, cotangent=cotangent, lengths=lengths, norm_gain=norm_gain, norm_shift=norm_shift, query_key_value_weight=query_key_value_weight, output_projection_weight=output_projection_weight, first_feedforward_weight=first_feedforward_weight, second_feedforward_weight=second_feedforward_weight, biases=biases, down_model=down_model, down_hidden=down_hidden, query_key_value_upward=query_key_value_upward, hidden_adapter_upward=hidden_adapter_upward, model_adapter_upward=model_adapter_upward, row_down_model=row_down_model, col_down_model=col_down_model, row_down_hidden=row_down_hidden, col_down_hidden=col_down_hidden, row_up_qkv=row_up_qkv, col_up_qkv=col_up_qkv, row_up_hidden=row_up_hidden, col_up_hidden=col_up_hidden, row_up_model=row_up_model, col_up_model=col_up_model)


@jax.custom_vjp
def lowrank_rows(v):
    return lax.optimization_barrier(v.astype(jnp.bfloat16)).astype(jnp.float32)

@jax.custom_vjp
def low_back(v):
    return v

def low_keep(v):
    return (lowrank_rows(v), None)

def low_pass(kept, grad):
    return (grad,)

def back_keep(v):
    return (v, None)

def back_low(kept, grad):
    return (lowrank_rows(grad),)
lowrank_rows.defvjp(low_keep, low_pass)
low_back.defvjp(back_keep, back_low)
NORM_EPS = 1e-05
ADAPTER_SCALE = 8.0
STAT_EPS = 1e-30
CLIP_LEVEL = 1.0
RATE = 0.3
DECAY_WEIGHT = 0.01
MASKED = -1e+30
HIGH = lax.Precision.HIGHEST

def product_result(left, right):
    return jnp.dot(left, right, precision=HIGH)

def normalize(values, gain, shift):
    centered = values - lax.optimization_barrier(jnp.mean(values, axis=-1, keepdims=True))
    spread = lax.optimization_barrier(jnp.mean(centered * centered, axis=-1, keepdims=True))
    return centered * lax.rsqrt(spread + NORM_EPS) * gain + shift

def head_attention(lengths, parts):
    query, keys, values = parts
    scores = jnp.einsum('nqd,nkd->nqk', query, keys, precision=HIGH) * HEAD_DIM ** (-0.5)
    scores = low_back(scores)
    position = jnp.arange(ROW_LEN)
    valid = (position[None, :] <= position[:, None])[None] & (position[None, None, :] < lengths[:, None, None])
    scores = jnp.where(valid, scores, MASKED)
    top = lax.optimization_barrier(jnp.max(scores, axis=-1, keepdims=True))
    weights = jnp.exp(scores - top)
    weights = weights / lax.optimization_barrier(jnp.sum(weights, axis=-1, keepdims=True))
    return jnp.einsum('nqk,nkd->nqd', lowrank_rows(weights), values, precision=HIGH)

def forward(frozen, lengths, tokens, adapters):
    norm_gain, norm_shift, query_key_value_weight, output_projection_weight, first_feedforward_weight, second_feedforward_weight, biases = frozen
    down_model, down_hidden, query_key_value_upward, hidden_adapter_upward, model_adapter_upward = adapters
    count = tokens.shape[0]
    flat = tokens.reshape(count * ROW_LEN, D)
    query_bias = biases[0:D]
    value_bias = biases[D:2 * D]
    projection_bias = biases[2 * D:3 * D]
    expand_bias_vector = biases[3 * D:3 * D + FF]
    contract_bias_vector = biases[3 * D + FF:4 * D + FF]
    query_key_value_bias = jnp.concatenate([query_bias, jnp.zeros_like(query_bias), value_bias])
    normalized_rows = lowrank_rows(normalize(flat, norm_gain[0], norm_shift[0]))
    narrowed_rows = lowrank_rows(low_back(product_result(normalized_rows, lowrank_rows(down_model[0]))))
    mixed_rows = product_result(normalized_rows, query_key_value_weight) + query_key_value_bias + ADAPTER_SCALE * product_result(narrowed_rows, lowrank_rows(query_key_value_upward))
    mixed_rows = lowrank_rows(low_back(mixed_rows))
    heads = mixed_rows.reshape(count, ROW_LEN, 3, HEADS, HEAD_DIM).transpose(2, 3, 0, 1, 4)
    attended_rows = lax.map(jax.checkpoint(partial(head_attention, lengths)), (heads[0], heads[1], heads[2]))
    attended_rows = attended_rows.transpose(1, 2, 0, 3).reshape(count * ROW_LEN, D)
    attended_rows = lowrank_rows(low_back(attended_rows))
    narrowed_rows = lowrank_rows(low_back(product_result(attended_rows, lowrank_rows(down_model[1]))))
    branch_path = product_result(attended_rows, output_projection_weight) + projection_bias + ADAPTER_SCALE * product_result(narrowed_rows, lowrank_rows(model_adapter_upward[0]))
    middle = flat + low_back(branch_path)
    normalized_rows = lowrank_rows(normalize(middle, norm_gain[1], norm_shift[1]))
    narrowed_rows = lowrank_rows(low_back(product_result(normalized_rows, lowrank_rows(down_model[2]))))
    hidden_activation = product_result(normalized_rows, first_feedforward_weight) + expand_bias_vector + ADAPTER_SCALE * product_result(narrowed_rows, lowrank_rows(hidden_adapter_upward))
    hidden_activation = lowrank_rows(jax.nn.gelu(low_back(hidden_activation), approximate=True))
    narrowed_rows = lowrank_rows(low_back(product_result(hidden_activation, lowrank_rows(down_hidden))))
    branch_path = product_result(hidden_activation, second_feedforward_weight) + contract_bias_vector + ADAPTER_SCALE * product_result(narrowed_rows, lowrank_rows(model_adapter_upward[1]))
    return (middle + low_back(branch_path)).reshape(count, ROW_LEN, D)

def factored(grad, weight_matrix, row, col):
    decay = 1.0 - STEP ** (-0.8)
    squares = grad * grad + STAT_EPS
    new_row = decay * row + (1.0 - decay) * lax.optimization_barrier(jnp.mean(squares, axis=-1))
    new_col = decay * col + (1.0 - decay) * lax.optimization_barrier(jnp.mean(squares, axis=-2))
    second = new_row[..., :, None] * new_col[..., None, :] / lax.optimization_barrier(jnp.mean(new_row, axis=-1))[..., None, None]
    unit = grad * lax.rsqrt(second)
    level = jnp.sqrt(lax.optimization_barrier(jnp.mean(unit * unit, axis=(-2, -1), keepdims=True)))
    unit = unit / jnp.maximum(1.0, level / CLIP_LEVEL)
    rate = RATE * jnp.sqrt(lax.optimization_barrier(jnp.mean(weight_matrix * weight_matrix, axis=(-2, -1), keepdims=True)))
    return (weight_matrix - rate * (unit + DECAY_WEIGHT * weight_matrix), new_row, new_col)

def reference(inputs, cotangent, lengths, norm_gain, norm_shift, query_key_value_weight, output_projection_weight, first_feedforward_weight, second_feedforward_weight, biases, down_model, down_hidden, query_key_value_upward, hidden_adapter_upward, model_adapter_upward, row_down_model, col_down_model, row_down_hidden, col_down_hidden, row_up_qkv, col_up_qkv, row_up_hidden, col_up_hidden, row_up_model, col_up_model):
    frozen = tuple((item.astype(jnp.float32) for item in (norm_gain, norm_shift, query_key_value_weight, output_projection_weight, first_feedforward_weight, second_feedforward_weight, biases)))
    adapters = (down_model, down_hidden, query_key_value_upward, hidden_adapter_upward, model_adapter_upward)
    groups = BATCH // ROWS
    stacked = (inputs.reshape(groups, ROWS, ROW_LEN, D), cotangent.reshape(groups, ROWS, ROW_LEN, D), lengths.reshape(groups, ROWS))

    def group_step(totals, item):
        block_in, block_grad, block_len = item
        run = partial(forward, frozen, block_len)
        result, pull = jax.vjp(run, block_in.astype(jnp.float32), adapters)
        position = jnp.arange(ROW_LEN)
        keep = (position[None, :] < block_len[:, None]).astype(jnp.float32)[:, :, None]
        input_grad, adapter_grad = pull(block_grad.astype(jnp.float32) * keep)
        totals = jax.tree.map(lambda left, right: left + right, totals, adapter_grad)
        return (totals, (result.astype(jnp.bfloat16), input_grad.astype(jnp.bfloat16)))
    zeros = jax.tree.map(jnp.zeros_like, adapters)
    totals, (output, input_grad) = lax.scan(group_step, zeros, stacked)
    output = output.reshape(BATCH, ROW_LEN, D)
    input_grad = input_grad.reshape(BATCH, ROW_LEN, D)
    grad_dm, grad_dh, grad_uq, grad_uh, grad_um = totals
    new_dm, row_dm, col_dm = factored(grad_dm, down_model, row_down_model, col_down_model)
    new_dh, row_dh, col_dh = factored(grad_dh, down_hidden, row_down_hidden, col_down_hidden)
    new_uq, row_uq, col_uq = factored(grad_uq, query_key_value_upward, row_up_qkv, col_up_qkv)
    new_uh, row_uh, col_uh = factored(grad_uh, hidden_adapter_upward, row_up_hidden, col_up_hidden)
    new_um, row_um, col_um = factored(grad_um, model_adapter_upward, row_up_model, col_up_model)
    return (output, input_grad, grad_dm, grad_dh, grad_uq, grad_uh, grad_um, new_dm, new_dh, new_uq, new_uh, new_um, row_dm, row_dh, row_uq, row_uh, row_um, col_dm, col_dh, col_uq, col_uh, col_um)
```

```python
from functools import partial

import jax
import jax.numpy as jnp
from jax import lax
from jax.experimental import pallas as pl
from jax.experimental.pallas import tpu as pltpu
from jax.sharding import PartitionSpec as P

HEADS = 16
HEAD_DIM = 64
STEP = 10


NORM_EPS = 1e-05
ADAPTER_SCALE = 8.0
STAT_EPS = 1e-30
CLIP_LEVEL = 1.0
RATE = 0.3
DECAY_WEIGHT = 0.01
MASKED = -1e30


def as_sent(array):

    def short(part):
        return part.astype(jnp.bfloat16) if part.dtype == jnp.float32 else part

    return jax.tree.map(short, array)


def normalize(values, gain, shift):
    centered = values - jnp.mean(values, axis=-1, keepdims=True)
    spread = jnp.mean(centered * centered, axis=-1, keepdims=True)
    scaled = lax.rsqrt(spread + NORM_EPS)
    unit = centered * scaled
    return (unit * gain + shift, unit, scaled)


def normalize_back(grad, unit, scaled, gain):
    gained = grad * gain
    return scaled * (
        gained
        - jnp.mean(gained, axis=-1, keepdims=True)
        - unit * jnp.mean(gained * unit, axis=-1, keepdims=True)
    )


def matrix_multiply(left, right):
    return jnp.dot(left, right, preferred_element_type=jnp.float32)


def inner_product(left, right):
    return jnp.einsum("tr,tc->rc", left, right, preferred_element_type=jnp.float32)


def compared_with(left, right):
    return jnp.einsum("tc,rc->tr", left, right, preferred_element_type=jnp.float32)


def adapted(source_rows, weight_matrix, bias_vector, down, upward_matrix):
    narrowed_rows = matrix_multiply(source_rows, down).astype(jnp.bfloat16)
    return (
        matrix_multiply(source_rows, weight_matrix)
        + bias_vector
        + ADAPTER_SCALE * matrix_multiply(narrowed_rows, upward_matrix),
        narrowed_rows,
    )


def adapted_back(gradient_lowrank, source_rows, weight_matrix, down, upward_matrix, narrowed_rows):
    gradient_upward = ADAPTER_SCALE * inner_product(narrowed_rows, gradient_lowrank)
    gradient_narrowed = (ADAPTER_SCALE * compared_with(gradient_lowrank, upward_matrix)).astype(
        jnp.bfloat16
    )
    grad_down = inner_product(source_rows, gradient_narrowed)
    grad_source = compared_with(gradient_lowrank, weight_matrix) + compared_with(
        gradient_narrowed, down
    )
    return (grad_source, grad_down, gradient_upward)


def score_block(operand):
    query, keys = operand
    return jnp.einsum("gqe,gke->gqk", query, keys, preferred_element_type=jnp.float32)


def mix_block(operand):
    weights, values = operand
    return jnp.einsum("gqk,gke->gqe", weights, values, preferred_element_type=jnp.float32)


def spread_block(operand):
    weights, queries = operand
    return jnp.einsum("gqk,gqe->gke", weights, queries, preferred_element_type=jnp.float32)


def masked_scores(query, keys, spots, length):
    total = keys.shape[1]
    size = min(512, total)
    reach = jnp.minimum(length, jnp.max(spots) + 1)
    places = jnp.arange(total)
    valid = (places[None, :] <= spots[:, None]) & (places[None, :] < length)
    pieces = []
    for begin in range(0, total, size):
        pieces.append(score_block((query, keys[:, begin : begin + size])))
    scores = jnp.concatenate(pieces, axis=-1) * query.shape[-1] ** (-0.5)
    return (jnp.where(valid[None], scores, MASKED), reach, size)


def attend(query, keys, values, spots, length):
    scores, reach, size = masked_scores(query, keys, spots, length)
    top = jnp.max(scores, axis=-1, keepdims=True)
    weights = jnp.exp(scores - top)
    summed = jnp.sum(weights, axis=-1, keepdims=True)
    probs = (weights / summed).astype(jnp.bfloat16)
    result = jnp.zeros(query.shape, jnp.float32)
    for begin in range(0, keys.shape[1], size):
        operand = (probs[:, :, begin : begin + size], values[:, begin : begin + size])
        result = result + mix_block(operand)
    return (result, (top + jnp.log(summed))[..., 0])


def attend_back(query, keys, values, spots, length, grad_rows, lse):
    scores, reach, size = masked_scores(query, keys, spots, length)
    probs = jnp.exp(scores - lse[..., None])
    pieces = []
    for begin in range(0, keys.shape[1], size):
        pieces.append(score_block((grad_rows, values[:, begin : begin + size])))
    dprob = jnp.concatenate(pieces, axis=-1)
    delta = jnp.sum(probs * dprob, axis=-1, keepdims=True)
    dscore = (probs * (dprob - delta)).astype(jnp.bfloat16)
    probs_low = probs.astype(jnp.bfloat16)
    scale = query.shape[-1] ** (-0.5)
    grad_query = jnp.zeros(query.shape, jnp.float32)
    key_parts = []
    value_parts = []
    for begin in range(0, keys.shape[1], size):
        grad_query = grad_query + mix_block(
            (dscore[:, :, begin : begin + size], keys[:, begin : begin + size])
        )
        key_parts.append(spread_block((dscore[:, :, begin : begin + size], query)))
        value_parts.append(spread_block((probs_low[:, :, begin : begin + size], grad_rows)))
    return (
        grad_query * scale,
        jnp.concatenate(key_parts, axis=1) * scale,
        jnp.concatenate(value_parts, axis=1),
    )


def heads_split(triple):
    return tuple((jnp.transpose(triple[:, index], (1, 0, 2)) for index in range(3)))


def head_forward(skip, item):
    triple, length = item
    spots = jnp.arange(triple.shape[0])
    query, keys, values = heads_split(triple)
    result, lse = attend(query, keys, values, spots, length)
    return (jnp.transpose(result, (1, 0, 2)).astype(jnp.bfloat16), lse)


def head_backward(skip, item):
    triple, grad_rows, lse, length = item
    spots = jnp.arange(triple.shape[0])
    query, keys, values = heads_split(triple)
    grads = attend_back(
        query, keys, values, spots, length, jnp.transpose(grad_rows, (1, 0, 2)), lse
    )
    return jnp.stack(grads, axis=0).transpose(2, 0, 1, 3).astype(jnp.bfloat16)


def factored(grad, weight_matrix, row, col):
    decay = 1.0 - STEP ** (-0.8)
    squares = grad * grad + STAT_EPS
    new_row = decay * row + (1.0 - decay) * jnp.mean(squares, axis=-1)
    new_col = decay * col + (1.0 - decay) * jnp.mean(squares, axis=-2)
    second = (
        new_row[..., :, None] * new_col[..., None, :] / jnp.mean(new_row, axis=-1)[..., None, None]
    )
    unit = grad * lax.rsqrt(second)
    level = jnp.sqrt(jnp.mean(unit * unit, axis=(-2, -1), keepdims=True))
    unit = unit / jnp.maximum(1.0, level / CLIP_LEVEL)
    rate = RATE * jnp.sqrt(jnp.mean(weight_matrix * weight_matrix, axis=(-2, -1), keepdims=True))
    return (weight_matrix - rate * (unit + DECAY_WEIGHT * weight_matrix), new_row, new_col)


LOG2E = 1.4426950408889634
TILE = 256
NT = (((1,), (1,)), ((), ()))
TN = (((0,), (0,)), ((), ()))


def dotf(a, b, dims=(((1,), (0,)), ((), ()))):
    return lax.dot_general(a, b, dims, preferred_element_type=jnp.float32)


def triple(value):
    high = value.astype(jnp.bfloat16)
    rest = value - high.astype(jnp.float32)
    mid = rest.astype(jnp.bfloat16)
    low = (rest - mid.astype(jnp.float32)).astype(jnp.bfloat16)
    return high, mid, low


def attention_forward_kernel(length_ref, q_ref, k_ref, v_ref, out_ref, lse_ref):
    total = q_ref.shape[0]
    wide = q_ref.shape[1]
    half = wide // 2
    length = length_ref[0]
    lane = lax.broadcasted_iota(jnp.int32, (total, wide), 1)
    spot = lax.broadcasted_iota(jnp.int32, (total, wide), 0)
    bias = jnp.where(spot < length, 0.0, MASKED).astype(jnp.bfloat16)
    scale = half ** (-0.5)
    one = jnp.ones((total, wide), jnp.bfloat16)
    zero = jnp.zeros((total, wide), jnp.bfloat16)
    q = q_ref[...] * jnp.asarray(scale, jnp.bfloat16)
    k = k_ref[...]
    v = v_ref[...]
    row = lax.broadcasted_iota(jnp.int32, (TILE, TILE), 0)
    col = lax.broadcasted_iota(jnp.int32, (TILE, TILE), 1)
    outs = []
    lses = []
    for head in range(2):
        own = (lane < half) if head == 0 else (lane >= half)
        spare = half if head == 0 else 0
        qh = jnp.where(own, q, jnp.where(lane == spare, one, zero))
        kh = jnp.where(own, k, jnp.where(lane == spare, bias, zero))
        vh = jnp.where(own, v, one)
        parts = []
        lparts = []
        for begin in range(0, total, TILE):
            end = begin + TILE
            scores = dotf(qh[begin:end], kh[:end], NT)
            diag = jnp.where(col <= row, scores[:, begin:], MASKED)
            if begin:
                scores = jnp.concatenate([scores[:, :begin], diag], axis=1)
            else:
                scores = diag
            top = jnp.max(scores, axis=-1, keepdims=True)
            weights = jnp.exp2((scores - top) * LOG2E).astype(jnp.bfloat16)
            mixed = dotf(weights, vh[:end])
            summed = mixed[:, spare : spare + 1]
            parts.append(mixed * (1.0 / summed))
            lparts.append(jnp.broadcast_to(top + jnp.log(summed), (TILE, wide)))
        outs.append(jnp.concatenate(parts, axis=0))
        lses.append(jnp.concatenate(lparts, axis=0))
    out_ref[...] = jnp.where(lane < half, outs[0], outs[1]).astype(jnp.bfloat16)
    lse_ref[0] = jnp.where(lane < half, lses[1], lses[0])


def attention_forward(length, mixed):
    total = mixed.shape[0]
    width = mixed.shape[1] // 3
    pairs = width // 128

    def at(offset):
        return pl.BlockSpec((total, 128), lambda p, s: (0, offset + p))

    return pl.pallas_call(
        attention_forward_kernel,
        grid_spec=pltpu.PrefetchScalarGridSpec(
            num_scalar_prefetch=1,
            grid=(pairs,),
            in_specs=[at(0), at(pairs), at(2 * pairs)],
            out_specs=[
                at(0),
                pl.BlockSpec((1, total, 128), lambda p, s: (p, 0, 0)),
            ],
        ),
        out_shape=[
            jax.ShapeDtypeStruct((total, width), jnp.bfloat16),
            jax.ShapeDtypeStruct((pairs, total, 128), jnp.float32),
        ],
        compiler_params=pltpu.CompilerParams(vmem_limit_bytes=48 * 2**20),
        name="attention_forward",
    )(length, mixed, mixed, mixed)


def attention_backward_kernel(
    length_ref, q_ref, k_ref, v_ref, o_ref, g_ref, lse_ref, dq_ref, dk_ref, dv_ref, dq_acc
):
    total = q_ref.shape[0]
    wide = q_ref.shape[1]
    half = wide // 2
    length = length_ref[0]
    lane = lax.broadcasted_iota(jnp.int32, (total, wide), 1)
    spot = lax.broadcasted_iota(jnp.int32, (total, wide), 0)
    scale = half ** (-0.5)
    one = jnp.ones((total, wide), jnp.bfloat16)
    zero = jnp.zeros((total, wide), jnp.bfloat16)
    q = q_ref[...] * jnp.asarray(scale, jnp.bfloat16)
    k = k_ref[...]
    v = v_ref[...]
    g = g_ref[...]
    product = g.astype(jnp.float32) * o_ref[...].astype(jnp.float32)
    neglse = jnp.where(spot < length, -lse_ref[0], MASKED)
    row = lax.broadcasted_iota(jnp.int32, (TILE, TILE), 0)
    col = lax.broadcasted_iota(jnp.int32, (TILE, TILE), 1)
    l_high, l_mid, l_low = triple(neglse)
    dks = []
    dvs = []
    for head in range(2):
        own = (lane < half) if head == 0 else (lane >= half)
        spare = half if head == 0 else 0
        delta = -jnp.sum(jnp.where(own, product, 0.0), axis=-1, keepdims=True)
        d_high, d_mid, d_low = triple(jnp.broadcast_to(delta, (total, wide)))

        def extra(a, b, c):
            return jnp.where(
                lane == spare, a, jnp.where(lane == spare + 1, b, jnp.where(lane == spare + 2, c, zero))
            )

        qh = jnp.where(own, q, extra(l_high, l_mid, l_low))
        kh = jnp.where(own, k, one)
        gh = jnp.where(own, g, extra(d_high, d_mid, d_low))
        vh = jnp.where(own, v, one)
        kz = jnp.where(own, k, zero)
        dk_parts = []
        dv_parts = []
        for begin in range(0, total, TILE):
            end = begin + TILE
            scores = dotf(kh[begin:end], qh[begin:], NT)
            weights = jnp.exp2(scores * LOG2E)
            diag = jnp.where(row <= col, weights[:, :TILE], 0.0)
            if end < total:
                weights = jnp.concatenate([diag, weights[:, TILE:]], axis=1)
            else:
                weights = diag
            dprob = dotf(vh[begin:end], gh[begin:], NT)
            dscore = (weights * dprob).astype(jnp.bfloat16)
            dv_parts.append(dotf(weights.astype(jnp.bfloat16), g[begin:]))
            dk_parts.append(dotf(dscore, q[begin:]))
            dq_part = dotf(dscore, kz[begin:end], TN)
            if head == 0 and begin == 0:
                dq_acc[...] = dq_part
            else:
                dq_acc[begin:, :] += dq_part
        dks.append(jnp.concatenate(dk_parts, axis=0))
        dvs.append(jnp.concatenate(dv_parts, axis=0))
    dq_ref[...] = (dq_acc[...] * scale).astype(jnp.bfloat16)
    dk_ref[...] = jnp.where(lane < half, dks[0], dks[1]).astype(jnp.bfloat16)
    dv_ref[...] = jnp.where(lane < half, dvs[0], dvs[1]).astype(jnp.bfloat16)


def attention_backward(length, mixed, attended, grad, lse):
    total = mixed.shape[0]
    width = mixed.shape[1] // 3
    pairs = width // 128

    def at(offset):
        return pl.BlockSpec((total, 128), lambda p, s: (0, offset + p))

    return pl.pallas_call(
        attention_backward_kernel,
        grid_spec=pltpu.PrefetchScalarGridSpec(
            num_scalar_prefetch=1,
            grid=(pairs,),
            in_specs=[
                at(0),
                at(pairs),
                at(2 * pairs),
                at(0),
                at(0),
                pl.BlockSpec((1, total, 128), lambda p, s: (p, 0, 0)),
            ],
            out_specs=[at(0), at(0), at(0)],
            scratch_shapes=[pltpu.VMEM((total, 128), jnp.float32)],
        ),
        out_shape=[jax.ShapeDtypeStruct((total, width), jnp.bfloat16)] * 3,
        compiler_params=pltpu.CompilerParams(vmem_limit_bytes=48 * 2**20),
        name="attention_backward",
    )(length, mixed, mixed, mixed, attended, grad, lse)


def local_by_heads(
    inputs,
    cotangent,
    lengths,
    norm_gain,
    norm_shift,
    query_key_value_weight,
    output_projection_weight,
    first_feedforward_weight,
    second_feedforward_weight,
    biases,
    down_model,
    down_hidden,
    query_key_value_upward,
    hidden_adapter_upward,
    model_adapter_upward,
    row_down_model,
    col_down_model,
    row_down_hidden,
    col_down_hidden,
    row_up_qkv,
    col_up_qkv,
    row_up_hidden,
    col_up_hidden,
    row_up_model,
    col_up_model,
):
    rows, span, width = inputs.shape
    hidden_width = first_feedforward_weight.shape[1]
    count = rows * span
    spots = lax.axis_index("seq") * span + jnp.arange(span)
    keep = (spots[None, :] < lengths[:, None]).astype(jnp.float32).reshape(count, 1)
    flat = inputs.reshape(count, width).astype(jnp.float32)
    shifts = biases.astype(jnp.float32)
    query_bias = shifts[0:width]
    value_bias = shifts[width : 2 * width]
    projection_bias = shifts[2 * width : 3 * width]
    expand_bias_vector = shifts[3 * width : 3 * width + hidden_width]
    contract_bias_vector = shifts[3 * width + hidden_width : 4 * width + hidden_width]
    query_key_value_bias = jnp.concatenate([query_bias, jnp.zeros_like(query_bias), value_bias])
    gains = norm_gain.astype(jnp.float32)
    offsets = norm_shift.astype(jnp.float32)
    down_low = down_model.astype(jnp.bfloat16)
    hidden_down_low = down_hidden.astype(jnp.bfloat16)
    qkv_up_low = query_key_value_upward.astype(jnp.bfloat16)
    hidden_up_low = hidden_adapter_upward.astype(jnp.bfloat16)
    model_up_low = model_adapter_upward.astype(jnp.bfloat16)
    normalized_rows, unit_first, scaled_first = normalize(flat, gains[0], offsets[0])
    normalized_rows = normalized_rows.astype(jnp.bfloat16)
    mixed_rows, narrow_qkv = adapted(
        normalized_rows, query_key_value_weight, query_key_value_bias, down_low[0], qkv_up_low
    )
    mixed_rows = mixed_rows.astype(jnp.bfloat16).reshape(rows, span, 3, HEADS, HEAD_DIM)
    by_head = lax.all_to_all(mixed_rows, "seq", split_axis=3, concat_axis=1, tiled=True)
    out_heads, lse = lax.map(partial(head_forward, False), (by_head, lengths))
    attended_rows = jax.tree.map(
        lambda part, own: part.astype(own.dtype),
        lax.all_to_all(as_sent(out_heads), "seq", split_axis=1, concat_axis=2, tiled=True),
        out_heads,
    )
    attended_rows = attended_rows.reshape(count, width)
    branch_path, narrow_proj = adapted(
        attended_rows, output_projection_weight, projection_bias, down_low[1], model_up_low[0]
    )
    middle = flat + branch_path
    normed_mid, unit_second, scaled_second = normalize(middle, gains[1], offsets[1])
    normed_mid = normed_mid.astype(jnp.bfloat16)
    before, narrow_expand = adapted(
        normed_mid, first_feedforward_weight, expand_bias_vector, down_low[2], hidden_up_low
    )
    activated, gelu_pull = jax.vjp(lambda value: jax.nn.gelu(value, approximate=True), before)
    activated = activated.astype(jnp.bfloat16)
    branch_out, narrow_contract = adapted(
        activated, second_feedforward_weight, contract_bias_vector, hidden_down_low, model_up_low[1]
    )
    output = (middle + branch_out).astype(jnp.bfloat16).reshape(rows, span, width)
    grad_out = cotangent.reshape(count, width).astype(jnp.float32) * keep
    grad_act, grad_down_contract, grad_up_contract = adapted_back(
        grad_out.astype(jnp.bfloat16),
        activated,
        second_feedforward_weight,
        hidden_down_low,
        model_up_low[1],
        narrow_contract,
    )
    grad_before = gelu_pull(grad_act)[0].astype(jnp.bfloat16)
    grad_norm_mid, grad_down_expand, grad_up_expand = adapted_back(
        grad_before, normed_mid, first_feedforward_weight, down_low[2], hidden_up_low, narrow_expand
    )
    grad_mid = grad_out + normalize_back(grad_norm_mid, unit_second, scaled_second, gains[1])
    grad_att, grad_down_proj, grad_up_proj = adapted_back(
        grad_mid.astype(jnp.bfloat16),
        attended_rows,
        output_projection_weight,
        down_low[1],
        model_up_low[0],
        narrow_proj,
    )
    grad_att = grad_att.astype(jnp.bfloat16).reshape(rows, span, HEADS, HEAD_DIM)
    grad_heads = lax.all_to_all(grad_att, "seq", split_axis=2, concat_axis=1, tiled=True)
    grad_triple = lax.map(partial(head_backward, False), (by_head, grad_heads, lse, lengths))
    grad_mixed = jax.tree.map(
        lambda part, own: part.astype(own.dtype),
        lax.all_to_all(as_sent(grad_triple), "seq", split_axis=1, concat_axis=3, tiled=True),
        grad_triple,
    )
    grad_mixed = grad_mixed.reshape(count, 3 * width)
    grad_normed, grad_down_qkv, grad_up_qkv = adapted_back(
        grad_mixed, normalized_rows, query_key_value_weight, down_low[0], qkv_up_low, narrow_qkv
    )
    input_grad = (
        (grad_mid + normalize_back(grad_normed, unit_first, scaled_first, gains[0]))
        .astype(jnp.bfloat16)
        .reshape(rows, span, width)
    )
    grads = lax.psum(
        (
            jnp.stack([grad_down_qkv, grad_down_proj, grad_down_expand]),
            grad_down_contract,
            grad_up_qkv,
            grad_up_expand,
            jnp.stack([grad_up_proj, grad_up_contract]),
        ),
        ("dp", "seq"),
    )
    grad_dm, grad_dh, grad_uq, grad_uh, grad_um = grads
    new_dm, row_dm, col_dm = factored(grad_dm, down_model, row_down_model, col_down_model)
    new_dh, row_dh, col_dh = factored(grad_dh, down_hidden, row_down_hidden, col_down_hidden)
    new_uq, row_uq, col_uq = factored(grad_uq, query_key_value_upward, row_up_qkv, col_up_qkv)
    new_uh, row_uh, col_uh = factored(grad_uh, hidden_adapter_upward, row_up_hidden, col_up_hidden)
    new_um, row_um, col_um = factored(grad_um, model_adapter_upward, row_up_model, col_up_model)
    return (
        output,
        input_grad,
        grad_dm,
        grad_dh,
        grad_uq,
        grad_uh,
        grad_um,
        new_dm,
        new_dh,
        new_uq,
        new_uh,
        new_um,
        row_dm,
        row_dh,
        row_uq,
        row_uh,
        row_um,
        col_dm,
        col_dh,
        col_uq,
        col_uh,
        col_um,
    )


def local_by_rows(
    inputs,
    cotangent,
    lengths,
    norm_gain,
    norm_shift,
    query_key_value_weight,
    output_projection_weight,
    first_feedforward_weight,
    second_feedforward_weight,
    biases,
    down_model,
    down_hidden,
    query_key_value_upward,
    hidden_adapter_upward,
    model_adapter_upward,
    row_down_model,
    col_down_model,
    row_down_hidden,
    col_down_hidden,
    row_up_qkv,
    col_up_qkv,
    row_up_hidden,
    col_up_hidden,
    row_up_model,
    col_up_model,
):
    rows, span, width = inputs.shape
    hidden_width = first_feedforward_weight.shape[1]
    count = rows * span
    length = lax.dynamic_slice(lengths, (lax.axis_index("seq"),), (1,))
    keep = (jnp.arange(count) < length).astype(jnp.float32)[:, None]
    own_row = lax.all_to_all(inputs, "seq", split_axis=0, concat_axis=0, tiled=True)
    own_cotangent = lax.all_to_all(cotangent, "seq", split_axis=0, concat_axis=0, tiled=True)
    flat = own_row.reshape(count, width).astype(jnp.float32)
    shifts = biases.astype(jnp.float32)
    query_bias = shifts[0:width]
    value_bias = shifts[width : 2 * width]
    projection_bias = shifts[2 * width : 3 * width]
    expand_bias_vector = shifts[3 * width : 3 * width + hidden_width]
    contract_bias_vector = shifts[3 * width + hidden_width : 4 * width + hidden_width]
    query_key_value_bias = jnp.concatenate([query_bias, jnp.zeros_like(query_bias), value_bias])
    gains = norm_gain.astype(jnp.float32)
    offsets = norm_shift.astype(jnp.float32)
    down_low = down_model.astype(jnp.bfloat16)
    hidden_down_low = down_hidden.astype(jnp.bfloat16)
    qkv_up_low = query_key_value_upward.astype(jnp.bfloat16)
    hidden_up_low = hidden_adapter_upward.astype(jnp.bfloat16)
    model_up_low = model_adapter_upward.astype(jnp.bfloat16)
    normalized_rows, unit_first, scaled_first = normalize(flat, gains[0], offsets[0])
    normalized_rows = normalized_rows.astype(jnp.bfloat16)
    mixed_rows, narrow_qkv = adapted(
        normalized_rows, query_key_value_weight, query_key_value_bias, down_low[0], qkv_up_low
    )
    mixed_rows = mixed_rows.astype(jnp.bfloat16)
    attended_rows, lse = attention_forward(length, mixed_rows)
    branch_path, narrow_proj = adapted(
        attended_rows, output_projection_weight, projection_bias, down_low[1], model_up_low[0]
    )
    middle = flat + branch_path
    normed_mid, unit_second, scaled_second = normalize(middle, gains[1], offsets[1])
    normed_mid = normed_mid.astype(jnp.bfloat16)
    before, narrow_expand = adapted(
        normed_mid, first_feedforward_weight, expand_bias_vector, down_low[2], hidden_up_low
    )
    activated, gelu_pull = jax.vjp(lambda value: jax.nn.gelu(value, approximate=True), before)
    activated = activated.astype(jnp.bfloat16)
    branch_out, narrow_contract = adapted(
        activated, second_feedforward_weight, contract_bias_vector, hidden_down_low, model_up_low[1]
    )
    output = (middle + branch_out).astype(jnp.bfloat16).reshape(rows, span, width)
    output = lax.all_to_all(output, "seq", split_axis=0, concat_axis=0, tiled=True)
    grad_out = own_cotangent.reshape(count, width).astype(jnp.float32) * keep
    grad_act, grad_down_contract, grad_up_contract = adapted_back(
        grad_out.astype(jnp.bfloat16),
        activated,
        second_feedforward_weight,
        hidden_down_low,
        model_up_low[1],
        narrow_contract,
    )
    grad_before = gelu_pull(grad_act)[0].astype(jnp.bfloat16)
    grad_norm_mid, grad_down_expand, grad_up_expand = adapted_back(
        grad_before, normed_mid, first_feedforward_weight, down_low[2], hidden_up_low, narrow_expand
    )
    grad_mid = grad_out + normalize_back(grad_norm_mid, unit_second, scaled_second, gains[1])
    grad_att, grad_down_proj, grad_up_proj = adapted_back(
        grad_mid.astype(jnp.bfloat16),
        attended_rows,
        output_projection_weight,
        down_low[1],
        model_up_low[0],
        narrow_proj,
    )
    grad_att = grad_att.astype(jnp.bfloat16)
    grad_mixed = jnp.concatenate(
        attention_backward(length, mixed_rows, attended_rows, grad_att, lse), axis=1
    )
    grad_normed, grad_down_qkv, grad_up_qkv = adapted_back(
        grad_mixed, normalized_rows, query_key_value_weight, down_low[0], qkv_up_low, narrow_qkv
    )
    input_grad = (
        (grad_mid + normalize_back(grad_normed, unit_first, scaled_first, gains[0]))
        .astype(jnp.bfloat16)
        .reshape(rows, span, width)
    )
    input_grad = lax.all_to_all(input_grad, "seq", split_axis=0, concat_axis=0, tiled=True)
    grads = lax.psum(
        (
            jnp.stack([grad_down_qkv, grad_down_proj, grad_down_expand]),
            grad_down_contract,
            grad_up_qkv,
            grad_up_expand,
            jnp.stack([grad_up_proj, grad_up_contract]),
        ),
        ("dp", "seq"),
    )
    grad_dm, grad_dh, grad_uq, grad_uh, grad_um = grads
    new_dm, row_dm, col_dm = factored(grad_dm, down_model, row_down_model, col_down_model)
    new_dh, row_dh, col_dh = factored(grad_dh, down_hidden, row_down_hidden, col_down_hidden)
    new_uq, row_uq, col_uq = factored(grad_uq, query_key_value_upward, row_up_qkv, col_up_qkv)
    new_uh, row_uh, col_uh = factored(grad_uh, hidden_adapter_upward, row_up_hidden, col_up_hidden)
    new_um, row_um, col_um = factored(grad_um, model_adapter_upward, row_up_model, col_up_model)
    return (
        output,
        input_grad,
        grad_dm,
        grad_dh,
        grad_uq,
        grad_uh,
        grad_um,
        new_dm,
        new_dh,
        new_uq,
        new_uh,
        new_um,
        row_dm,
        row_dh,
        row_uq,
        row_uh,
        row_um,
        col_dm,
        col_dh,
        col_uq,
        col_uh,
        col_um,
    )


def local(pieces, inputs, *others):
    if inputs.shape[0] == pieces:
        return local_by_rows(inputs, *others)
    return local_by_heads(inputs, *others)


def solution(mesh):
    placed = (
        P("dp", "seq", None),
        P("dp", "seq", None),
        P("dp"),
        P(),
        P(),
        P(),
        P(),
        P(),
        P(),
        P(),
        P(),
        P(),
        P(),
        P(),
        P(),
        P(),
        P(),
        P(),
        P(),
        P(),
        P(),
        P(),
        P(),
        P(),
        P(),
    )
    return jax.shard_map(
        partial(local, mesh.shape["seq"]),
        mesh=mesh,
        in_specs=placed,
        out_specs=(
            P("dp", "seq", None),
            P("dp", "seq", None),
            P(),
            P(),
            P(),
            P(),
            P(),
            P(),
            P(),
            P(),
            P(),
            P(),
            P(),
            P(),
            P(),
            P(),
            P(),
            P(),
            P(),
            P(),
            P(),
            P(),
        ),
        check_vma=False,
    )
```

```python
from functools import partial

import jax
import jax.numpy as jnp
from jax import lax
from jax.experimental import pallas as pl
from jax.experimental.pallas import tpu as pltpu
from jax.sharding import PartitionSpec as P

HEADS = 16
HEAD_DIM = 64
STEP = 10


NORM_EPS = 1e-05
ADAPTER_SCALE = 8.0
STAT_EPS = 1e-30
CLIP_LEVEL = 1.0
RATE = 0.3
DECAY_WEIGHT = 0.01
MASKED = -1e30


def as_sent(array):

    def short(part):
        return part.astype(jnp.bfloat16) if part.dtype == jnp.float32 else part

    return jax.tree.map(short, array)


def normalize(values, gain, shift):
    centered = values - jnp.mean(values, axis=-1, keepdims=True)
    spread = jnp.mean(centered * centered, axis=-1, keepdims=True)
    scaled = lax.rsqrt(spread + NORM_EPS)
    unit = centered * scaled
    return (unit * gain + shift, unit, scaled)


def normalize_back(grad, unit, scaled, gain):
    gained = grad * gain
    return scaled * (
        gained
        - jnp.mean(gained, axis=-1, keepdims=True)
        - unit * jnp.mean(gained * unit, axis=-1, keepdims=True)
    )


def matrix_multiply(left, right):
    return jnp.dot(left, right, preferred_element_type=jnp.float32)


def inner_product(left, right):
    return jnp.einsum("tr,tc->rc", left, right, preferred_element_type=jnp.float32)


def compared_with(left, right):
    return jnp.einsum("tc,rc->tr", left, right, preferred_element_type=jnp.float32)


def adapted(source_rows, weight_matrix, bias_vector, down, upward_matrix):
    narrowed_rows = matrix_multiply(source_rows, down).astype(jnp.bfloat16)
    return (
        matrix_multiply(source_rows, weight_matrix)
        + bias_vector
        + ADAPTER_SCALE * matrix_multiply(narrowed_rows, upward_matrix),
        narrowed_rows,
    )


def adapted_back(gradient_lowrank, source_rows, weight_matrix, down, upward_matrix, narrowed_rows):
    gradient_upward = ADAPTER_SCALE * inner_product(narrowed_rows, gradient_lowrank)
    gradient_narrowed = (ADAPTER_SCALE * compared_with(gradient_lowrank, upward_matrix)).astype(
        jnp.bfloat16
    )
    grad_down = inner_product(source_rows, gradient_narrowed)
    grad_source = compared_with(gradient_lowrank, weight_matrix) + compared_with(
        gradient_narrowed, down
    )
    return (grad_source, grad_down, gradient_upward)


def score_block(operand):
    query, keys = operand
    return jnp.einsum("gqe,gke->gqk", query, keys, preferred_element_type=jnp.float32)


def mix_block(operand):
    weights, values = operand
    return jnp.einsum("gqk,gke->gqe", weights, values, preferred_element_type=jnp.float32)


def spread_block(operand):
    weights, queries = operand
    return jnp.einsum("gqk,gqe->gke", weights, queries, preferred_element_type=jnp.float32)


def masked_scores(query, keys, spots, length):
    total = keys.shape[1]
    size = min(512, total)
    reach = jnp.minimum(length, jnp.max(spots) + 1)
    places = jnp.arange(total)
    valid = (places[None, :] <= spots[:, None]) & (places[None, :] < length)
    pieces = []
    for begin in range(0, total, size):
        pieces.append(score_block((query, keys[:, begin : begin + size])))
    scores = jnp.concatenate(pieces, axis=-1) * query.shape[-1] ** (-0.5)
    return (jnp.where(valid[None], scores, MASKED), reach, size)


def attend(query, keys, values, spots, length):
    scores, reach, size = masked_scores(query, keys, spots, length)
    top = jnp.max(scores, axis=-1, keepdims=True)
    weights = jnp.exp(scores - top)
    summed = jnp.sum(weights, axis=-1, keepdims=True)
    probs = (weights / summed).astype(jnp.bfloat16)
    result = jnp.zeros(query.shape, jnp.float32)
    for begin in range(0, keys.shape[1], size):
        operand = (probs[:, :, begin : begin + size], values[:, begin : begin + size])
        result = result + mix_block(operand)
    return (result, (top + jnp.log(summed))[..., 0])


def attend_back(query, keys, values, spots, length, grad_rows, lse):
    scores, reach, size = masked_scores(query, keys, spots, length)
    probs = jnp.exp(scores - lse[..., None])
    pieces = []
    for begin in range(0, keys.shape[1], size):
        pieces.append(score_block((grad_rows, values[:, begin : begin + size])))
    dprob = jnp.concatenate(pieces, axis=-1)
    delta = jnp.sum(probs * dprob, axis=-1, keepdims=True)
    dscore = (probs * (dprob - delta)).astype(jnp.bfloat16)
    probs_low = probs.astype(jnp.bfloat16)
    scale = query.shape[-1] ** (-0.5)
    grad_query = jnp.zeros(query.shape, jnp.float32)
    key_parts = []
    value_parts = []
    for begin in range(0, keys.shape[1], size):
        grad_query = grad_query + mix_block(
            (dscore[:, :, begin : begin + size], keys[:, begin : begin + size])
        )
        key_parts.append(spread_block((dscore[:, :, begin : begin + size], query)))
        value_parts.append(spread_block((probs_low[:, :, begin : begin + size], grad_rows)))
    return (
        grad_query * scale,
        jnp.concatenate(key_parts, axis=1) * scale,
        jnp.concatenate(value_parts, axis=1),
    )


def heads_split(triple):
    return tuple((jnp.transpose(triple[:, index], (1, 0, 2)) for index in range(3)))


def head_forward(skip, item):
    triple, length = item
    spots = jnp.arange(triple.shape[0])
    query, keys, values = heads_split(triple)
    result, lse = attend(query, keys, values, spots, length)
    return (jnp.transpose(result, (1, 0, 2)).astype(jnp.bfloat16), lse)


def head_backward(skip, item):
    triple, grad_rows, lse, length = item
    spots = jnp.arange(triple.shape[0])
    query, keys, values = heads_split(triple)
    grads = attend_back(
        query, keys, values, spots, length, jnp.transpose(grad_rows, (1, 0, 2)), lse
    )
    return jnp.stack(grads, axis=0).transpose(2, 0, 1, 3).astype(jnp.bfloat16)


def factored(grad, weight_matrix, row, col):
    decay = 1.0 - STEP ** (-0.8)
    squares = grad * grad + STAT_EPS
    new_row = decay * row + (1.0 - decay) * jnp.mean(squares, axis=-1)
    new_col = decay * col + (1.0 - decay) * jnp.mean(squares, axis=-2)
    second = (
        new_row[..., :, None] * new_col[..., None, :] / jnp.mean(new_row, axis=-1)[..., None, None]
    )
    unit = grad * lax.rsqrt(second)
    level = jnp.sqrt(jnp.mean(unit * unit, axis=(-2, -1), keepdims=True))
    unit = unit / jnp.maximum(1.0, level / CLIP_LEVEL)
    rate = RATE * jnp.sqrt(jnp.mean(weight_matrix * weight_matrix, axis=(-2, -1), keepdims=True))
    return (weight_matrix - rate * (unit + DECAY_WEIGHT * weight_matrix), new_row, new_col)


LOG2E = 1.4426950408889634
TILE = 256
NT = (((1,), (1,)), ((), ()))
TN = (((0,), (0,)), ((), ()))


def dotf(a, b, dims=(((1,), (0,)), ((), ()))):
    return lax.dot_general(a, b, dims, preferred_element_type=jnp.float32)


def triple(value):
    high = value.astype(jnp.bfloat16)
    rest = value - high.astype(jnp.float32)
    mid = rest.astype(jnp.bfloat16)
    low = (rest - mid.astype(jnp.float32)).astype(jnp.bfloat16)
    return high, mid, low


def attention_forward_kernel(length_ref, q_ref, k_ref, v_ref, out_ref, lse_ref):
    total = q_ref.shape[0]
    wide = q_ref.shape[1]
    half = wide // 2
    length = length_ref[0]
    lane = lax.broadcasted_iota(jnp.int32, (total, wide), 1)
    spot = lax.broadcasted_iota(jnp.int32, (total, wide), 0)
    bias = jnp.where(spot < length, 0.0, MASKED).astype(jnp.bfloat16)
    scale = half ** (-0.5)
    one = jnp.ones((total, wide), jnp.bfloat16)
    zero = jnp.zeros((total, wide), jnp.bfloat16)
    q = q_ref[...] * jnp.asarray(scale, jnp.bfloat16)
    k = k_ref[...]
    v = v_ref[...]
    row = lax.broadcasted_iota(jnp.int32, (TILE, TILE), 0)
    col = lax.broadcasted_iota(jnp.int32, (TILE, TILE), 1)
    outs = []
    lses = []
    for head in range(2):
        own = (lane < half) if head == 0 else (lane >= half)
        spare = half if head == 0 else 0
        qh = jnp.where(own, q, jnp.where(lane == spare, one, zero))
        kh = jnp.where(own, k, jnp.where(lane == spare, bias, zero))
        vh = jnp.where(own, v, one)
        parts = []
        lparts = []
        for begin in range(0, total, TILE):
            end = begin + TILE
            scores = dotf(qh[begin:end], kh[:end], NT)
            diag = jnp.where(col <= row, scores[:, begin:], MASKED)
            if begin:
                scores = jnp.concatenate([scores[:, :begin], diag], axis=1)
            else:
                scores = diag
            top = jnp.max(scores, axis=-1, keepdims=True)
            weights = jnp.exp2((scores - top) * LOG2E).astype(jnp.bfloat16)
            mixed = dotf(weights, vh[:end])
            summed = mixed[:, spare : spare + 1]
            parts.append(mixed * (1.0 / summed))
            lparts.append(jnp.broadcast_to(top + jnp.log(summed), (TILE, wide)))
        outs.append(jnp.concatenate(parts, axis=0))
        lses.append(jnp.concatenate(lparts, axis=0))
    out_ref[...] = jnp.where(lane < half, outs[0], outs[1]).astype(jnp.bfloat16)
    lse_ref[0] = jnp.where(lane < half, lses[1], lses[0])


def attention_forward(length, mixed):
    total = mixed.shape[0]
    width = mixed.shape[1] // 3
    pairs = width // 128

    def at(offset):
        return pl.BlockSpec((total, 128), lambda p, s: (0, offset + p))

    return pl.pallas_call(
        attention_forward_kernel,
        grid_spec=pltpu.PrefetchScalarGridSpec(
            num_scalar_prefetch=1,
            grid=(pairs,),
            in_specs=[at(0), at(pairs), at(2 * pairs)],
            out_specs=[
                at(0),
                pl.BlockSpec((1, total, 128), lambda p, s: (p, 0, 0)),
            ],
        ),
        out_shape=[
            jax.ShapeDtypeStruct((total, width), jnp.bfloat16),
            jax.ShapeDtypeStruct((pairs, total, 128), jnp.float32),
        ],
        compiler_params=pltpu.CompilerParams(vmem_limit_bytes=48 * 2**20),
        name="attention_forward",
    )(length, mixed, mixed, mixed)


def attention_backward_kernel(
    length_ref, q_ref, k_ref, v_ref, o_ref, g_ref, lse_ref, dq_ref, dk_ref, dv_ref, dq_acc
):
    total = q_ref.shape[0]
    wide = q_ref.shape[1]
    half = wide // 2
    length = length_ref[0]
    lane = lax.broadcasted_iota(jnp.int32, (total, wide), 1)
    spot = lax.broadcasted_iota(jnp.int32, (total, wide), 0)
    scale = half ** (-0.5)
    one = jnp.ones((total, wide), jnp.bfloat16)
    zero = jnp.zeros((total, wide), jnp.bfloat16)
    q = q_ref[...] * jnp.asarray(scale, jnp.bfloat16)
    k = k_ref[...]
    v = v_ref[...]
    g = g_ref[...]
    product = g.astype(jnp.float32) * o_ref[...].astype(jnp.float32)
    neglse = jnp.where(spot < length, -lse_ref[0], MASKED)
    row = lax.broadcasted_iota(jnp.int32, (TILE, TILE), 0)
    col = lax.broadcasted_iota(jnp.int32, (TILE, TILE), 1)
    l_high, l_mid, l_low = triple(neglse)
    dks = []
    dvs = []
    for head in range(2):
        own = (lane < half) if head == 0 else (lane >= half)
        spare = half if head == 0 else 0
        delta = -jnp.sum(jnp.where(own, product, 0.0), axis=-1, keepdims=True)
        d_high, d_mid, d_low = triple(jnp.broadcast_to(delta, (total, wide)))

        def extra(a, b, c):
            return jnp.where(
                lane == spare, a, jnp.where(lane == spare + 1, b, jnp.where(lane == spare + 2, c, zero))
            )

        qh = jnp.where(own, q, extra(l_high, l_mid, l_low))
        kh = jnp.where(own, k, one)
        gh = jnp.where(own, g, extra(d_high, d_mid, d_low))
        vh = jnp.where(own, v, one)
        kz = jnp.where(own, k, zero)
        dk_parts = []
        dv_parts = []
        for begin in range(0, total, TILE):
            end = begin + TILE
            scores = dotf(kh[begin:end], qh[begin:], NT)
            weights = jnp.exp2(scores * LOG2E)
            diag = jnp.where(row <= col, weights[:, :TILE], 0.0)
            if end < total:
                weights = jnp.concatenate([diag, weights[:, TILE:]], axis=1)
            else:
                weights = diag
            dprob = dotf(vh[begin:end], gh[begin:], NT)
            dscore = (weights * dprob).astype(jnp.bfloat16)
            dv_parts.append(dotf(weights.astype(jnp.bfloat16), g[begin:]))
            dk_parts.append(dotf(dscore, q[begin:]))
            dq_part = dotf(dscore, kz[begin:end], TN)
            if head == 0 and begin == 0:
                dq_acc[...] = dq_part
            else:
                dq_acc[begin:, :] += dq_part
        dks.append(jnp.concatenate(dk_parts, axis=0))
        dvs.append(jnp.concatenate(dv_parts, axis=0))
    dq_ref[...] = (dq_acc[...] * scale).astype(jnp.bfloat16)
    dk_ref[...] = jnp.where(lane < half, dks[0], dks[1]).astype(jnp.bfloat16)
    dv_ref[...] = jnp.where(lane < half, dvs[0], dvs[1]).astype(jnp.bfloat16)


def attention_backward(length, mixed, attended, grad, lse):
    total = mixed.shape[0]
    width = mixed.shape[1] // 3
    pairs = width // 128

    def at(offset):
        return pl.BlockSpec((total, 128), lambda p, s: (0, offset + p))

    return pl.pallas_call(
        attention_backward_kernel,
        grid_spec=pltpu.PrefetchScalarGridSpec(
            num_scalar_prefetch=1,
            grid=(pairs,),
            in_specs=[
                at(0),
                at(pairs),
                at(2 * pairs),
                at(0),
                at(0),
                pl.BlockSpec((1, total, 128), lambda p, s: (p, 0, 0)),
            ],
            out_specs=[at(0), at(0), at(0)],
            scratch_shapes=[pltpu.VMEM((total, 128), jnp.float32)],
        ),
        out_shape=[jax.ShapeDtypeStruct((total, width), jnp.bfloat16)] * 3,
        compiler_params=pltpu.CompilerParams(vmem_limit_bytes=48 * 2**20),
        name="attention_backward",
    )(length, mixed, mixed, mixed, attended, grad, lse)


RANK = 4


def peers_of(axis, size):
    me = lax.axis_index(axis)
    return me, [lax.rem(me + shift, size) for shift in range(1, size)]


def greet(axes):
    barrier = pltpu.get_barrier_semaphore()
    count = 0
    for axis, size in axes:
        _, peers = peers_of(axis, size)
        for peer in peers:
            pl.semaphore_signal(
                barrier, inc=1, device_id={axis: peer}, device_id_type=pl.DeviceIdType.MESH
            )
        count += len(peers)
    pl.semaphore_wait(barrier, count)


def send(source, target, sent, landed, axis, peer):
    return pltpu.make_async_remote_copy(
        src_ref=source,
        dst_ref=target,
        send_sem=sent,
        recv_sem=landed,
        device_id={axis: peer},
        device_id_type=pl.DeviceIdType.MESH,
    )


def sum_everywhere(
    splits, copies, part_ref, total_ref, seq_in, dp_in, own, s_sent, s_land, d_sent, d_land, g_sent, g_land
):
    size = part_ref.shape[1] // splits
    me, peers = peers_of("seq", splits)
    mine, others = peers_of("dp", copies)

    def columns(index):
        return pl.ds(pl.multiple_of(index * size, size), size)

    first = []
    for shift, peer in enumerate(peers):
        copy = send(part_ref.at[:, columns(peer)], seq_in.at[me], s_sent.at[shift], s_land.at[me], "seq", peer)
        copy.start()
        first.append(copy)
    seq_in[me] = part_ref[:, columns(me)]
    for peer in peers:
        send(part_ref.at[:, columns(me)], seq_in.at[peer], s_sent.at[0], s_land.at[peer], "seq", peer).wait_recv()
    summed = seq_in[0]
    for index in range(1, splits):
        summed = summed + seq_in[index]
    own[...] = summed
    second = []
    for shift, peer in enumerate(others):
        copy = send(own, dp_in.at[mine], d_sent.at[shift], d_land.at[mine], "dp", peer)
        copy.start()
        second.append(copy)
    dp_in[mine] = summed
    for peer in others:
        send(own, dp_in.at[peer], d_sent.at[0], d_land.at[peer], "dp", peer).wait_recv()
    summed = dp_in[0]
    for index in range(1, copies):
        summed = summed + dp_in[index]
    total_ref[:, columns(me)] = summed
    third = []
    for shift, peer in enumerate(peers):
        copy = send(
            total_ref.at[:, columns(me)], total_ref.at[:, columns(me)], g_sent.at[shift], g_land.at[me], "seq", peer
        )
        copy.start()
        third.append(copy)
    for peer in peers:
        part = total_ref.at[:, columns(peer)]
        send(part, part, g_sent.at[0], g_land.at[peer], "seq", peer).wait_recv()
    for copy in first + second + third:
        copy.wait_send()


def sum_kernel(splits, copies, part_ref, total_ref, *scratch):
    greet((("seq", splits), ("dp", copies)))
    sum_everywhere(splits, copies, part_ref, total_ref, *scratch)


def sum_scratch(splits, copies, width):
    size = width // splits
    dma = pltpu.SemaphoreType.DMA
    return [
        pltpu.VMEM((splits, 8, size), jnp.float32),
        pltpu.VMEM((copies, 8, size), jnp.float32),
        pltpu.VMEM((8, size), jnp.float32),
        dma((splits,)),
        dma((splits,)),
        dma((copies,)),
        dma((copies,)),
        dma((splits,)),
        dma((splits,)),
    ]


def sum_devices(splits, copies, part):
    return pl.pallas_call(
        lambda *refs: sum_kernel(splits, copies, *refs),
        out_shape=jax.ShapeDtypeStruct(part.shape, jnp.float32),
        in_specs=[pl.BlockSpec(memory_space=pltpu.VMEM)],
        out_specs=pl.BlockSpec(memory_space=pltpu.VMEM),
        scratch_shapes=sum_scratch(splits, copies, part.shape[1]),
        compiler_params=pltpu.CompilerParams(collective_id=1, has_side_effects=True),
        name="sum_devices",
    )(part)


def across(column):
    count = column.shape[0]
    diagonal = lax.broadcasted_iota(jnp.int32, (count, count), 0) == lax.broadcasted_iota(
        jnp.int32, (count, count), 1
    )
    return jnp.sum(jnp.where(diagonal, jnp.broadcast_to(column, (count, count)), 0.0), axis=0, keepdims=True)


def upright(line):
    count = line.shape[1]
    diagonal = lax.broadcasted_iota(jnp.int32, (count, count), 0) == lax.broadcasted_iota(
        jnp.int32, (count, count), 1
    )
    return jnp.sum(jnp.where(diagonal, jnp.broadcast_to(line, (count, count)), 0.0), axis=1, keepdims=True)


def factored_step(grad, weight, short_line, long_line, rows_long):
    decay = 1.0 - STEP ** (-0.8)
    squares = grad * grad + STAT_EPS
    new_short = decay * upright(short_line) + (1.0 - decay) * jnp.mean(squares, axis=1, keepdims=True)
    new_long = decay * long_line + (1.0 - decay) * jnp.mean(squares, axis=0, keepdims=True)
    if rows_long:
        middle = jnp.mean(new_long, axis=1, keepdims=True)
    else:
        middle = jnp.mean(new_short, axis=0, keepdims=True)
    unit = grad * lax.rsqrt(new_short * new_long / middle)
    entries = grad.shape[0] * grad.shape[1]

    def mean_square(value):
        return jnp.sum(jnp.sum(value * value, axis=1, keepdims=True), axis=0, keepdims=True) / entries

    level = jnp.sqrt(mean_square(unit))
    unit = unit / jnp.maximum(1.0, level / CLIP_LEVEL)
    rate = RATE * jnp.sqrt(mean_square(weight))
    return weight - rate * (unit + DECAY_WEIGHT * weight), across(new_short), new_long


def update_kernel(
    total_ref, dm, dh, uq, uh, um, row_dm, col_dm, row_dh, col_dh, row_uq, col_uq, row_uh, col_uh, row_um, col_um,
    g_dm, g_dh, g_uq, g_uh, g_um, n_dm, n_dh, n_uq, n_uh, n_um,
    r_dm, r_dh, r_uq, r_uh, r_um, c_dm, c_dh, c_uq, c_uh, c_um,
):
    width = dm.shape[2]
    hidden = dh.shape[1]
    for index in range(3):
        grad = total_ref[0:RANK, index * width : (index + 1) * width]
        g_dm[index] = grad
        n_dm[index], c_dm[index : index + 1, :], r_dm[index : index + 1, :] = factored_step(
            grad, dm[index], col_dm[index : index + 1, :], row_dm[index : index + 1, :], True
        )
    grad = total_ref[0:RANK, 3 * width : 6 * width]
    g_uq[...] = grad
    n_uq[...], r_uq[...], c_uq[...] = factored_step(grad, uq[...], row_uq[...], col_uq[...], False)
    for index in range(2):
        grad = total_ref[0:RANK, (6 + index) * width : (7 + index) * width]
        g_um[index] = grad
        n_um[index], r_um[index : index + 1, :], c_um[index : index + 1, :] = factored_step(
            grad, um[index], row_um[index : index + 1, :], col_um[index : index + 1, :], False
        )
    grad = total_ref[RANK : 2 * RANK, 0:hidden]
    g_dh[...] = grad
    n_dh[...], c_dh[...], r_dh[...] = factored_step(grad, dh[...], col_dh[...], row_dh[...], True)
    grad = total_ref[RANK : 2 * RANK, hidden : 2 * hidden]
    g_uh[...] = grad
    n_uh[...], r_uh[...], c_uh[...] = factored_step(grad, uh[...], row_uh[...], col_uh[...], False)


def update(total, dm, dh, uq, uh, um, row_dm, col_dm, row_dh, col_dh, row_uq, col_uq, row_uh, col_uh, row_um, col_um):
    flip = lambda array: jnp.swapaxes(array, -1, -2)
    line = lambda array: array.reshape(1, -1)
    given = [
        total, flip(dm), flip(dh), uq, uh, um, row_dm, col_dm, line(row_dh), line(col_dh),
        line(row_uq), line(col_uq), line(row_uh), line(col_uh), row_um, col_um,
    ]
    like = [given[1], given[2], uq, uh, um]
    stats = [row_dm, line(row_dh), line(row_uq), line(row_uh), row_um, col_dm, line(col_dh), line(col_uq), line(col_uh), col_um]
    results = pl.pallas_call(
        update_kernel,
        out_shape=[jax.ShapeDtypeStruct(a.shape, jnp.float32) for a in like + like + stats],
        in_specs=[pl.BlockSpec(memory_space=pltpu.VMEM)] * len(given),
        out_specs=[pl.BlockSpec(memory_space=pltpu.VMEM)] * 20,
        name="factored_update",
    )(*given)
    results = list(results)
    for index in (0, 1, 5, 6):
        results[index] = flip(results[index])
    for index, old in zip(range(10, 20), (row_dm, row_dh, row_uq, row_uh, row_um, col_dm, col_dh, col_uq, col_uh, col_um)):
        results[index] = results[index].reshape(old.shape)
    return tuple(results)


def pack(grad_dm, grad_dh, grad_uq, grad_uh, grad_um):
    upper = jnp.concatenate(list(grad_dm) + [grad_uq] + list(grad_um), axis=1)
    lower = jnp.concatenate([grad_dh, grad_uh], axis=1)
    return jnp.concatenate([upper, lower], axis=0)


def local_by_heads(
    inputs,
    cotangent,
    lengths,
    norm_gain,
    norm_shift,
    query_key_value_weight,
    output_projection_weight,
    first_feedforward_weight,
    second_feedforward_weight,
    biases,
    down_model,
    down_hidden,
    query_key_value_upward,
    hidden_adapter_upward,
    model_adapter_upward,
    row_down_model,
    col_down_model,
    row_down_hidden,
    col_down_hidden,
    row_up_qkv,
    col_up_qkv,
    row_up_hidden,
    col_up_hidden,
    row_up_model,
    col_up_model,
):
    rows, span, width = inputs.shape
    hidden_width = first_feedforward_weight.shape[1]
    count = rows * span
    spots = lax.axis_index("seq") * span + jnp.arange(span)
    keep = (spots[None, :] < lengths[:, None]).astype(jnp.float32).reshape(count, 1)
    flat = inputs.reshape(count, width).astype(jnp.float32)
    shifts = biases.astype(jnp.float32)
    query_bias = shifts[0:width]
    value_bias = shifts[width : 2 * width]
    projection_bias = shifts[2 * width : 3 * width]
    expand_bias_vector = shifts[3 * width : 3 * width + hidden_width]
    contract_bias_vector = shifts[3 * width + hidden_width : 4 * width + hidden_width]
    query_key_value_bias = jnp.concatenate([query_bias, jnp.zeros_like(query_bias), value_bias])
    gains = norm_gain.astype(jnp.float32)
    offsets = norm_shift.astype(jnp.float32)
    down_low = down_model.astype(jnp.bfloat16)
    hidden_down_low = down_hidden.astype(jnp.bfloat16)
    qkv_up_low = query_key_value_upward.astype(jnp.bfloat16)
    hidden_up_low = hidden_adapter_upward.astype(jnp.bfloat16)
    model_up_low = model_adapter_upward.astype(jnp.bfloat16)
    normalized_rows, unit_first, scaled_first = normalize(flat, gains[0], offsets[0])
    normalized_rows = normalized_rows.astype(jnp.bfloat16)
    mixed_rows, narrow_qkv = adapted(
        normalized_rows, query_key_value_weight, query_key_value_bias, down_low[0], qkv_up_low
    )
    mixed_rows = mixed_rows.astype(jnp.bfloat16).reshape(rows, span, 3, HEADS, HEAD_DIM)
    by_head = lax.all_to_all(mixed_rows, "seq", split_axis=3, concat_axis=1, tiled=True)
    out_heads, lse = lax.map(partial(head_forward, False), (by_head, lengths))
    attended_rows = jax.tree.map(
        lambda part, own: part.astype(own.dtype),
        lax.all_to_all(as_sent(out_heads), "seq", split_axis=1, concat_axis=2, tiled=True),
        out_heads,
    )
    attended_rows = attended_rows.reshape(count, width)
    branch_path, narrow_proj = adapted(
        attended_rows, output_projection_weight, projection_bias, down_low[1], model_up_low[0]
    )
    middle = flat + branch_path
    normed_mid, unit_second, scaled_second = normalize(middle, gains[1], offsets[1])
    normed_mid = normed_mid.astype(jnp.bfloat16)
    before, narrow_expand = adapted(
        normed_mid, first_feedforward_weight, expand_bias_vector, down_low[2], hidden_up_low
    )
    activated, gelu_pull = jax.vjp(lambda value: jax.nn.gelu(value, approximate=True), before)
    activated = activated.astype(jnp.bfloat16)
    branch_out, narrow_contract = adapted(
        activated, second_feedforward_weight, contract_bias_vector, hidden_down_low, model_up_low[1]
    )
    output = (middle + branch_out).astype(jnp.bfloat16).reshape(rows, span, width)
    grad_out = cotangent.reshape(count, width).astype(jnp.float32) * keep
    grad_act, grad_down_contract, grad_up_contract = adapted_back(
        grad_out.astype(jnp.bfloat16),
        activated,
        second_feedforward_weight,
        hidden_down_low,
        model_up_low[1],
        narrow_contract,
    )
    grad_before = gelu_pull(grad_act)[0].astype(jnp.bfloat16)
    grad_norm_mid, grad_down_expand, grad_up_expand = adapted_back(
        grad_before, normed_mid, first_feedforward_weight, down_low[2], hidden_up_low, narrow_expand
    )
    grad_mid = grad_out + normalize_back(grad_norm_mid, unit_second, scaled_second, gains[1])
    grad_att, grad_down_proj, grad_up_proj = adapted_back(
        grad_mid.astype(jnp.bfloat16),
        attended_rows,
        output_projection_weight,
        down_low[1],
        model_up_low[0],
        narrow_proj,
    )
    grad_att = grad_att.astype(jnp.bfloat16).reshape(rows, span, HEADS, HEAD_DIM)
    grad_heads = lax.all_to_all(grad_att, "seq", split_axis=2, concat_axis=1, tiled=True)
    grad_triple = lax.map(partial(head_backward, False), (by_head, grad_heads, lse, lengths))
    grad_mixed = jax.tree.map(
        lambda part, own: part.astype(own.dtype),
        lax.all_to_all(as_sent(grad_triple), "seq", split_axis=1, concat_axis=3, tiled=True),
        grad_triple,
    )
    grad_mixed = grad_mixed.reshape(count, 3 * width)
    grad_normed, grad_down_qkv, grad_up_qkv = adapted_back(
        grad_mixed, normalized_rows, query_key_value_weight, down_low[0], qkv_up_low, narrow_qkv
    )
    input_grad = (
        (grad_mid + normalize_back(grad_normed, unit_first, scaled_first, gains[0]))
        .astype(jnp.bfloat16)
        .reshape(rows, span, width)
    )
    grads = lax.psum(
        (
            jnp.stack([grad_down_qkv, grad_down_proj, grad_down_expand]),
            grad_down_contract,
            grad_up_qkv,
            grad_up_expand,
            jnp.stack([grad_up_proj, grad_up_contract]),
        ),
        ("dp", "seq"),
    )
    grad_dm, grad_dh, grad_uq, grad_uh, grad_um = grads
    new_dm, row_dm, col_dm = factored(grad_dm, down_model, row_down_model, col_down_model)
    new_dh, row_dh, col_dh = factored(grad_dh, down_hidden, row_down_hidden, col_down_hidden)
    new_uq, row_uq, col_uq = factored(grad_uq, query_key_value_upward, row_up_qkv, col_up_qkv)
    new_uh, row_uh, col_uh = factored(grad_uh, hidden_adapter_upward, row_up_hidden, col_up_hidden)
    new_um, row_um, col_um = factored(grad_um, model_adapter_upward, row_up_model, col_up_model)
    return (
        output,
        input_grad,
        grad_dm,
        grad_dh,
        grad_uq,
        grad_uh,
        grad_um,
        new_dm,
        new_dh,
        new_uq,
        new_uh,
        new_um,
        row_dm,
        row_dh,
        row_uq,
        row_uh,
        row_um,
        col_dm,
        col_dh,
        col_uq,
        col_uh,
        col_um,
    )


def local_by_rows(
    inputs,
    cotangent,
    lengths,
    norm_gain,
    norm_shift,
    query_key_value_weight,
    output_projection_weight,
    first_feedforward_weight,
    second_feedforward_weight,
    biases,
    down_model,
    down_hidden,
    query_key_value_upward,
    hidden_adapter_upward,
    model_adapter_upward,
    row_down_model,
    col_down_model,
    row_down_hidden,
    col_down_hidden,
    row_up_qkv,
    col_up_qkv,
    row_up_hidden,
    col_up_hidden,
    row_up_model,
    col_up_model,
):
    rows, span, width = inputs.shape
    hidden_width = first_feedforward_weight.shape[1]
    count = rows * span
    length = lax.dynamic_slice(lengths, (lax.axis_index("seq"),), (1,))
    keep = (jnp.arange(count) < length).astype(jnp.float32)[:, None]
    own_row = lax.all_to_all(inputs, "seq", split_axis=0, concat_axis=0, tiled=True)
    own_cotangent = lax.all_to_all(cotangent, "seq", split_axis=0, concat_axis=0, tiled=True)
    flat = own_row.reshape(count, width).astype(jnp.float32)
    shifts = biases.astype(jnp.float32)
    query_bias = shifts[0:width]
    value_bias = shifts[width : 2 * width]
    projection_bias = shifts[2 * width : 3 * width]
    expand_bias_vector = shifts[3 * width : 3 * width + hidden_width]
    contract_bias_vector = shifts[3 * width + hidden_width : 4 * width + hidden_width]
    query_key_value_bias = jnp.concatenate([query_bias, jnp.zeros_like(query_bias), value_bias])
    gains = norm_gain.astype(jnp.float32)
    offsets = norm_shift.astype(jnp.float32)
    down_low = down_model.astype(jnp.bfloat16)
    hidden_down_low = down_hidden.astype(jnp.bfloat16)
    qkv_up_low = query_key_value_upward.astype(jnp.bfloat16)
    hidden_up_low = hidden_adapter_upward.astype(jnp.bfloat16)
    model_up_low = model_adapter_upward.astype(jnp.bfloat16)
    normalized_rows, unit_first, scaled_first = normalize(flat, gains[0], offsets[0])
    normalized_rows = normalized_rows.astype(jnp.bfloat16)
    mixed_rows, narrow_qkv = adapted(
        normalized_rows, query_key_value_weight, query_key_value_bias, down_low[0], qkv_up_low
    )
    mixed_rows = mixed_rows.astype(jnp.bfloat16)
    attended_rows, lse = attention_forward(length, mixed_rows)
    branch_path, narrow_proj = adapted(
        attended_rows, output_projection_weight, projection_bias, down_low[1], model_up_low[0]
    )
    middle = flat + branch_path
    normed_mid, unit_second, scaled_second = normalize(middle, gains[1], offsets[1])
    normed_mid = normed_mid.astype(jnp.bfloat16)
    before, narrow_expand = adapted(
        normed_mid, first_feedforward_weight, expand_bias_vector, down_low[2], hidden_up_low
    )
    activated, gelu_pull = jax.vjp(lambda value: jax.nn.gelu(value, approximate=True), before)
    activated = activated.astype(jnp.bfloat16)
    branch_out, narrow_contract = adapted(
        activated, second_feedforward_weight, contract_bias_vector, hidden_down_low, model_up_low[1]
    )
    output = (middle + branch_out).astype(jnp.bfloat16).reshape(rows, span, width)
    output = lax.all_to_all(output, "seq", split_axis=0, concat_axis=0, tiled=True)
    grad_out = own_cotangent.reshape(count, width).astype(jnp.float32) * keep
    grad_act, grad_down_contract, grad_up_contract = adapted_back(
        grad_out.astype(jnp.bfloat16),
        activated,
        second_feedforward_weight,
        hidden_down_low,
        model_up_low[1],
        narrow_contract,
    )
    grad_before = gelu_pull(grad_act)[0].astype(jnp.bfloat16)
    grad_norm_mid, grad_down_expand, grad_up_expand = adapted_back(
        grad_before, normed_mid, first_feedforward_weight, down_low[2], hidden_up_low, narrow_expand
    )
    grad_mid = grad_out + normalize_back(grad_norm_mid, unit_second, scaled_second, gains[1])
    grad_att, grad_down_proj, grad_up_proj = adapted_back(
        grad_mid.astype(jnp.bfloat16),
        attended_rows,
        output_projection_weight,
        down_low[1],
        model_up_low[0],
        narrow_proj,
    )
    grad_att = grad_att.astype(jnp.bfloat16)
    grad_mixed = jnp.concatenate(
        attention_backward(length, mixed_rows, attended_rows, grad_att, lse), axis=1
    )
    grad_normed, grad_down_qkv, grad_up_qkv = adapted_back(
        grad_mixed, normalized_rows, query_key_value_weight, down_low[0], qkv_up_low, narrow_qkv
    )
    input_grad = (
        (grad_mid + normalize_back(grad_normed, unit_first, scaled_first, gains[0]))
        .astype(jnp.bfloat16)
        .reshape(rows, span, width)
    )
    input_grad = lax.all_to_all(input_grad, "seq", split_axis=0, concat_axis=0, tiled=True)
    part = pack(
        [grad_down_qkv.T, grad_down_proj.T, grad_down_expand.T],
        grad_down_contract.T,
        grad_up_qkv,
        grad_up_expand,
        [grad_up_proj, grad_up_contract],
    )
    total = sum_devices(lax.axis_size("seq"), lax.axis_size("dp"), part)
    return (output, input_grad) + update(
        total,
        down_model,
        down_hidden,
        query_key_value_upward,
        hidden_adapter_upward,
        model_adapter_upward,
        row_down_model,
        col_down_model,
        row_down_hidden,
        col_down_hidden,
        row_up_qkv,
        col_up_qkv,
        row_up_hidden,
        col_up_hidden,
        row_up_model,
        col_up_model,
    )


def local(pieces, inputs, *others):
    if inputs.shape[0] == pieces:
        return local_by_rows(inputs, *others)
    return local_by_heads(inputs, *others)


def solution(mesh):
    placed = (
        P("dp", "seq", None),
        P("dp", "seq", None),
        P("dp"),
        P(),
        P(),
        P(),
        P(),
        P(),
        P(),
        P(),
        P(),
        P(),
        P(),
        P(),
        P(),
        P(),
        P(),
        P(),
        P(),
        P(),
        P(),
        P(),
        P(),
        P(),
        P(),
    )
    return jax.shard_map(
        partial(local, mesh.shape["seq"]),
        mesh=mesh,
        in_specs=placed,
        out_specs=(
            P("dp", "seq", None),
            P("dp", "seq", None),
            P(),
            P(),
            P(),
            P(),
            P(),
            P(),
            P(),
            P(),
            P(),
            P(),
            P(),
            P(),
            P(),
            P(),
            P(),
            P(),
            P(),
            P(),
            P(),
            P(),
        ),
        check_vma=False,
    )
```

```python
from functools import partial

import jax
import jax.numpy as jnp
from jax import lax
from jax.experimental import pallas as pl
from jax.experimental.pallas import tpu as pltpu
from jax.sharding import PartitionSpec as P


HEADS = 16
HEAD_DIM = 64
STEP = 10


NORM_EPS = 1e-05
ADAPTER_SCALE = 8.0
STAT_EPS = 1e-30
CLIP_LEVEL = 1.0
RATE = 0.3
DECAY_WEIGHT = 0.01
MASKED = -1e30


def as_sent(array):

    def short(part):
        return part.astype(jnp.bfloat16) if part.dtype == jnp.float32 else part

    return jax.tree.map(short, array)


def normalize(values, gain, shift):
    centered = values - jnp.mean(values, axis=-1, keepdims=True)
    spread = jnp.mean(centered * centered, axis=-1, keepdims=True)
    scaled = lax.rsqrt(spread + NORM_EPS)
    unit = centered * scaled
    return (unit * gain + shift, unit, scaled)


def normalize_back(grad, unit, scaled, gain):
    gained = grad * gain
    return scaled * (
        gained
        - jnp.mean(gained, axis=-1, keepdims=True)
        - unit * jnp.mean(gained * unit, axis=-1, keepdims=True)
    )


def matrix_multiply(left, right):
    return jnp.dot(left, right, preferred_element_type=jnp.float32)


def inner_product(left, right):
    return jnp.einsum("tr,tc->rc", left, right, preferred_element_type=jnp.float32)


def compared_with(left, right):
    return jnp.einsum("tc,rc->tr", left, right, preferred_element_type=jnp.float32)


def adapted(source_rows, weight_matrix, bias_vector, down, upward_matrix):
    narrowed_rows = matrix_multiply(source_rows, down).astype(jnp.bfloat16)
    return (
        matrix_multiply(source_rows, weight_matrix)
        + bias_vector
        + ADAPTER_SCALE * matrix_multiply(narrowed_rows, upward_matrix),
        narrowed_rows,
    )


def adapted_back(gradient_lowrank, source_rows, weight_matrix, down, upward_matrix, narrowed_rows):
    gradient_upward = ADAPTER_SCALE * inner_product(narrowed_rows, gradient_lowrank)
    gradient_narrowed = (ADAPTER_SCALE * compared_with(gradient_lowrank, upward_matrix)).astype(
        jnp.bfloat16
    )
    grad_down = inner_product(source_rows, gradient_narrowed)
    grad_source = compared_with(gradient_lowrank, weight_matrix) + compared_with(
        gradient_narrowed, down
    )
    return (grad_source, grad_down, gradient_upward)


def score_block(operand):
    query, keys = operand
    return jnp.einsum("gqe,gke->gqk", query, keys, preferred_element_type=jnp.float32)


def mix_block(operand):
    weights, values = operand
    return jnp.einsum("gqk,gke->gqe", weights, values, preferred_element_type=jnp.float32)


def spread_block(operand):
    weights, queries = operand
    return jnp.einsum("gqk,gqe->gke", weights, queries, preferred_element_type=jnp.float32)


def masked_scores(query, keys, spots, length):
    total = keys.shape[1]
    size = min(512, total)
    reach = jnp.minimum(length, jnp.max(spots) + 1)
    places = jnp.arange(total)
    valid = (places[None, :] <= spots[:, None]) & (places[None, :] < length)
    pieces = []
    for begin in range(0, total, size):
        pieces.append(score_block((query, keys[:, begin : begin + size])))
    scores = jnp.concatenate(pieces, axis=-1) * query.shape[-1] ** (-0.5)
    return (jnp.where(valid[None], scores, MASKED), reach, size)


def attend(query, keys, values, spots, length):
    scores, reach, size = masked_scores(query, keys, spots, length)
    top = jnp.max(scores, axis=-1, keepdims=True)
    weights = jnp.exp(scores - top)
    summed = jnp.sum(weights, axis=-1, keepdims=True)
    probs = (weights / summed).astype(jnp.bfloat16)
    result = jnp.zeros(query.shape, jnp.float32)
    for begin in range(0, keys.shape[1], size):
        operand = (probs[:, :, begin : begin + size], values[:, begin : begin + size])
        result = result + mix_block(operand)
    return (result, (top + jnp.log(summed))[..., 0])


def attend_back(query, keys, values, spots, length, grad_rows, lse):
    scores, reach, size = masked_scores(query, keys, spots, length)
    probs = jnp.exp(scores - lse[..., None])
    pieces = []
    for begin in range(0, keys.shape[1], size):
        pieces.append(score_block((grad_rows, values[:, begin : begin + size])))
    dprob = jnp.concatenate(pieces, axis=-1)
    delta = jnp.sum(probs * dprob, axis=-1, keepdims=True)
    dscore = (probs * (dprob - delta)).astype(jnp.bfloat16)
    probs_low = probs.astype(jnp.bfloat16)
    scale = query.shape[-1] ** (-0.5)
    grad_query = jnp.zeros(query.shape, jnp.float32)
    key_parts = []
    value_parts = []
    for begin in range(0, keys.shape[1], size):
        grad_query = grad_query + mix_block(
            (dscore[:, :, begin : begin + size], keys[:, begin : begin + size])
        )
        key_parts.append(spread_block((dscore[:, :, begin : begin + size], query)))
        value_parts.append(spread_block((probs_low[:, :, begin : begin + size], grad_rows)))
    return (
        grad_query * scale,
        jnp.concatenate(key_parts, axis=1) * scale,
        jnp.concatenate(value_parts, axis=1),
    )


def heads_split(triple):
    return tuple((jnp.transpose(triple[:, index], (1, 0, 2)) for index in range(3)))


def head_forward(skip, item):
    triple, length = item
    spots = jnp.arange(triple.shape[0])
    query, keys, values = heads_split(triple)
    result, lse = attend(query, keys, values, spots, length)
    return (jnp.transpose(result, (1, 0, 2)).astype(jnp.bfloat16), lse)


def head_backward(skip, item):
    triple, grad_rows, lse, length = item
    spots = jnp.arange(triple.shape[0])
    query, keys, values = heads_split(triple)
    grads = attend_back(
        query, keys, values, spots, length, jnp.transpose(grad_rows, (1, 0, 2)), lse
    )
    return jnp.stack(grads, axis=0).transpose(2, 0, 1, 3).astype(jnp.bfloat16)


def factored(grad, weight_matrix, row, col):
    decay = 1.0 - STEP ** (-0.8)
    squares = grad * grad + STAT_EPS
    new_row = decay * row + (1.0 - decay) * jnp.mean(squares, axis=-1)
    new_col = decay * col + (1.0 - decay) * jnp.mean(squares, axis=-2)
    second = (
        new_row[..., :, None] * new_col[..., None, :] / jnp.mean(new_row, axis=-1)[..., None, None]
    )
    unit = grad * lax.rsqrt(second)
    level = jnp.sqrt(jnp.mean(unit * unit, axis=(-2, -1), keepdims=True))
    unit = unit / jnp.maximum(1.0, level / CLIP_LEVEL)
    rate = RATE * jnp.sqrt(jnp.mean(weight_matrix * weight_matrix, axis=(-2, -1), keepdims=True))
    return (weight_matrix - rate * (unit + DECAY_WEIGHT * weight_matrix), new_row, new_col)


LOG2E = 1.4426950408889634
NT = (((1,), (1,)), ((), ()))
TN = (((0,), (0,)), ((), ()))


def dotf(a, b, dims=(((1,), (0,)), ((), ()))):
    return lax.dot_general(a, b, dims, preferred_element_type=jnp.float32)


def triple(value):
    high = value.astype(jnp.bfloat16)
    rest = value - high.astype(jnp.float32)
    mid = rest.astype(jnp.bfloat16)
    low = (rest - mid.astype(jnp.float32)).astype(jnp.bfloat16)
    return high, mid, low


GELU_A = 0.7978845608028654
GELU_B = 0.7978845608028654 * 0.044715
RANK = 4


def norm_parts(values):
    centered = values - jnp.mean(values, axis=-1, keepdims=True)
    spread = jnp.mean(centered * centered, axis=-1, keepdims=True)
    scaled = lax.rsqrt(spread + NORM_EPS)
    return centered * scaled, scaled


def norm_back(grad, unit, scaled, gain):
    gained = grad * gain
    return scaled * (
        gained
        - jnp.mean(gained, axis=-1, keepdims=True)
        - unit * jnp.mean(gained * unit, axis=-1, keepdims=True)
    )


def low(value):
    return value.astype(jnp.bfloat16)


def wide(value):
    return value.astype(jnp.float32)


def gelu_pair(value):
    square = value * value
    half = 0.5 * value
    bent = jnp.tanh(value * (GELU_A + GELU_B * square))
    slope = (0.5 + 0.5 * bent) + half * (1.0 - bent * bent) * (GELU_A + 3.0 * GELU_B * square)
    return half + half * bent, slope


def peers_of(axis, size):
    me = lax.axis_index(axis)
    return me, [lax.rem(me + shift, size) for shift in range(1, size)]


def greet(axes):
    barrier = pltpu.get_barrier_semaphore()
    count = 0
    for axis, size in axes:
        _, peers = peers_of(axis, size)
        for peer in peers:
            pl.semaphore_signal(
                barrier, inc=1, device_id={axis: peer}, device_id_type=pl.DeviceIdType.MESH
            )
        count += len(peers)
    pl.semaphore_wait(barrier, count)


def send(source, target, sent, landed, axis, peer):
    return pltpu.make_async_remote_copy(
        src_ref=source,
        dst_ref=target,
        send_sem=sent,
        recv_sem=landed,
        device_id={axis: peer},
        device_id_type=pl.DeviceIdType.MESH,
    )


def sum_everywhere(
    splits, copies, part_ref, total_ref, seq_in, dp_in, own, s_sent, s_land, d_sent, d_land, g_sent, g_land
):
    size = part_ref.shape[1] // splits
    me, peers = peers_of("seq", splits)
    mine, others = peers_of("dp", copies)

    def columns(index):
        return pl.ds(pl.multiple_of(index * size, size), size)

    first = []
    for shift, peer in enumerate(peers):
        copy = send(part_ref.at[:, columns(peer)], seq_in.at[me], s_sent.at[shift], s_land.at[me], "seq", peer)
        copy.start()
        first.append(copy)
    seq_in[me] = part_ref[:, columns(me)]
    for peer in peers:
        send(part_ref.at[:, columns(me)], seq_in.at[peer], s_sent.at[0], s_land.at[peer], "seq", peer).wait_recv()
    summed = seq_in[0]
    for index in range(1, splits):
        summed = summed + seq_in[index]
    own[...] = summed
    second = []
    for shift, peer in enumerate(others):
        copy = send(own, dp_in.at[mine], d_sent.at[shift], d_land.at[mine], "dp", peer)
        copy.start()
        second.append(copy)
    dp_in[mine] = summed
    for peer in others:
        send(own, dp_in.at[peer], d_sent.at[0], d_land.at[peer], "dp", peer).wait_recv()
    summed = dp_in[0]
    for index in range(1, copies):
        summed = summed + dp_in[index]
    total_ref[:, columns(me)] = summed
    third = []
    for shift, peer in enumerate(peers):
        copy = send(
            total_ref.at[:, columns(me)], total_ref.at[:, columns(me)], g_sent.at[shift], g_land.at[me], "seq", peer
        )
        copy.start()
        third.append(copy)
    for peer in peers:
        part = total_ref.at[:, columns(peer)]
        send(part, part, g_sent.at[0], g_land.at[peer], "seq", peer).wait_recv()
    for copy in first + second + third:
        copy.wait_send()


def sum_scratch(splits, copies, width):
    size = width // splits
    dma = pltpu.SemaphoreType.DMA
    return [
        pltpu.VMEM((splits, 8, size), jnp.float32),
        pltpu.VMEM((copies, 8, size), jnp.float32),
        pltpu.VMEM((8, size), jnp.float32),
        dma((splits,)),
        dma((splits,)),
        dma((copies,)),
        dma((copies,)),
        dma((splits,)),
        dma((splits,)),
    ]


def across(column):
    count = column.shape[0]
    diagonal = lax.broadcasted_iota(jnp.int32, (count, count), 0) == lax.broadcasted_iota(
        jnp.int32, (count, count), 1
    )
    return jnp.sum(jnp.where(diagonal, jnp.broadcast_to(column, (count, count)), 0.0), axis=0, keepdims=True)


def upright(line):
    count = line.shape[1]
    diagonal = lax.broadcasted_iota(jnp.int32, (count, count), 0) == lax.broadcasted_iota(
        jnp.int32, (count, count), 1
    )
    return jnp.sum(jnp.where(diagonal, jnp.broadcast_to(line, (count, count)), 0.0), axis=1, keepdims=True)


def factored_step(grad, weight, short_line, long_line, rows_long):
    decay = 1.0 - STEP ** (-0.8)
    squares = grad * grad + STAT_EPS
    new_short = decay * upright(short_line) + (1.0 - decay) * jnp.mean(squares, axis=1, keepdims=True)
    new_long = decay * long_line + (1.0 - decay) * jnp.mean(squares, axis=0, keepdims=True)
    if rows_long:
        middle = jnp.mean(new_long, axis=1, keepdims=True)
    else:
        middle = jnp.mean(new_short, axis=0, keepdims=True)
    unit = grad * lax.rsqrt(new_short * new_long / middle)
    entries = grad.shape[0] * grad.shape[1]

    def mean_square(value):
        return jnp.sum(jnp.sum(value * value, axis=1, keepdims=True), axis=0, keepdims=True) / entries

    level = jnp.sqrt(mean_square(unit))
    unit = unit / jnp.maximum(1.0, level / CLIP_LEVEL)
    rate = RATE * jnp.sqrt(mean_square(weight))
    return weight - rate * (unit + DECAY_WEIGHT * weight), across(new_short), new_long


def update_kernel(
    total_ref, output_in, grad_in, dm, dh, uq, uh, um, row_dm, col_dm, row_dh, col_dh, row_uq, col_uq, row_uh, col_uh, row_um, col_um,
    output_out, grad_out, g_dm, g_dh, g_uq, g_uh, g_um, n_dm, n_dh, n_uq, n_uh, n_um,
    r_dm, r_dh, r_uq, r_uh, r_um, c_dm, c_dh, c_uq, c_uh, c_um, held_out, held_grad, sems,
):
    moves = [
        pltpu.make_async_copy(output_in, held_out, sems.at[0]),
        pltpu.make_async_copy(grad_in, held_grad, sems.at[1]),
    ]
    for move in moves:
        move.start()
    moves = [
        (moves[0], pltpu.make_async_copy(held_out, output_out, sems.at[0])),
        (moves[1], pltpu.make_async_copy(held_grad, grad_out, sems.at[1])),
    ]
    for move, onward in moves:
        move.wait()
        onward.start()
    width = dm.shape[2]
    hidden = dh.shape[1]
    for index in range(3):
        grad = total_ref[0:RANK, index * width : (index + 1) * width]
        g_dm[index] = grad
        n_dm[index], c_dm[index : index + 1, :], r_dm[index : index + 1, :] = factored_step(
            grad, dm[index], col_dm[index : index + 1, :], row_dm[index : index + 1, :], True
        )
    grad = total_ref[0:RANK, 3 * width : 6 * width]
    g_uq[...] = grad
    n_uq[...], r_uq[...], c_uq[...] = factored_step(grad, uq[...], row_uq[...], col_uq[...], False)
    for index in range(2):
        grad = total_ref[0:RANK, (6 + index) * width : (7 + index) * width]
        g_um[index] = grad
        n_um[index], r_um[index : index + 1, :], c_um[index : index + 1, :] = factored_step(
            grad, um[index], row_um[index : index + 1, :], col_um[index : index + 1, :], False
        )
    grad = total_ref[RANK : 2 * RANK, 0:hidden]
    g_dh[...] = grad
    n_dh[...], c_dh[...], r_dh[...] = factored_step(grad, dh[...], col_dh[...], row_dh[...], True)
    grad = total_ref[RANK : 2 * RANK, hidden : 2 * hidden]
    g_uh[...] = grad
    n_uh[...], r_uh[...], c_uh[...] = factored_step(grad, uh[...], row_uh[...], col_uh[...], False)
    for _, onward in moves:
        onward.wait()


def update(total, output, input_grad, adapters, row_dm, col_dm, row_dh, col_dh, row_uq, col_uq, row_uh, col_uh, row_um, col_um):
    flip = lambda array: jnp.swapaxes(array, -1, -2)
    line = lambda array: array.reshape(1, -1)
    given = [
        row_dm, col_dm, line(row_dh), line(col_dh), line(row_uq), line(col_uq), line(row_uh), line(col_uh), row_um, col_um,
    ]
    stats = given[0::2] + given[1::2]
    anyspace = pl.BlockSpec(memory_space=pl.ANY)
    vmem = pl.BlockSpec(memory_space=pltpu.VMEM)
    results = pl.pallas_call(
        update_kernel,
        out_shape=[jax.ShapeDtypeStruct(a.shape, a.dtype) for a in [output, input_grad] + adapters + adapters + stats],
        in_specs=[vmem, anyspace, anyspace] + [vmem] * 15,
        out_specs=[anyspace, anyspace] + [vmem] * 20,
        scratch_shapes=[
            pltpu.VMEM(output.shape, output.dtype),
            pltpu.VMEM(output.shape, output.dtype),
            pltpu.SemaphoreType.DMA((2,)),
        ],
        compiler_params=pltpu.CompilerParams(vmem_limit_bytes=24 * 2**20),
        name="factored_update",
    )(total, output, input_grad, *adapters, *given)
    results = list(results)
    for index in (2, 3, 7, 8):
        results[index] = flip(results[index])
    olds = (row_dm, row_dh, row_uq, row_uh, row_um, col_dm, col_dh, col_uq, col_uh, col_um)
    for index, old in zip(range(12, 22), olds):
        results[index] = results[index].reshape(old.shape)
    return tuple(results)


TILE = 256
GROUP = 4
LANES = 128


def peer_order(me, splits, far_first):
    half = splits // 2
    side, place = me // half, lax.rem(me, half)
    far = [(1 - side) * half + lax.rem(place + shift, half) for shift in range(half)]
    near = [side * half + lax.rem(place + shift, half) for shift in range(1, half)]
    return far + near if far_first else near + far


def fill_adapters(dm_ref, dh_ref, uq_ref, uh_ref, um_ref, aq, ap, a1, a2, bq, bp, b2, b1):
    for index, ref in enumerate((aq, ap, a1)):
        ref[...] = low(dm_ref[index])
    a2[...] = low(dh_ref[...])
    for ref, value in ((bq, uq_ref[...]), (bp, um_ref[0]), (b2, um_ref[1]), (b1, uh_ref[...])):
        ref[...] = low(ADAPTER_SCALE * wide(low(value)))


def adapter_scratch(width, hidden):
    sizes = [width, width, width, hidden, 3 * width, width, width, hidden]
    return [pltpu.VMEM((RANK, size), jnp.bfloat16) for size in sizes]


def forward_kernel(
    splits, solo,
    lengths_ref, inputs, cotangent, wqkv_hbm, wo_hbm, w1_hbm, w2_hbm,
    bias_ref, gain_ref, shift_ref, dm_ref, dh_ref, uq_ref, uh_ref, um_ref,
    x_out, cot_out, out_out, qx_out, kx_out, vx_out, att_out, mid_out, nmid_out, act_out, slope_out, narrow_out,
    xr, wqkv, wo, w1, w2, kx, vx, qs, qb, att, mid, nmid, act, slope, outs, narrow,
    aq, ap, a1, a2, bq, bp, b2, b1,
    w_sem, x_sent, x_land, c_sent, c_land, o_sem, kv_sem, own_sem,
):
    me = 0 if solo else lax.axis_index("seq")
    span, width = xr.shape[1], xr.shape[2]
    total = splits * span
    hidden = w1.shape[1]
    blocks = TILE // span
    heads = kx.shape[0]
    half = LANES // 2
    length = lengths_ref[me]
    loads = [
        pltpu.make_async_copy(source, target, w_sem.at[index])
        for index, (source, target) in enumerate(((wqkv_hbm, wqkv), (wo_hbm, wo), (w1_hbm, w1), (w2_hbm, w2)))
    ]
    own_x = pltpu.make_async_copy(inputs.at[me], xr.at[me], own_sem.at[0])
    own_c = pltpu.make_async_copy(cotangent.at[me], cot_out.at[me], own_sem.at[1])
    save_x = pltpu.make_async_copy(xr, x_out, own_sem.at[2])
    if not solo:
        greet((("seq", splits),))
        own_x.start()
    else:
        all_x = pltpu.make_async_copy(inputs, xr, own_sem.at[0])
        all_x.start()
    loads[0].start()

    def x_copy(peer, slot):
        return send(inputs.at[peer], xr.at[me], x_sent.at[slot], x_land.at[me], "seq", peer)

    def c_copy(peer, slot):
        return send(cotangent.at[peer], cot_out.at[me], c_sent.at[slot], c_land.at[me], "seq", peer)

    if not solo:
        pair = me // 2
        outward = jnp.logical_or(pair == 0, pair == splits // 2 - 2)

        @pl.when(outward)
        def _():
            for slot, peer in enumerate(peer_order(me, splits, True)):
                x_copy(peer, slot).start()

        @pl.when(jnp.logical_not(outward))
        def _():
            for slot, peer in enumerate(peer_order(me, splits, False)):
                x_copy(peer, slot).start()

    for load in loads[1:]:
        load.start()
    fill_adapters(dm_ref, dh_ref, uq_ref, uh_ref, um_ref, aq, ap, a1, a2, bq, bp, b2, b1)
    if solo:
        all_x.wait()
    else:
        own_x.wait()

    lane = lax.broadcasted_iota(jnp.int32, (TILE, LANES), 1)
    row = lax.broadcasted_iota(jnp.int32, (TILE, TILE), 0)
    col = lax.broadcasted_iota(jnp.int32, (TILE, TILE), 1)
    causal = col <= row
    zero = jnp.zeros((TILE, LANES), jnp.bfloat16)
    one = jnp.ones((TILE, LANES), jnp.bfloat16)
    scale = jnp.asarray(half ** (-0.5), jnp.bfloat16)
    owns = (lane < half, lane >= half)
    spares = (half, 0)

    def bias(start, size):
        return wide(bias_ref[0:1, start : start + size])

    def saves(tile):
        rows = pl.ds(tile * TILE, TILE)
        return [
            pltpu.make_async_copy(source, target, o_sem.at[index])
            for index, (source, target) in enumerate(
                (
                    (qb, qx_out.at[:, rows, :]),
                    (att, att_out.at[:, rows, :]),
                    (mid, mid_out.at[rows, :]),
                    (nmid, nmid_out.at[rows, :]),
                    (act, act_out.at[rows, :]),
                    (slope, slope_out.at[rows, :]),
                    (outs, out_out.at[rows, :]),
                    (narrow, narrow_out.at[rows, :]),
                )
            )
        ]

    def kv_saves(tile):
        rows = pl.ds(tile * TILE, TILE)
        return [
            pltpu.make_async_copy(kx.at[:, rows, :], kx_out.at[:, rows, :], kv_sem.at[2 * tile]),
            pltpu.make_async_copy(vx.at[:, rows, :], vx_out.at[:, rows, :], kv_sem.at[2 * tile + 1]),
        ]

    tiles = total // TILE
    for tile in range(tiles):
        begin, end = tile * TILE, (tile + 1) * TILE
        for block in range(tile * blocks, (tile + 1) * blocks):
            if solo:
                continue

            @pl.when(me != block)
            def _():
                send(inputs.at[block], xr.at[block], x_sent.at[0], x_land.at[block], "seq", block).wait_recv()

        if tile == tiles - 1 and not solo:
            save_x.start()
            own_c.start()
            for slot, peer in enumerate(peer_order(me, splits, True)):
                c_copy(peer, slot).start()
        if tile == 0:
            loads[0].wait()
        else:
            saves(tile - 1)[7].wait()
        x = wide(xr[tile * blocks : (tile + 1) * blocks].reshape(TILE, width))
        unit, _ = norm_parts(x)
        normed = low(unit * wide(gain_ref[0:1, :]) + wide(shift_ref[0:1, :]))
        narrow_q = low(dotf(normed, aq[...], NT))
        narrow[:, 0:RANK] = narrow_q
        spot = begin + lax.broadcasted_iota(jnp.int32, (TILE, LANES), 0)
        valid = spot < length
        limit = jnp.where(valid, 0.0, MASKED).astype(jnp.bfloat16)
        size = 512
        for part in range(3):
            for start in range(0, width, size):
                column = part * width + start
                value = dotf(normed, wqkv[:, column : column + size]) + dotf(narrow_q, bq[:, column : column + size])
                if part == 0:
                    value = value + bias(start, size)
                if part == 2:
                    value = value + bias(width + start, size)
                value = low(value)
                for index in range(size // LANES):
                    piece = value[:, index * LANES : (index + 1) * LANES]
                    for parity in range(2):
                        head = 2 * (start // LANES + index) + parity
                        own, spare = owns[parity], spares[parity]
                        if part == 0:
                            qs[head] = jnp.where(own, piece * scale, jnp.where(lane == spare + 3, one, zero))
                        elif part == 1:
                            extra = jnp.where(lane == spare + 3, limit, jnp.where(lane < spare + 3, one, zero))
                            kx[head, begin:end, :] = jnp.where(own, piece, extra)
                        else:
                            vx[head, begin:end, :] = jnp.where(own, piece, one)
        for save in kv_saves(tile):
            save.start()
        if tile:
            for save in saves(tile - 1)[0:2]:
                save.wait()

        def attend(index, carry):
            def scores(unit):
                head = index * GROUP + unit
                return dotf(qs[head], kx[head, 0:end, :], NT)

            def mix(unit, value):
                head = index * GROUP + unit
                last = jnp.where(causal, value[:, begin:], MASKED)
                value = jnp.concatenate([value[:, :begin], last], axis=1) if begin else last
                top = jnp.max(value, axis=-1, keepdims=True)
                weights = low(jnp.exp2((value - top) * LOG2E))
                mixed = dotf(weights, vx[head, 0:end, :])
                spare, own = spares[unit % 2], owns[unit % 2]
                summed = mixed[:, spare : spare + 1]
                back = jnp.where(valid, -(top + jnp.log(summed)), MASKED)
                high, middle, rest = triple(back)
                extra = jnp.where(
                    lane == spare, high, jnp.where(lane == spare + 1, middle, jnp.where(lane == spare + 2, rest, zero))
                )
                qb[head] = jnp.where(own, qs[head], extra)
                return mixed * (1.0 / summed)

            ahead = scores(0)
            results = []
            for unit in range(GROUP):
                value = ahead
                if unit + 1 < GROUP:
                    ahead = scores(unit + 1)
                results.append(mix(unit, value))
            for unit in range(0, GROUP, 2):
                att[index * (GROUP // 2) + unit // 2] = low(jnp.where(owns[0], results[unit], results[unit + 1]))
            return carry

        lax.fori_loop(0, heads // GROUP, attend, 0)
        for save in saves(tile)[0:2]:
            save.start()
        if tile == 0:
            for load in loads[1:]:
                load.wait()
        else:
            for save in saves(tile - 1)[2:7]:
                save.wait()
        attended = jnp.concatenate([att[index] for index in range(heads // 2)], axis=1)
        narrow_p = low(dotf(attended, ap[...], NT))
        middle = (
            wide(xr[tile * blocks : (tile + 1) * blocks].reshape(TILE, width))
            + dotf(attended, wo[...])
            + bias(2 * width, width)
            + dotf(narrow_p, bp[...])
        )
        mid[...] = middle
        unit, _ = norm_parts(middle)
        normed = low(unit * wide(gain_ref[1:2, :]) + wide(shift_ref[1:2, :]))
        nmid[...] = normed
        narrow_1 = low(dotf(normed, a1[...], NT))
        size = 256

        def expand(start):
            return (
                dotf(normed, w1[:, start : start + size])
                + bias(3 * width + start, size)
                + dotf(narrow_1, b1[:, start : start + size])
            )

        result = middle + bias(3 * width + hidden, width)
        narrow_2 = jnp.zeros((TILE, RANK), jnp.float32)
        ahead = expand(0)
        for start in range(0, hidden, size):
            stop = start + size
            before = ahead
            if stop < hidden:
                ahead = expand(stop)
            active, bend = gelu_pair(before)
            active = low(active)
            act[:, start:stop] = active
            slope[:, start:stop] = low(bend)
            result = result + dotf(active, w2[start:stop, :])
            narrow_2 = narrow_2 + dotf(active, a2[:, start:stop], NT)
        narrow_2 = low(narrow_2)
        outs[...] = low(result + dotf(narrow_2, b2[...]))
        narrow[:, RANK : 2 * RANK] = narrow_p
        narrow[:, 2 * RANK : 3 * RANK] = narrow_1
        narrow[:, 3 * RANK : 4 * RANK] = narrow_2
        for save in saves(tile)[2:8]:
            save.start()

    for save in saves(tiles - 1):
        save.wait()
    for tile in range(tiles):
        for save in kv_saves(tile):
            save.wait()
    if solo:
        return
    save_x.wait()
    own_c.wait()
    for slot, peer in enumerate(peer_order(me, splits, True)):
        x_copy(peer, slot).wait_send()
        c_copy(peer, slot).wait_send()
        send(cotangent.at[me], cot_out.at[peer], c_sent.at[slot], c_land.at[peer], "seq", peer).wait_recv()


def forward(splits, solo, lengths, inputs, cotangent, small, weights):
    rows, span, width = inputs.shape
    total = splits * span
    hidden = weights[2].shape[1]
    heads = 2 * width // LANES
    anyspace = pl.BlockSpec(memory_space=pl.ANY)
    vmem = pl.BlockSpec(memory_space=pltpu.VMEM)
    bf, f32 = jnp.bfloat16, jnp.float32
    shapes = [
        ((splits, span, width), bf),
        ((splits, span, width), bf),
        ((total, width), bf),
        ((heads, total, LANES), bf),
        ((heads, total, LANES), bf),
        ((heads, total, LANES), bf),
        ((heads // 2, total, LANES), bf),
        ((total, width), f32),
        ((total, width), bf),
        ((total, hidden), bf),
        ((total, hidden), bf),
        ((total, LANES), bf),
    ]
    dma = pltpu.SemaphoreType.DMA
    tiles = total // TILE
    return pl.pallas_call(
        lambda *refs: forward_kernel(splits, solo, *refs),
        out_shape=[jax.ShapeDtypeStruct(s, d) for s, d in shapes],
        in_specs=[pl.BlockSpec(memory_space=pltpu.SMEM)] + [anyspace] * 6 + [vmem] * len(small),
        out_specs=[anyspace] * len(shapes),
        scratch_shapes=[
            pltpu.VMEM((splits, span, width), bf),
            *[pltpu.VMEM(w.shape, bf) for w in weights],
            pltpu.VMEM((heads, total, LANES), bf),
            pltpu.VMEM((heads, total, LANES), bf),
            pltpu.VMEM((heads, TILE, LANES), bf),
            pltpu.VMEM((heads, TILE, LANES), bf),
            pltpu.VMEM((heads // 2, TILE, LANES), bf),
            pltpu.VMEM((TILE, width), f32),
            pltpu.VMEM((TILE, width), bf),
            pltpu.VMEM((TILE, hidden), bf),
            pltpu.VMEM((TILE, hidden), bf),
            pltpu.VMEM((TILE, width), bf),
            pltpu.VMEM((TILE, LANES), bf),
            *adapter_scratch(width, hidden),
            dma((4,)),
            dma((splits,)),
            dma((splits,)),
            dma((splits,)),
            dma((splits,)),
            dma((8,)),
            dma((2 * tiles,)),
            dma((3,)),
        ],
        compiler_params=pltpu.CompilerParams(
            collective_id=None if solo else 2, has_side_effects=not solo, vmem_limit_bytes=62 * 2**20
        ),
        name="forward",
    )(lengths, inputs, cotangent, *weights, *small)


def backward_kernel(
    splits, copies, solo,
    lengths_ref, x_row, cot_row, out_row, qx_hbm, kx_hbm, vx_hbm, att_hbm, mid_hbm, nmid_hbm, act_hbm, slope_hbm,
    narrow_hbm, wqkv_hbm, wo_hbm, w1_hbm, w2_hbm,
    gain_ref, shift_ref, dm_ref, dh_ref, uq_ref, uh_ref, um_ref,
    output, dx_out, total_ref,
    wqkv, wo, w1, w2, kx, vx, dk, dv, x_t, cot_t, mid_t, nmid_t, act_t, slope_t, narrow_t, att_t, qx_t,
    gx, dq, gmid, dx_s, part, aq, ap, a1, a2, bq, bp, b2, b1,
    w_sem, t_sem, kv_sem, own_sem, f_sent, f_land, b_sent, b_land,
    *sum_refs,
):
    me = 0 if solo else lax.axis_index("seq")
    span, width = x_t.shape[1], x_t.shape[2]
    hidden = w1.shape[1]
    blocks = TILE // span
    total = splits * span
    tiles = total // TILE
    heads = kx.shape[0]
    half = LANES // 2
    length = lengths_ref[me]
    scale = half ** (-0.5)

    def load_first(tile):
        rows = pl.ds(tile * TILE, TILE)
        pairs = (
            (cot_row.at[pl.ds(tile * blocks, blocks)], cot_t),
            (slope_hbm.at[rows, :], slope_t),
            (act_hbm.at[rows, :], act_t),
            (narrow_hbm.at[rows, :], narrow_t),
            (mid_hbm.at[rows, :], mid_t),
            (nmid_hbm.at[rows, :], nmid_t),
            (att_hbm.at[:, rows, :], att_t),
        )
        return [pltpu.make_async_copy(a, b, t_sem.at[i]) for i, (a, b) in enumerate(pairs)]

    def load_q(tile):
        return pltpu.make_async_copy(qx_hbm.at[:, pl.ds(tile * TILE, TILE), :], qx_t, t_sem.at[7])

    def load_x(tile):
        return pltpu.make_async_copy(x_row.at[pl.ds(tile * blocks, blocks)], x_t, t_sem.at[8])

    get_w2, get_w1, get_wo, get_wqkv = (
        pltpu.make_async_copy(source, target, w_sem.at[index])
        for index, (source, target) in enumerate(((w2_hbm, w2), (w1_hbm, w1), (wo_hbm, wo), (wqkv_hbm, wqkv)))
    )
    get_k = pltpu.make_async_copy(kx_hbm, kx, kv_sem.at[0])
    get_v = pltpu.make_async_copy(vx_hbm, vx, kv_sem.at[1])
    own_f = pltpu.make_async_copy(out_row.at[me], output.at[me], own_sem.at[0])
    own_b = pltpu.make_async_copy(dx_s.at[me], dx_out.at[me], own_sem.at[1])

    first = load_first(tiles - 1)
    first[0].start()
    get_w2.start()
    for load in first[1:4]:
        load.start()
    get_w1.start()
    for load in first[4:]:
        load.start()
    get_wo.start()
    load_q(tiles - 1).start()
    get_k.start()
    get_v.start()
    get_wqkv.start()
    load_x(tiles - 1).start()
    if not solo:
        greet((("seq", splits), ("dp", copies)))
        own_f.start()
        for slot, peer in enumerate(peer_order(me, splits, True)):
            send(out_row.at[peer], output.at[me], f_sent.at[slot], f_land.at[me], "seq", peer).start()
    fill_adapters(dm_ref, dh_ref, uq_ref, uh_ref, um_ref, aq, ap, a1, a2, bq, bp, b2, b1)
    part[...] = jnp.zeros_like(part)

    lane = lax.broadcasted_iota(jnp.int32, (TILE, LANES), 1)
    row = lax.broadcasted_iota(jnp.int32, (TILE, TILE), 0)
    col = lax.broadcasted_iota(jnp.int32, (TILE, TILE), 1)
    causal = row <= col
    zero = jnp.zeros((TILE, LANES), jnp.bfloat16)
    owns = (lane < half, lane >= half)
    spares = (half, 0)

    def add_upper(start, value):
        part[0:RANK, start : start + value.shape[1]] += value

    def add_lower(start, value):
        part[RANK : 2 * RANK, start : start + value.shape[1]] += value

    def b_copy(block):
        return send(dx_s.at[block], dx_out.at[me], b_sent.at[block], b_land.at[me], "seq", block)

    for tile in reversed(range(tiles)):
        begin, end = tile * TILE, (tile + 1) * TILE
        newest = tile == tiles - 1
        for load in load_first(tile):
            load.wait()
        if newest:
            get_w2.wait()
            get_w1.wait()
        spot = begin + lax.broadcasted_iota(jnp.int32, (TILE, width), 0)
        given = cot_t[...].reshape(TILE, width)
        gout = jnp.where(spot < length, given, jnp.zeros_like(given))
        narrow_q = narrow_t[:, 0:RANK]
        narrow_p = narrow_t[:, RANK : 2 * RANK]
        narrow_1 = narrow_t[:, 2 * RANK : 3 * RANK]
        narrow_2 = narrow_t[:, 3 * RANK : 4 * RANK]
        gn2 = low(dotf(gout, b2[...], NT))
        add_upper(7 * width, dotf(narrow_2, gout, TN))
        size = 512

        def contract(start):
            return dotf(gout, w2[start : start + size, :], NT) + dotf(gn2, a2[:, start : start + size])

        gnorm = jnp.zeros((TILE, width), jnp.float32)
        gn1 = jnp.zeros((TILE, RANK), jnp.float32)
        ahead = contract(0)
        for start in range(0, hidden, size):
            stop = start + size
            gact = ahead
            if stop < hidden:
                ahead = contract(stop)
            gbefore = low(gact * wide(slope_t[:, start:stop]))
            add_lower(start, dotf(gn2, act_t[:, start:stop], TN))
            add_lower(hidden + start, dotf(narrow_1, gbefore, TN))
            gn1 = gn1 + dotf(gbefore, b1[:, start:stop], NT)
            gnorm = gnorm + dotf(gbefore, w1[:, start:stop], NT)
        gn1 = low(gn1)
        gnorm = gnorm + dotf(gn1, a1[...])
        add_upper(2 * width, dotf(gn1, nmid_t[...], TN))
        unit, scaled = norm_parts(mid_t[...])
        grad = wide(gout) + norm_back(gnorm, unit, scaled, wide(gain_ref[1:2, :]))
        gmid[...] = grad
        glow = low(grad)
        if newest:
            get_wo.wait()
        gnp = low(dotf(glow, bp[...], NT))
        add_upper(6 * width, dotf(narrow_p, glow, TN))
        gatt = low(dotf(glow, wo[...], NT) + dotf(gnp, ap[...]))
        attended = jnp.concatenate([att_t[index] for index in range(heads // 2)], axis=1)
        add_upper(width, dotf(gnp, attended, TN))
        for index in range(heads // 2):
            piece = gatt[:, index * LANES : (index + 1) * LANES]
            product = wide(piece) * wide(att_t[index])
            for parity in range(2):
                own, spare = owns[parity], spares[parity]
                delta = -jnp.sum(jnp.where(own, product, 0.0), axis=-1, keepdims=True)
                high, middle, rest = triple(jnp.broadcast_to(delta, (TILE, LANES)))
                extra = jnp.where(
                    lane == spare, high, jnp.where(lane == spare + 1, middle, jnp.where(lane == spare + 2, rest, zero))
                )
                gx[2 * index + parity] = jnp.where(own, piece, extra)
        if tile:
            for load in load_first(tile - 1):
                load.start()
        load_q(tile).wait()
        if newest:
            get_k.wait()
            get_v.wait()

        def attend(index, carry):
            def products(unit):
                head = index * GROUP + unit
                return (
                    dotf(kx[head, 0:end, :], qx_t[head], NT),
                    dotf(vx[head, 0:end, :], gx[head], NT),
                )

            def spread(unit, scores, dprob):
                head = index * GROUP + unit
                weights = jnp.exp2(scores * LOG2E)
                last = jnp.where(causal, weights[begin:], 0.0)
                weights = jnp.concatenate([weights[:begin], last], axis=0) if begin else last
                dscore = low(weights * dprob)
                return (
                    dotf(dscore, kx[head, 0:end, :], TN),
                    dotf(dscore, qx_t[head]),
                    dotf(low(weights), gx[head]),
                )

            ahead = products(0)
            results = []
            for unit in range(GROUP):
                given = ahead
                if unit + 1 < GROUP:
                    ahead = products(unit + 1)
                results.append(spread(unit, *given))
            first_lanes = lax.broadcasted_iota(jnp.int32, (end, LANES), 1) < half
            for unit in range(0, GROUP, 2):
                pair = index * (GROUP // 2) + unit // 2
                even, odd = results[unit], results[unit + 1]
                dq[pair] = low(jnp.where(owns[0], even[0], odd[0]) * scale)
                more_k = jnp.where(first_lanes, even[1], odd[1])
                more_v = jnp.where(first_lanes, even[2], odd[2])
                if newest:
                    dk[pair] = more_k
                    dv[pair] = more_v
                else:
                    dk[pair, 0:end, :] += more_k
                    dv[pair, 0:end, :] += more_v
            return carry

        lax.fori_loop(0, heads // GROUP, attend, 0)
        if tile:
            load_q(tile - 1).start()
        load_x(tile).wait()
        if newest:
            get_wqkv.wait()
        pairs = range(heads // 2)
        parts = [
            jnp.concatenate([dq[index] for index in pairs], axis=1),
            jnp.concatenate([low(dk[index, begin:end, :]) for index in pairs], axis=1),
            jnp.concatenate([low(dv[index, begin:end, :]) for index in pairs], axis=1),
        ]
        gnq = jnp.zeros((TILE, RANK), jnp.float32)
        gnormed = jnp.zeros((TILE, width), jnp.float32)
        for index, value in enumerate(parts):
            start, stop = index * width, (index + 1) * width
            gnq = gnq + dotf(value, bq[:, start:stop], NT)
            add_upper(3 * width + start, dotf(narrow_q, value, TN))
            gnormed = gnormed + dotf(value, wqkv[:, start:stop], NT)
        gnq = low(gnq)
        gnormed = gnormed + dotf(gnq, aq[...])
        unit, scaled = norm_parts(wide(x_t[...].reshape(TILE, width)))
        normed = low(unit * wide(gain_ref[0:1, :]) + wide(shift_ref[0:1, :]))
        add_upper(0, dotf(gnq, normed, TN))
        dx = low(gmid[...] + norm_back(gnormed, unit, scaled, wide(gain_ref[0:1, :])))
        dx_s[tile * blocks : (tile + 1) * blocks] = dx.reshape(blocks, span, width)
        if tile:
            load_x(tile - 1).start()
        if not solo:
            for block in range(tile * blocks, (tile + 1) * blocks):

                @pl.when(me != block)
                def _():
                    b_copy(block).start()

                @pl.when(me == block)
                def _():
                    own_b.start()

    part[0:RANK, 3 * width :] = ADAPTER_SCALE * part[0:RANK, 3 * width :]
    part[RANK : 2 * RANK, hidden:] = ADAPTER_SCALE * part[RANK : 2 * RANK, hidden:]
    if solo:
        total_ref[...] = part[...]
        return
    sum_everywhere(splits, copies, part, total_ref, *sum_refs)
    own_f.wait()
    own_b.wait()
    for slot, peer in enumerate(peer_order(me, splits, True)):
        send(out_row.at[peer], output.at[peer], f_sent.at[slot], f_land.at[peer], "seq", peer).wait()
        send(dx_s.at[peer], dx_out.at[peer], b_sent.at[peer], b_land.at[peer], "seq", peer).wait()


def backward(splits, copies, solo, lengths, saved, weights, small):
    span, width = saved[0].shape[1:]
    hidden = weights[2].shape[1]
    total = splits * span
    heads = saved[3].shape[0]
    blocks = TILE // span
    anyspace = pl.BlockSpec(memory_space=pl.ANY)
    vmem = pl.BlockSpec(memory_space=pltpu.VMEM)
    bf, f32 = jnp.bfloat16, jnp.float32
    dma = pltpu.SemaphoreType.DMA
    scratch = [
        *[pltpu.VMEM(w.shape, bf) for w in weights],
        pltpu.VMEM((heads, total, LANES), bf),
        pltpu.VMEM((heads, total, LANES), bf),
        pltpu.VMEM((heads // 2, total, LANES), f32),
        pltpu.VMEM((heads // 2, total, LANES), f32),
        pltpu.VMEM((blocks, span, width), bf),
        pltpu.VMEM((blocks, span, width), bf),
        pltpu.VMEM((TILE, width), f32),
        pltpu.VMEM((TILE, width), bf),
        pltpu.VMEM((TILE, hidden), bf),
        pltpu.VMEM((TILE, hidden), bf),
        pltpu.VMEM((TILE, LANES), bf),
        pltpu.VMEM((heads // 2, TILE, LANES), bf),
        pltpu.VMEM((heads, TILE, LANES), bf),
        pltpu.VMEM((heads, TILE, LANES), bf),
        pltpu.VMEM((heads // 2, TILE, LANES), bf),
        pltpu.VMEM((TILE, width), f32),
        pltpu.VMEM((splits, span, width), bf),
        pltpu.VMEM((2 * RANK, 8 * width), f32),
        *adapter_scratch(width, hidden),
        dma((4,)),
        dma((9,)),
        dma((2,)),
        dma((2,)),
        dma((splits,)),
        dma((splits,)),
        dma((splits,)),
        dma((splits,)),
    ]
    if not solo:
        scratch += sum_scratch(splits, copies, 8 * width)
    return pl.pallas_call(
        lambda *refs: backward_kernel(splits, copies, solo, *refs),
        out_shape=[
            jax.ShapeDtypeStruct((splits, span, width), bf),
            jax.ShapeDtypeStruct((splits, span, width), bf),
            jax.ShapeDtypeStruct((2 * RANK, 8 * width), f32),
        ],
        in_specs=[pl.BlockSpec(memory_space=pltpu.SMEM)]
        + [anyspace] * (len(saved) + len(weights))
        + [vmem] * len(small),
        out_specs=[anyspace, anyspace, vmem],
        scratch_shapes=scratch,
        compiler_params=pltpu.CompilerParams(
            collective_id=None if solo else 3, has_side_effects=not solo, vmem_limit_bytes=63 * 2**20
        ),
        name="backward",
    )(lengths, *saved, *weights, *small)


def local_by_heads(
    inputs,
    cotangent,
    lengths,
    norm_gain,
    norm_shift,
    query_key_value_weight,
    output_projection_weight,
    first_feedforward_weight,
    second_feedforward_weight,
    biases,
    down_model,
    down_hidden,
    query_key_value_upward,
    hidden_adapter_upward,
    model_adapter_upward,
    row_down_model,
    col_down_model,
    row_down_hidden,
    col_down_hidden,
    row_up_qkv,
    col_up_qkv,
    row_up_hidden,
    col_up_hidden,
    row_up_model,
    col_up_model,
):
    rows, span, width = inputs.shape
    hidden_width = first_feedforward_weight.shape[1]
    count = rows * span
    spots = lax.axis_index("seq") * span + jnp.arange(span)
    keep = (spots[None, :] < lengths[:, None]).astype(jnp.float32).reshape(count, 1)
    flat = inputs.reshape(count, width).astype(jnp.float32)
    shifts = biases.astype(jnp.float32)
    query_bias = shifts[0:width]
    value_bias = shifts[width : 2 * width]
    projection_bias = shifts[2 * width : 3 * width]
    expand_bias_vector = shifts[3 * width : 3 * width + hidden_width]
    contract_bias_vector = shifts[3 * width + hidden_width : 4 * width + hidden_width]
    query_key_value_bias = jnp.concatenate([query_bias, jnp.zeros_like(query_bias), value_bias])
    gains = norm_gain.astype(jnp.float32)
    offsets = norm_shift.astype(jnp.float32)
    down_low = down_model.astype(jnp.bfloat16)
    hidden_down_low = down_hidden.astype(jnp.bfloat16)
    qkv_up_low = query_key_value_upward.astype(jnp.bfloat16)
    hidden_up_low = hidden_adapter_upward.astype(jnp.bfloat16)
    model_up_low = model_adapter_upward.astype(jnp.bfloat16)
    normalized_rows, unit_first, scaled_first = normalize(flat, gains[0], offsets[0])
    normalized_rows = normalized_rows.astype(jnp.bfloat16)
    mixed_rows, narrow_qkv = adapted(
        normalized_rows, query_key_value_weight, query_key_value_bias, down_low[0], qkv_up_low
    )
    mixed_rows = mixed_rows.astype(jnp.bfloat16).reshape(rows, span, 3, HEADS, HEAD_DIM)
    by_head = lax.all_to_all(mixed_rows, "seq", split_axis=3, concat_axis=1, tiled=True)
    out_heads, lse = lax.map(partial(head_forward, False), (by_head, lengths))
    attended_rows = jax.tree.map(
        lambda part, own: part.astype(own.dtype),
        lax.all_to_all(as_sent(out_heads), "seq", split_axis=1, concat_axis=2, tiled=True),
        out_heads,
    )
    attended_rows = attended_rows.reshape(count, width)
    branch_path, narrow_proj = adapted(
        attended_rows, output_projection_weight, projection_bias, down_low[1], model_up_low[0]
    )
    middle = flat + branch_path
    normed_mid, unit_second, scaled_second = normalize(middle, gains[1], offsets[1])
    normed_mid = normed_mid.astype(jnp.bfloat16)
    before, narrow_expand = adapted(
        normed_mid, first_feedforward_weight, expand_bias_vector, down_low[2], hidden_up_low
    )
    activated, gelu_pull = jax.vjp(lambda value: jax.nn.gelu(value, approximate=True), before)
    activated = activated.astype(jnp.bfloat16)
    branch_out, narrow_contract = adapted(
        activated, second_feedforward_weight, contract_bias_vector, hidden_down_low, model_up_low[1]
    )
    output = (middle + branch_out).astype(jnp.bfloat16).reshape(rows, span, width)
    grad_out = cotangent.reshape(count, width).astype(jnp.float32) * keep
    grad_act, grad_down_contract, grad_up_contract = adapted_back(
        grad_out.astype(jnp.bfloat16),
        activated,
        second_feedforward_weight,
        hidden_down_low,
        model_up_low[1],
        narrow_contract,
    )
    grad_before = gelu_pull(grad_act)[0].astype(jnp.bfloat16)
    grad_norm_mid, grad_down_expand, grad_up_expand = adapted_back(
        grad_before, normed_mid, first_feedforward_weight, down_low[2], hidden_up_low, narrow_expand
    )
    grad_mid = grad_out + normalize_back(grad_norm_mid, unit_second, scaled_second, gains[1])
    grad_att, grad_down_proj, grad_up_proj = adapted_back(
        grad_mid.astype(jnp.bfloat16),
        attended_rows,
        output_projection_weight,
        down_low[1],
        model_up_low[0],
        narrow_proj,
    )
    grad_att = grad_att.astype(jnp.bfloat16).reshape(rows, span, HEADS, HEAD_DIM)
    grad_heads = lax.all_to_all(grad_att, "seq", split_axis=2, concat_axis=1, tiled=True)
    grad_triple = lax.map(partial(head_backward, False), (by_head, grad_heads, lse, lengths))
    grad_mixed = jax.tree.map(
        lambda part, own: part.astype(own.dtype),
        lax.all_to_all(as_sent(grad_triple), "seq", split_axis=1, concat_axis=3, tiled=True),
        grad_triple,
    )
    grad_mixed = grad_mixed.reshape(count, 3 * width)
    grad_normed, grad_down_qkv, grad_up_qkv = adapted_back(
        grad_mixed, normalized_rows, query_key_value_weight, down_low[0], qkv_up_low, narrow_qkv
    )
    input_grad = (
        (grad_mid + normalize_back(grad_normed, unit_first, scaled_first, gains[0]))
        .astype(jnp.bfloat16)
        .reshape(rows, span, width)
    )
    grads = lax.psum(
        (
            jnp.stack([grad_down_qkv, grad_down_proj, grad_down_expand]),
            grad_down_contract,
            grad_up_qkv,
            grad_up_expand,
            jnp.stack([grad_up_proj, grad_up_contract]),
        ),
        ("dp", "seq"),
    )
    grad_dm, grad_dh, grad_uq, grad_uh, grad_um = grads
    new_dm, row_dm, col_dm = factored(grad_dm, down_model, row_down_model, col_down_model)
    new_dh, row_dh, col_dh = factored(grad_dh, down_hidden, row_down_hidden, col_down_hidden)
    new_uq, row_uq, col_uq = factored(grad_uq, query_key_value_upward, row_up_qkv, col_up_qkv)
    new_uh, row_uh, col_uh = factored(grad_uh, hidden_adapter_upward, row_up_hidden, col_up_hidden)
    new_um, row_um, col_um = factored(grad_um, model_adapter_upward, row_up_model, col_up_model)
    return (
        output,
        input_grad,
        grad_dm,
        grad_dh,
        grad_uq,
        grad_uh,
        grad_um,
        new_dm,
        new_dh,
        new_uq,
        new_uh,
        new_um,
        row_dm,
        row_dh,
        row_uq,
        row_uh,
        row_um,
        col_dm,
        col_dh,
        col_uq,
        col_uh,
        col_um,
    )


def local_by_rows(
    pieces,
    copies,
    inputs,
    cotangent,
    lengths,
    norm_gain,
    norm_shift,
    query_key_value_weight,
    output_projection_weight,
    first_feedforward_weight,
    second_feedforward_weight,
    biases,
    down_model,
    down_hidden,
    query_key_value_upward,
    hidden_adapter_upward,
    model_adapter_upward,
    row_down_model,
    col_down_model,
    row_down_hidden,
    col_down_hidden,
    row_up_qkv,
    col_up_qkv,
    row_up_hidden,
    col_up_hidden,
    row_up_model,
    col_up_model,
):
    flip = lambda array: jnp.swapaxes(array, -1, -2)
    adapters = [
        flip(down_model),
        flip(down_hidden),
        query_key_value_upward,
        hidden_adapter_upward,
        model_adapter_upward,
    ]
    norms = [norm_gain, norm_shift]
    weights = [
        query_key_value_weight,
        output_projection_weight,
        first_feedforward_weight,
        second_feedforward_weight,
    ]
    saved = list(forward(
        pieces, False, lengths, inputs, cotangent, [biases.reshape(1, -1)] + norms + adapters, weights
    ))
    saved[2] = saved[2].reshape(inputs.shape)
    output, input_grad, total = backward(
        pieces, copies, False, lengths, saved, weights, norms + adapters
    )
    return update(
        total,
        output,
        input_grad,
        adapters,
        row_down_model,
        col_down_model,
        row_down_hidden,
        col_down_hidden,
        row_up_qkv,
        col_up_qkv,
        row_up_hidden,
        col_up_hidden,
        row_up_model,
        col_up_model,
    )


def local(pieces, copies, inputs, *others):
    if inputs.shape[0] == pieces and TILE % inputs.shape[1] == 0:
        return local_by_rows(pieces, copies, inputs, *others)
    return local_by_heads(inputs, *others)


def solution(mesh):
    placed = (
        P("dp", "seq", None),
        P("dp", "seq", None),
        P("dp"),
        P(),
        P(),
        P(),
        P(),
        P(),
        P(),
        P(),
        P(),
        P(),
        P(),
        P(),
        P(),
        P(),
        P(),
        P(),
        P(),
        P(),
        P(),
        P(),
        P(),
        P(),
        P(),
    )
    return jax.shard_map(
        partial(local, mesh.shape["seq"], mesh.shape["dp"]),
        mesh=mesh,
        in_specs=placed,
        out_specs=(
            P("dp", "seq", None),
            P("dp", "seq", None),
            P(),
            P(),
            P(),
            P(),
            P(),
            P(),
            P(),
            P(),
            P(),
            P(),
            P(),
            P(),
            P(),
            P(),
            P(),
            P(),
            P(),
            P(),
            P(),
            P(),
        ),
        check_vma=False,
    )
```

```python
from functools import partial

import jax
import jax.numpy as jnp
from jax import lax
from jax.experimental import pallas as pl
from jax.experimental.pallas import tpu as pltpu
from jax.sharding import PartitionSpec as P


HEADS = 16
HEAD_DIM = 64
STEP = 10


NORM_EPS = 1e-05
ADAPTER_SCALE = 8.0
STAT_EPS = 1e-30
CLIP_LEVEL = 1.0
RATE = 0.3
DECAY_WEIGHT = 0.01
MASKED = -1e30


def as_sent(array):

    def short(part):
        return part.astype(jnp.bfloat16) if part.dtype == jnp.float32 else part

    return jax.tree.map(short, array)


def normalize(values, gain, shift):
    centered = values - jnp.mean(values, axis=-1, keepdims=True)
    spread = jnp.mean(centered * centered, axis=-1, keepdims=True)
    scaled = lax.rsqrt(spread + NORM_EPS)
    unit = centered * scaled
    return (unit * gain + shift, unit, scaled)


def normalize_back(grad, unit, scaled, gain):
    gained = grad * gain
    return scaled * (
        gained
        - jnp.mean(gained, axis=-1, keepdims=True)
        - unit * jnp.mean(gained * unit, axis=-1, keepdims=True)
    )


def matrix_multiply(left, right):
    return jnp.dot(left, right, preferred_element_type=jnp.float32)


def inner_product(left, right):
    return jnp.einsum("tr,tc->rc", left, right, preferred_element_type=jnp.float32)


def compared_with(left, right):
    return jnp.einsum("tc,rc->tr", left, right, preferred_element_type=jnp.float32)


def adapted(source_rows, weight_matrix, bias_vector, down, upward_matrix):
    narrowed_rows = matrix_multiply(source_rows, down).astype(jnp.bfloat16)
    return (
        matrix_multiply(source_rows, weight_matrix)
        + bias_vector
        + ADAPTER_SCALE * matrix_multiply(narrowed_rows, upward_matrix),
        narrowed_rows,
    )


def adapted_back(gradient_lowrank, source_rows, weight_matrix, down, upward_matrix, narrowed_rows):
    gradient_upward = ADAPTER_SCALE * inner_product(narrowed_rows, gradient_lowrank)
    gradient_narrowed = (ADAPTER_SCALE * compared_with(gradient_lowrank, upward_matrix)).astype(
        jnp.bfloat16
    )
    grad_down = inner_product(source_rows, gradient_narrowed)
    grad_source = compared_with(gradient_lowrank, weight_matrix) + compared_with(
        gradient_narrowed, down
    )
    return (grad_source, grad_down, gradient_upward)


def score_block(operand):
    query, keys = operand
    return jnp.einsum("gqe,gke->gqk", query, keys, preferred_element_type=jnp.float32)


def mix_block(operand):
    weights, values = operand
    return jnp.einsum("gqk,gke->gqe", weights, values, preferred_element_type=jnp.float32)


def spread_block(operand):
    weights, queries = operand
    return jnp.einsum("gqk,gqe->gke", weights, queries, preferred_element_type=jnp.float32)


def masked_scores(query, keys, spots, length):
    total = keys.shape[1]
    size = min(512, total)
    reach = jnp.minimum(length, jnp.max(spots) + 1)
    places = jnp.arange(total)
    valid = (places[None, :] <= spots[:, None]) & (places[None, :] < length)
    pieces = []
    for begin in range(0, total, size):
        pieces.append(score_block((query, keys[:, begin : begin + size])))
    scores = jnp.concatenate(pieces, axis=-1) * query.shape[-1] ** (-0.5)
    return (jnp.where(valid[None], scores, MASKED), reach, size)


def attend(query, keys, values, spots, length):
    scores, reach, size = masked_scores(query, keys, spots, length)
    top = jnp.max(scores, axis=-1, keepdims=True)
    weights = jnp.exp(scores - top)
    summed = jnp.sum(weights, axis=-1, keepdims=True)
    probs = (weights / summed).astype(jnp.bfloat16)
    result = jnp.zeros(query.shape, jnp.float32)
    for begin in range(0, keys.shape[1], size):
        operand = (probs[:, :, begin : begin + size], values[:, begin : begin + size])
        result = result + mix_block(operand)
    return (result, (top + jnp.log(summed))[..., 0])


def attend_back(query, keys, values, spots, length, grad_rows, lse):
    scores, reach, size = masked_scores(query, keys, spots, length)
    probs = jnp.exp(scores - lse[..., None])
    pieces = []
    for begin in range(0, keys.shape[1], size):
        pieces.append(score_block((grad_rows, values[:, begin : begin + size])))
    dprob = jnp.concatenate(pieces, axis=-1)
    delta = jnp.sum(probs * dprob, axis=-1, keepdims=True)
    dscore = (probs * (dprob - delta)).astype(jnp.bfloat16)
    probs_low = probs.astype(jnp.bfloat16)
    scale = query.shape[-1] ** (-0.5)
    grad_query = jnp.zeros(query.shape, jnp.float32)
    key_parts = []
    value_parts = []
    for begin in range(0, keys.shape[1], size):
        grad_query = grad_query + mix_block(
            (dscore[:, :, begin : begin + size], keys[:, begin : begin + size])
        )
        key_parts.append(spread_block((dscore[:, :, begin : begin + size], query)))
        value_parts.append(spread_block((probs_low[:, :, begin : begin + size], grad_rows)))
    return (
        grad_query * scale,
        jnp.concatenate(key_parts, axis=1) * scale,
        jnp.concatenate(value_parts, axis=1),
    )


def heads_split(triple):
    return tuple((jnp.transpose(triple[:, index], (1, 0, 2)) for index in range(3)))


def head_forward(skip, item):
    triple, length = item
    spots = jnp.arange(triple.shape[0])
    query, keys, values = heads_split(triple)
    result, lse = attend(query, keys, values, spots, length)
    return (jnp.transpose(result, (1, 0, 2)).astype(jnp.bfloat16), lse)


def head_backward(skip, item):
    triple, grad_rows, lse, length = item
    spots = jnp.arange(triple.shape[0])
    query, keys, values = heads_split(triple)
    grads = attend_back(
        query, keys, values, spots, length, jnp.transpose(grad_rows, (1, 0, 2)), lse
    )
    return jnp.stack(grads, axis=0).transpose(2, 0, 1, 3).astype(jnp.bfloat16)


def factored(grad, weight_matrix, row, col):
    decay = 1.0 - STEP ** (-0.8)
    squares = grad * grad + STAT_EPS
    new_row = decay * row + (1.0 - decay) * jnp.mean(squares, axis=-1)
    new_col = decay * col + (1.0 - decay) * jnp.mean(squares, axis=-2)
    second = (
        new_row[..., :, None] * new_col[..., None, :] / jnp.mean(new_row, axis=-1)[..., None, None]
    )
    unit = grad * lax.rsqrt(second)
    level = jnp.sqrt(jnp.mean(unit * unit, axis=(-2, -1), keepdims=True))
    unit = unit / jnp.maximum(1.0, level / CLIP_LEVEL)
    rate = RATE * jnp.sqrt(jnp.mean(weight_matrix * weight_matrix, axis=(-2, -1), keepdims=True))
    return (weight_matrix - rate * (unit + DECAY_WEIGHT * weight_matrix), new_row, new_col)


LOG2E = 1.4426950408889634
NT = (((1,), (1,)), ((), ()))
TN = (((0,), (0,)), ((), ()))


def dotf(a, b, dims=(((1,), (0,)), ((), ()))):
    return lax.dot_general(a, b, dims, preferred_element_type=jnp.float32)


def triple(value):
    high = value.astype(jnp.bfloat16)
    rest = value - high.astype(jnp.float32)
    mid = rest.astype(jnp.bfloat16)
    low = (rest - mid.astype(jnp.float32)).astype(jnp.bfloat16)
    return high, mid, low


GELU_A = 0.7978845608028654
GELU_B = 0.7978845608028654 * 0.044715
RANK = 4


def norm_parts(values):
    centered = values - jnp.mean(values, axis=-1, keepdims=True)
    spread = jnp.mean(centered * centered, axis=-1, keepdims=True)
    scaled = lax.rsqrt(spread + NORM_EPS)
    return centered * scaled, scaled


def norm_back(grad, unit, scaled, gain):
    gained = grad * gain
    return scaled * (
        gained
        - jnp.mean(gained, axis=-1, keepdims=True)
        - unit * jnp.mean(gained * unit, axis=-1, keepdims=True)
    )


def low(value):
    return value.astype(jnp.bfloat16)


def wide(value):
    return value.astype(jnp.float32)


def gelu_pair(value):
    square = value * value
    half = 0.5 * value
    bent = jnp.tanh(value * (GELU_A + GELU_B * square))
    slope = (0.5 + 0.5 * bent) + half * (1.0 - bent * bent) * (GELU_A + 3.0 * GELU_B * square)
    return half + half * bent, slope


def peers_of(axis, size):
    me = lax.axis_index(axis)
    return me, [lax.rem(me + shift, size) for shift in range(1, size)]


def greet(axes):
    barrier = pltpu.get_barrier_semaphore()
    count = 0
    for axis, size in axes:
        _, peers = peers_of(axis, size)
        for peer in peers:
            pl.semaphore_signal(
                barrier, inc=1, device_id={axis: peer}, device_id_type=pl.DeviceIdType.MESH
            )
        count += len(peers)
    pl.semaphore_wait(barrier, count)


def send(source, target, sent, landed, axis, peer):
    return pltpu.make_async_remote_copy(
        src_ref=source,
        dst_ref=target,
        send_sem=sent,
        recv_sem=landed,
        device_id={axis: peer},
        device_id_type=pl.DeviceIdType.MESH,
    )


def sum_everywhere(
    splits, copies, part_ref, total_ref, seq_in, dp_in, own, s_sent, s_land, d_sent, d_land, g_sent, g_land
):
    size = part_ref.shape[1] // splits
    me, peers = peers_of("seq", splits)
    mine, others = peers_of("dp", copies)

    def columns(index):
        return pl.ds(pl.multiple_of(index * size, size), size)

    first = []
    for shift, peer in enumerate(peers):
        copy = send(part_ref.at[:, columns(peer)], seq_in.at[me], s_sent.at[shift], s_land.at[me], "seq", peer)
        copy.start()
        first.append(copy)
    seq_in[me] = part_ref[:, columns(me)]
    for peer in peers:
        send(part_ref.at[:, columns(me)], seq_in.at[peer], s_sent.at[0], s_land.at[peer], "seq", peer).wait_recv()
    summed = seq_in[0]
    for index in range(1, splits):
        summed = summed + seq_in[index]
    own[...] = summed
    second = []
    for shift, peer in enumerate(others):
        copy = send(own, dp_in.at[mine], d_sent.at[shift], d_land.at[mine], "dp", peer)
        copy.start()
        second.append(copy)
    dp_in[mine] = summed
    for peer in others:
        send(own, dp_in.at[peer], d_sent.at[0], d_land.at[peer], "dp", peer).wait_recv()
    summed = dp_in[0]
    for index in range(1, copies):
        summed = summed + dp_in[index]
    total_ref[:, columns(me)] = summed
    third = []
    for shift, peer in enumerate(peers):
        copy = send(
            total_ref.at[:, columns(me)], total_ref.at[:, columns(me)], g_sent.at[shift], g_land.at[me], "seq", peer
        )
        copy.start()
        third.append(copy)
    for peer in peers:
        part = total_ref.at[:, columns(peer)]
        send(part, part, g_sent.at[0], g_land.at[peer], "seq", peer).wait_recv()
    for copy in first + second + third:
        copy.wait_send()


def sum_scratch(splits, copies, width):
    size = width // splits
    dma = pltpu.SemaphoreType.DMA
    return [
        pltpu.VMEM((splits, 8, size), jnp.float32),
        pltpu.VMEM((copies, 8, size), jnp.float32),
        pltpu.VMEM((8, size), jnp.float32),
        dma((splits,)),
        dma((splits,)),
        dma((copies,)),
        dma((copies,)),
        dma((splits,)),
        dma((splits,)),
    ]


def across(column):
    count = column.shape[0]
    diagonal = lax.broadcasted_iota(jnp.int32, (count, count), 0) == lax.broadcasted_iota(
        jnp.int32, (count, count), 1
    )
    return jnp.sum(jnp.where(diagonal, jnp.broadcast_to(column, (count, count)), 0.0), axis=0, keepdims=True)


def upright(line):
    count = line.shape[1]
    diagonal = lax.broadcasted_iota(jnp.int32, (count, count), 0) == lax.broadcasted_iota(
        jnp.int32, (count, count), 1
    )
    return jnp.sum(jnp.where(diagonal, jnp.broadcast_to(line, (count, count)), 0.0), axis=1, keepdims=True)


def factored_step(grad, weight, short_line, long_line, rows_long):
    decay = 1.0 - STEP ** (-0.8)
    squares = grad * grad + STAT_EPS
    new_short = decay * upright(short_line) + (1.0 - decay) * jnp.mean(squares, axis=1, keepdims=True)
    new_long = decay * long_line + (1.0 - decay) * jnp.mean(squares, axis=0, keepdims=True)
    if rows_long:
        middle = jnp.mean(new_long, axis=1, keepdims=True)
    else:
        middle = jnp.mean(new_short, axis=0, keepdims=True)
    unit = grad * lax.rsqrt(new_short * new_long / middle)
    entries = grad.shape[0] * grad.shape[1]

    def mean_square(value):
        return jnp.sum(jnp.sum(value * value, axis=1, keepdims=True), axis=0, keepdims=True) / entries

    level = jnp.sqrt(mean_square(unit))
    unit = unit / jnp.maximum(1.0, level / CLIP_LEVEL)
    rate = RATE * jnp.sqrt(mean_square(weight))
    return weight - rate * (unit + DECAY_WEIGHT * weight), across(new_short), new_long


def update_kernel(
    total_ref, output_in, grad_in, dm, dh, uq, uh, um, row_dm, col_dm, row_dh, col_dh, row_uq, col_uq, row_uh, col_uh, row_um, col_um,
    output_out, grad_out, g_dm, g_dh, g_uq, g_uh, g_um, n_dm, n_dh, n_uq, n_uh, n_um,
    r_dm, r_dh, r_uq, r_uh, r_um, c_dm, c_dh, c_uq, c_uh, c_um, held_out, held_grad, sems,
):
    moves = [
        pltpu.make_async_copy(output_in, held_out, sems.at[0]),
        pltpu.make_async_copy(grad_in, held_grad, sems.at[1]),
    ]
    for move in moves:
        move.start()
    moves = [
        (moves[0], pltpu.make_async_copy(held_out, output_out, sems.at[0])),
        (moves[1], pltpu.make_async_copy(held_grad, grad_out, sems.at[1])),
    ]
    for move, onward in moves:
        move.wait()
        onward.start()
    width = dm.shape[2]
    hidden = dh.shape[1]
    for index in range(3):
        grad = total_ref[0:RANK, index * width : (index + 1) * width]
        g_dm[index] = grad
        n_dm[index], c_dm[index : index + 1, :], r_dm[index : index + 1, :] = factored_step(
            grad, dm[index], col_dm[index : index + 1, :], row_dm[index : index + 1, :], True
        )
    grad = total_ref[0:RANK, 3 * width : 6 * width]
    g_uq[...] = grad
    n_uq[...], r_uq[...], c_uq[...] = factored_step(grad, uq[...], row_uq[...], col_uq[...], False)
    for index in range(2):
        grad = total_ref[0:RANK, (6 + index) * width : (7 + index) * width]
        g_um[index] = grad
        n_um[index], r_um[index : index + 1, :], c_um[index : index + 1, :] = factored_step(
            grad, um[index], row_um[index : index + 1, :], col_um[index : index + 1, :], False
        )
    grad = total_ref[RANK : 2 * RANK, 0:hidden]
    g_dh[...] = grad
    n_dh[...], c_dh[...], r_dh[...] = factored_step(grad, dh[...], col_dh[...], row_dh[...], True)
    grad = total_ref[RANK : 2 * RANK, hidden : 2 * hidden]
    g_uh[...] = grad
    n_uh[...], r_uh[...], c_uh[...] = factored_step(grad, uh[...], row_uh[...], col_uh[...], False)
    for _, onward in moves:
        onward.wait()


def update(total, output, input_grad, adapters, row_dm, col_dm, row_dh, col_dh, row_uq, col_uq, row_uh, col_uh, row_um, col_um):
    flip = lambda array: jnp.swapaxes(array, -1, -2)
    line = lambda array: array.reshape(1, -1)
    given = [
        row_dm, col_dm, line(row_dh), line(col_dh), line(row_uq), line(col_uq), line(row_uh), line(col_uh), row_um, col_um,
    ]
    stats = given[0::2] + given[1::2]
    anyspace = pl.BlockSpec(memory_space=pl.ANY)
    vmem = pl.BlockSpec(memory_space=pltpu.VMEM)
    results = pl.pallas_call(
        update_kernel,
        out_shape=[jax.ShapeDtypeStruct(a.shape, a.dtype) for a in [output, input_grad] + adapters + adapters + stats],
        in_specs=[vmem, anyspace, anyspace] + [vmem] * 15,
        out_specs=[anyspace, anyspace] + [vmem] * 20,
        scratch_shapes=[
            pltpu.VMEM(output.shape, output.dtype),
            pltpu.VMEM(output.shape, output.dtype),
            pltpu.SemaphoreType.DMA((2,)),
        ],
        compiler_params=pltpu.CompilerParams(vmem_limit_bytes=60 * 2**20),
        name="factored_update",
    )(total, output, input_grad, *adapters, *given)
    results = list(results)
    for index in (2, 3, 7, 8):
        results[index] = flip(results[index])
    olds = (row_dm, row_dh, row_uq, row_uh, row_um, col_dm, col_dh, col_uq, col_uh, col_um)
    for index, old in zip(range(12, 22), olds):
        results[index] = results[index].reshape(old.shape)
    return tuple(results)


def fill_adapters(dm_ref, dh_ref, uq_ref, uh_ref, um_ref, aq, ap, a1, a2, bq, bp, b2, b1):
    for index, ref in enumerate((aq, ap, a1)):
        ref[...] = low(dm_ref[index])
    a2[...] = low(dh_ref[...])
    for ref, value in ((bq, uq_ref[...]), (bp, um_ref[0]), (b2, um_ref[1]), (b1, uh_ref[...])):
        ref[...] = low(ADAPTER_SCALE * wide(low(value)))


def adapter_scratch(width, hidden):
    sizes = [width, width, width, hidden, 3 * width, width, width, hidden]
    return [pltpu.VMEM((RANK, size), jnp.bfloat16) for size in sizes]


TILE = 256
GROUP = 4
LANES = 128


def peer_order(me, splits):
    half = splits // 2
    side, place = me // half, lax.rem(me, half)
    far = [(1 - side) * half + lax.rem(place + shift, half) for shift in range(half)]
    near = [side * half + lax.rem(place + shift, half) for shift in range(1, half)]
    return far, near


def block_kernel(
    splits, copies, solo,
    lengths_ref, inputs, cotangent, wqkv_hbm, wo_hbm, w1_hbm, w2_hbm,
    bias_ref, gain_ref, shift_ref, dm_ref, dh_ref, uq_ref, uh_ref, um_ref,
    output, dx_out, total_ref, cot_in, out_row, att_hbm, mid_hbm, act_hbm, slope_hbm,
    wqkv, wo, w1, w2, kx, vx, qx, dk, dv, xr, att, mid, act, slope, cot_t, outs, gx, dq, narrow, part,
    aq, ap, a1, a2, bq, bp, b2, b1,
    w_sem, s_sem, l_sem, own_sem, x_sent, x_land, c_sent, c_land, f_sent, f_land, b_sent, b_land,
    *sum_refs,
):
    me = 0 if solo else lax.axis_index("seq")
    span, width = xr.shape[1], xr.shape[2]
    hidden = w1.shape[1]
    total = splits * span
    tiles = total // TILE
    blocks = TILE // span
    heads = kx.shape[0]
    pairs = heads // 2
    half = LANES // 2
    length = lengths_ref[me]
    upper = me >= splits // 2

    loads = [
        pltpu.make_async_copy(source, target, w_sem.at[index])
        for index, (source, target) in enumerate(((wqkv_hbm, wqkv), (wo_hbm, wo), (w1_hbm, w1), (w2_hbm, w2)))
    ]
    own_x = pltpu.make_async_copy(inputs if solo else inputs.at[me], xr if solo else xr.at[me], own_sem.at[0])
    own_b = pltpu.make_async_copy(xr.at[me], dx_out.at[me], own_sem.at[1])

    def saves(tile):
        rows = pl.ds(tile * TILE, TILE)
        moves = (
            (att, att_hbm.at[:, rows, :]),
            (mid, mid_hbm.at[rows, :]),
            (act, act_hbm.at[rows, :]),
            (slope, slope_hbm.at[rows, :]),
            (outs, out_row.at[pl.ds(tile * blocks, blocks)]),
        )
        return [pltpu.make_async_copy(a, b, s_sem.at[i]) for i, (a, b) in enumerate(moves)]

    def fetches(tile):
        rows = pl.ds(tile * TILE, TILE)
        moves = (
            (slope_hbm.at[rows, :], slope),
            (act_hbm.at[rows, :], act),
            (att_hbm.at[:, rows, :], att),
            (mid_hbm.at[rows, :], mid),
        )
        return [pltpu.make_async_copy(a, b, l_sem.at[i]) for i, (a, b) in enumerate(moves)]

    def x_copy(peer, slot):
        return send(inputs.at[peer], xr.at[me], x_sent.at[slot], x_land.at[me], "seq", peer)

    def c_copy(peer, slot):
        return send(cotangent.at[peer], cot_in.at[me], c_sent.at[slot], c_land.at[me], "seq", peer)

    def f_copy(block):
        return send(out_row.at[block], output.at[me], f_sent.at[block], f_land.at[me], "seq", block)

    def b_copy(block):
        return send(xr.at[block], dx_out.at[me], b_sent.at[block], b_land.at[me], "seq", block)

    def tile_blocks(tile):
        return range(tile * blocks, (tile + 1) * blocks)

    def cot_move(block, fetched):
        slot = cot_t.at[block % blocks]
        source = cotangent.at[me] if fetched else cot_in.at[block]
        return pltpu.make_async_copy(source, slot, l_sem.at[4 + block % blocks])

    def cot_fetch(tile):
        if solo:
            for block in tile_blocks(tile):
                cot_move(block, False).start()
            return
        for block in tile_blocks(tile):

            @pl.when(me == block)
            def _():
                cot_move(block, True).start()

            @pl.when(me != block)
            def _():
                send(cotangent.at[block], cot_in.at[block], c_sent.at[0], c_land.at[block], "seq", block).wait_recv()
                cot_move(block, False).start()

    def x_wait(tile):
        if solo:
            return
        for block in tile_blocks(tile):

            @pl.when(me != block)
            def _():
                send(inputs.at[block], xr.at[block], x_sent.at[0], x_land.at[block], "seq", block).wait_recv()

    def send_output(tile):
        if solo:
            return
        for block in tile_blocks(tile):

            @pl.when(me != block)
            def _():
                f_copy(block).start()

    if not solo:
        greet((("seq", splits), ("dp", copies)))
    own_x.start()
    loads[0].start()
    if not solo:
        far, near = peer_order(me, splits)
        quarter = lax.rem(me, splits // 2) // 2
        outward = jnp.logical_or(
            jnp.logical_and(me < splits // 2, quarter == 0), jnp.logical_and(upper, quarter == 0)
        )

        @pl.when(outward)
        def _():
            for slot, peer in enumerate(far + near):
                x_copy(peer, slot).start()

        @pl.when(jnp.logical_not(outward))
        def _():
            for slot, peer in enumerate(near + far):
                x_copy(peer, slot).start()

    for load in loads[1:]:
        load.start()
    fill_adapters(dm_ref, dh_ref, uq_ref, uh_ref, um_ref, aq, ap, a1, a2, bq, bp, b2, b1)
    part[...] = jnp.zeros_like(part)

    lane = lax.broadcasted_iota(jnp.int32, (TILE, LANES), 1)
    row = lax.broadcasted_iota(jnp.int32, (TILE, TILE), 0)
    col = lax.broadcasted_iota(jnp.int32, (TILE, TILE), 1)
    zero = jnp.zeros((TILE, LANES), jnp.bfloat16)
    one = jnp.ones((TILE, LANES), jnp.bfloat16)
    scale = half ** (-0.5)
    owns = (lane < half, lane >= half)
    spares = (half, 0)

    def with_extra(own, spare, value, extra):
        high, middle, rest = triple(extra)
        return jnp.where(
            own,
            value,
            jnp.where(lane == spare, high, jnp.where(lane == spare + 1, middle, jnp.where(lane == spare + 2, rest, zero))),
        )

    def bias(start, size):
        return wide(bias_ref[0:1, start : start + size])

    def rows_of(tile):
        if isinstance(tile, int):
            return pl.ds(tile * TILE, TILE)
        return pl.ds(pl.multiple_of(tile * TILE, TILE), TILE)

    def project(tile):
        rows = rows_of(tile)
        x = wide(xr[pl.ds(tile * blocks, blocks)].reshape(TILE, width))
        unit, _ = norm_parts(x)
        normed = low(unit * wide(gain_ref[0:1, :]) + wide(shift_ref[0:1, :]))
        narrow_q = low(dotf(normed, aq[...], NT))
        narrow[rows, 0:RANK] = narrow_q
        spot = tile * TILE + lax.broadcasted_iota(jnp.int32, (TILE, LANES), 0)
        limit = jnp.where(spot < length, 0.0, MASKED).astype(jnp.bfloat16)
        size = 512
        for index in range(3):
            for start in range(0, width, size):
                column = index * width + start
                value = dotf(normed, wqkv[:, column : column + size]) + dotf(narrow_q, bq[:, column : column + size])
                if index == 0:
                    value = value + bias(start, size)
                if index == 2:
                    value = value + bias(width + start, size)
                value = low(value)
                for pair in range(size // LANES):
                    piece = value[:, pair * LANES : (pair + 1) * LANES]
                    for parity in range(2):
                        head = 2 * (start // LANES + pair) + parity
                        own, spare = owns[parity], spares[parity]
                        if index == 0:
                            extra = jnp.where(lane == spare + 3, one, zero)
                            qx[head, rows, :] = jnp.where(own, piece * jnp.asarray(scale, jnp.bfloat16), extra)
                        elif index == 1:
                            extra = jnp.where(lane == spare + 3, limit, jnp.where(lane < spare + 3, one, zero))
                            kx[head, rows, :] = jnp.where(own, piece, extra)
                        else:
                            vx[head, rows, :] = jnp.where(own, piece, one)

    if not solo:

        @pl.when(upper)
        def _():
            for tile in range(tiles // 2, tiles):
                x_wait(tile)

    own_x.wait()
    loads[0].wait()
    if not solo:

        @pl.when(upper)
        def _():
            lax.fori_loop(tiles // 2, tiles, lambda tile, carry: (project(tile), carry)[1], 0)

    for tile in range(tiles):
        begin, end = tile * TILE, (tile + 1) * TILE
        if tile < tiles // 2:
            x_wait(tile)
            project(tile)
        elif solo:
            project(tile)
        else:

            @pl.when(jnp.logical_not(upper))
            def _():
                x_wait(tile)
                project(tile)

        if not solo:
            ready = upper if tile == tiles // 2 - 1 else jnp.logical_not(upper)
            if tile == tiles // 2 - 1 or tile == tiles // 2:

                @pl.when(ready)
                def _():
                    for slot, peer in enumerate(far + near):
                        c_copy(peer, slot).start()

        if tile:
            saves(tile - 1)[0].wait()
        valid = begin + lax.broadcasted_iota(jnp.int32, (TILE, LANES), 0) < length
        causal = col <= row

        def attend(index, carry):
            def scores(unit):
                head = index * GROUP + unit
                return dotf(qx[head, begin:end, :], kx[head, 0:end, :], NT)

            def mix(unit, value):
                head = index * GROUP + unit
                last = jnp.where(causal, value[:, begin:], MASKED)
                value = jnp.concatenate([value[:, :begin], last], axis=1) if begin else last
                top = jnp.max(value, axis=-1, keepdims=True)
                weights = low(jnp.exp2((value - top) * LOG2E))
                mixed = dotf(weights, vx[head, 0:end, :])
                spare, own = spares[unit % 2], owns[unit % 2]
                summed = mixed[:, spare : spare + 1]
                back = jnp.where(valid, -(top + jnp.log(summed)), MASKED)
                qx[head, begin:end, :] = with_extra(own, spare, qx[head, begin:end, :], back)
                return mixed * (1.0 / summed)

            ahead = scores(0)
            results = []
            for unit in range(GROUP):
                value = ahead
                if unit + 1 < GROUP:
                    ahead = scores(unit + 1)
                results.append(mix(unit, value))
            for unit in range(0, GROUP, 2):
                att[index * (GROUP // 2) + unit // 2] = low(jnp.where(owns[0], results[unit], results[unit + 1]))
            return carry

        lax.fori_loop(0, heads // GROUP, attend, 0)
        if tile == 0:
            for load in loads[1:]:
                load.wait()
        else:
            for save in saves(tile - 1)[1:]:
                save.wait()
            send_output(tile - 1)
        attended = jnp.concatenate([att[index] for index in range(pairs)], axis=1)
        narrow_p = low(dotf(attended, ap[...], NT))
        middle = (
            wide(xr[tile * blocks : (tile + 1) * blocks].reshape(TILE, width))
            + dotf(attended, wo[...])
            + bias(2 * width, width)
            + dotf(narrow_p, bp[...])
        )
        mid[...] = middle
        unit, _ = norm_parts(middle)
        normed = low(unit * wide(gain_ref[1:2, :]) + wide(shift_ref[1:2, :]))
        narrow_1 = low(dotf(normed, a1[...], NT))
        size = 256

        def expand(start):
            return (
                dotf(normed, w1[:, start : start + size])
                + bias(3 * width + start, size)
                + dotf(narrow_1, b1[:, start : start + size])
            )

        result = middle + bias(3 * width + hidden, width)
        narrow_2 = jnp.zeros((TILE, RANK), jnp.float32)
        ahead = expand(0)
        for start in range(0, hidden, size):
            stop = start + size
            before = ahead
            if stop < hidden:
                ahead = expand(stop)
            active, bend = gelu_pair(before)
            active = low(active)
            act[:, start:stop] = active
            slope[:, start:stop] = low(bend)
            result = result + dotf(active, w2[start:stop, :])
            narrow_2 = narrow_2 + dotf(active, a2[:, start:stop], NT)
        narrow_2 = low(narrow_2)
        outs[...] = low(result + dotf(narrow_2, b2[...])).reshape(blocks, span, width)
        narrow[begin:end, RANK : 2 * RANK] = narrow_p
        narrow[begin:end, 2 * RANK : 3 * RANK] = narrow_1
        narrow[begin:end, 3 * RANK : 4 * RANK] = narrow_2
        if tile < tiles - 1:
            for save in saves(tile):
                save.start()
        else:
            saves(tile)[4].start()

    def add_upper(start, value):
        part[0:RANK, start : start + value.shape[1]] += value

    def add_lower(start, value):
        part[RANK : 2 * RANK, start : start + value.shape[1]] += value

    cot_fetch(tiles - 1)
    for tile in reversed(range(tiles)):
        begin, end = tile * TILE, (tile + 1) * TILE
        newest = tile == tiles - 1
        if newest:
            saves(tile)[4].wait()
            send_output(tile)
        else:
            for fetch in fetches(tile)[0:3]:
                fetch.wait()
        for block in tile_blocks(tile):
            cot_move(block, False).wait()
        spot = begin + lax.broadcasted_iota(jnp.int32, (TILE, width), 0)
        given = cot_t[...].reshape(TILE, width)
        gout = jnp.where(spot < length, given, jnp.zeros_like(given))
        narrow_q = narrow[begin:end, 0:RANK]
        narrow_p = narrow[begin:end, RANK : 2 * RANK]
        narrow_1 = narrow[begin:end, 2 * RANK : 3 * RANK]
        narrow_2 = narrow[begin:end, 3 * RANK : 4 * RANK]
        gn2 = low(dotf(gout, b2[...], NT))
        add_upper(7 * width, dotf(narrow_2, gout, TN))
        size = 512

        def contract(start):
            return dotf(gout, w2[start : start + size, :], NT) + dotf(gn2, a2[:, start : start + size])

        gnorm = jnp.zeros((TILE, width), jnp.float32)
        gn1 = jnp.zeros((TILE, RANK), jnp.float32)
        ahead = contract(0)
        for start in range(0, hidden, size):
            stop = start + size
            gact = ahead
            if stop < hidden:
                ahead = contract(stop)
            gbefore = low(gact * wide(slope[:, start:stop]))
            add_lower(start, dotf(gn2, act[:, start:stop], TN))
            add_lower(hidden + start, dotf(narrow_1, gbefore, TN))
            gn1 = gn1 + dotf(gbefore, b1[:, start:stop], NT)
            gnorm = gnorm + dotf(gbefore, w1[:, start:stop], NT)
        gn1 = low(gn1)
        gnorm = gnorm + dotf(gn1, a1[...])
        if not newest:
            fetches(tile)[3].wait()
        unit, scaled = norm_parts(mid[...])
        normed = low(unit * wide(gain_ref[1:2, :]) + wide(shift_ref[1:2, :]))
        add_upper(2 * width, dotf(gn1, normed, TN))
        grad = wide(gout) + norm_back(gnorm, unit, scaled, wide(gain_ref[1:2, :]))
        mid[...] = grad
        glow = low(grad)
        gnp = low(dotf(glow, bp[...], NT))
        add_upper(6 * width, dotf(narrow_p, glow, TN))
        gatt = low(dotf(glow, wo[...], NT) + dotf(gnp, ap[...]))
        attended = jnp.concatenate([att[index] for index in range(pairs)], axis=1)
        add_upper(width, dotf(gnp, attended, TN))
        for index in range(pairs):
            piece = gatt[:, index * LANES : (index + 1) * LANES]
            product = wide(piece) * wide(att[index])
            for parity in range(2):
                own, spare = owns[parity], spares[parity]
                delta = -jnp.sum(jnp.where(own, product, 0.0), axis=-1, keepdims=True)
                gx[2 * index + parity] = with_extra(own, spare, piece, jnp.broadcast_to(delta, (TILE, LANES)))
        if tile:
            for fetch in fetches(tile - 1)[0:3]:
                fetch.start()
            cot_fetch(tile - 1)
        causal = row <= col

        def attend_back(index, carry):
            def products(unit):
                head = index * GROUP + unit
                return (
                    dotf(kx[head, 0:end, :], qx[head, begin:end, :], NT),
                    dotf(vx[head, 0:end, :], gx[head], NT),
                )

            def spread(unit, scores, dprob):
                head = index * GROUP + unit
                weights = jnp.exp2(scores * LOG2E)
                last = jnp.where(causal, weights[begin:], 0.0)
                weights = jnp.concatenate([weights[:begin], last], axis=0) if begin else last
                dscore = low(weights * dprob)
                return (
                    dotf(dscore, kx[head, 0:end, :], TN),
                    dotf(dscore, qx[head, begin:end, :]),
                    dotf(low(weights), gx[head]),
                )

            ahead = products(0)
            results = []
            for unit in range(GROUP):
                given = ahead
                if unit + 1 < GROUP:
                    ahead = products(unit + 1)
                results.append(spread(unit, *given))
            first_lanes = lax.broadcasted_iota(jnp.int32, (end, LANES), 1) < half
            for unit in range(0, GROUP, 2):
                pair = index * (GROUP // 2) + unit // 2
                even, odd = results[unit], results[unit + 1]
                dq[pair] = low(jnp.where(owns[0], even[0], odd[0]) * scale)
                more_k = jnp.where(first_lanes, even[1], odd[1])
                more_v = jnp.where(first_lanes, even[2], odd[2])
                if newest:
                    dk[pair] = more_k
                    dv[pair] = more_v
                else:
                    dk[pair, 0:end, :] += more_k
                    dv[pair, 0:end, :] += more_v
            return carry

        lax.fori_loop(0, heads // GROUP, attend_back, 0)
        values = [
            jnp.concatenate([dq[index] for index in range(pairs)], axis=1),
            jnp.concatenate([low(dk[index, begin:end, :]) for index in range(pairs)], axis=1),
            jnp.concatenate([low(dv[index, begin:end, :]) for index in range(pairs)], axis=1),
        ]
        gnq = jnp.zeros((TILE, RANK), jnp.float32)
        gnormed = jnp.zeros((TILE, width), jnp.float32)
        for index, value in enumerate(values):
            start, stop = index * width, (index + 1) * width
            gnq = gnq + dotf(value, bq[:, start:stop], NT)
            add_upper(3 * width + start, dotf(narrow_q, value, TN))
            gnormed = gnormed + dotf(value, wqkv[:, start:stop], NT)
        gnq = low(gnq)
        gnormed = gnormed + dotf(gnq, aq[...])
        unit, scaled = norm_parts(wide(xr[tile * blocks : (tile + 1) * blocks].reshape(TILE, width)))
        normed = low(unit * wide(gain_ref[0:1, :]) + wide(shift_ref[0:1, :]))
        add_upper(0, dotf(gnq, normed, TN))
        dx = low(mid[...] + norm_back(gnormed, unit, scaled, wide(gain_ref[0:1, :])))
        if tile:
            fetches(tile - 1)[3].start()
        xr[tile * blocks : (tile + 1) * blocks] = dx.reshape(blocks, span, width)
        if not solo:
            for block in tile_blocks(tile):

                @pl.when(me != block)
                def _():
                    b_copy(block).start()

                @pl.when(me == block)
                def _():
                    own_b.start()

    part[0:RANK, 3 * width :] = ADAPTER_SCALE * part[0:RANK, 3 * width :]
    part[RANK : 2 * RANK, hidden:] = ADAPTER_SCALE * part[RANK : 2 * RANK, hidden:]
    if solo:
        total_ref[...] = part[...]
        return
    own_f = pltpu.make_async_copy(out_row.at[me], output.at[me], own_sem.at[2])
    own_f.start()
    sum_everywhere(splits, copies, part, total_ref, *sum_refs)
    own_f.wait()
    own_b.wait()
    for slot, peer in enumerate(far + near):
        x_copy(peer, slot).wait_send()
        c_copy(peer, slot).wait_send()
        send(out_row.at[peer], output.at[peer], f_sent.at[peer], f_land.at[peer], "seq", peer).wait()
        send(xr.at[peer], dx_out.at[peer], b_sent.at[peer], b_land.at[peer], "seq", peer).wait()


def whole_block(splits, copies, solo, lengths, inputs, cotangent, small, weights):
    span, width = inputs.shape[1:]
    total = splits * span
    hidden = weights[2].shape[1]
    heads = 2 * width // LANES
    blocks = TILE // span
    anyspace = pl.BlockSpec(memory_space=pl.ANY)
    vmem = pl.BlockSpec(memory_space=pltpu.VMEM)
    bf, f32 = jnp.bfloat16, jnp.float32
    row = (splits, span, width)
    shapes = [
        (row, bf),
        (row, bf),
        ((2 * RANK, 8 * width), f32),
        (row, bf),
        (row, bf),
        ((heads // 2, total, LANES), bf),
        ((total, width), f32),
        ((total, hidden), bf),
        ((total, hidden), bf),
    ]
    dma = pltpu.SemaphoreType.DMA
    scratch = [
        *[pltpu.VMEM(w.shape, bf) for w in weights],
        pltpu.VMEM((heads, total, LANES), bf),
        pltpu.VMEM((heads, total, LANES), bf),
        pltpu.VMEM((heads, total, LANES), bf),
        pltpu.VMEM((heads // 2, total, LANES), f32),
        pltpu.VMEM((heads // 2, total, LANES), f32),
        pltpu.VMEM(row, bf),
        pltpu.VMEM((heads // 2, TILE, LANES), bf),
        pltpu.VMEM((TILE, width), f32),
        pltpu.VMEM((TILE, hidden), bf),
        pltpu.VMEM((TILE, hidden), bf),
        pltpu.VMEM((blocks, span, width), bf),
        pltpu.VMEM((blocks, span, width), bf),
        pltpu.VMEM((heads, TILE, LANES), bf),
        pltpu.VMEM((heads // 2, TILE, LANES), bf),
        pltpu.VMEM((total, LANES), bf),
        pltpu.VMEM((2 * RANK, 8 * width), f32),
        *adapter_scratch(width, hidden),
        dma((4,)),
        dma((5,)),
        dma((4 + blocks,)),
        dma((3,)),
        *[dma((splits,)) for _ in range(8)],
    ]
    if not solo:
        scratch += sum_scratch(splits, copies, 8 * width)
    return pl.pallas_call(
        lambda *refs: block_kernel(splits, copies, solo, *refs),
        out_shape=[jax.ShapeDtypeStruct(s, d) for s, d in shapes],
        in_specs=[pl.BlockSpec(memory_space=pltpu.SMEM)] + [anyspace] * 6 + [vmem] * len(small),
        out_specs=[anyspace, anyspace, vmem] + [anyspace] * 6,
        scratch_shapes=scratch,
        compiler_params=pltpu.CompilerParams(
            collective_id=None if solo else 4, has_side_effects=not solo, vmem_limit_bytes=64 * 2**20 - 2**18
        ),
        name="block",
    )(lengths, inputs, cotangent, *weights, *small)[:3]


def local_by_heads(
    inputs,
    cotangent,
    lengths,
    norm_gain,
    norm_shift,
    query_key_value_weight,
    output_projection_weight,
    first_feedforward_weight,
    second_feedforward_weight,
    biases,
    down_model,
    down_hidden,
    query_key_value_upward,
    hidden_adapter_upward,
    model_adapter_upward,
    row_down_model,
    col_down_model,
    row_down_hidden,
    col_down_hidden,
    row_up_qkv,
    col_up_qkv,
    row_up_hidden,
    col_up_hidden,
    row_up_model,
    col_up_model,
):
    rows, span, width = inputs.shape
    hidden_width = first_feedforward_weight.shape[1]
    count = rows * span
    spots = lax.axis_index("seq") * span + jnp.arange(span)
    keep = (spots[None, :] < lengths[:, None]).astype(jnp.float32).reshape(count, 1)
    flat = inputs.reshape(count, width).astype(jnp.float32)
    shifts = biases.astype(jnp.float32)
    query_bias = shifts[0:width]
    value_bias = shifts[width : 2 * width]
    projection_bias = shifts[2 * width : 3 * width]
    expand_bias_vector = shifts[3 * width : 3 * width + hidden_width]
    contract_bias_vector = shifts[3 * width + hidden_width : 4 * width + hidden_width]
    query_key_value_bias = jnp.concatenate([query_bias, jnp.zeros_like(query_bias), value_bias])
    gains = norm_gain.astype(jnp.float32)
    offsets = norm_shift.astype(jnp.float32)
    down_low = down_model.astype(jnp.bfloat16)
    hidden_down_low = down_hidden.astype(jnp.bfloat16)
    qkv_up_low = query_key_value_upward.astype(jnp.bfloat16)
    hidden_up_low = hidden_adapter_upward.astype(jnp.bfloat16)
    model_up_low = model_adapter_upward.astype(jnp.bfloat16)
    normalized_rows, unit_first, scaled_first = normalize(flat, gains[0], offsets[0])
    normalized_rows = normalized_rows.astype(jnp.bfloat16)
    mixed_rows, narrow_qkv = adapted(
        normalized_rows, query_key_value_weight, query_key_value_bias, down_low[0], qkv_up_low
    )
    mixed_rows = mixed_rows.astype(jnp.bfloat16).reshape(rows, span, 3, HEADS, HEAD_DIM)
    by_head = lax.all_to_all(mixed_rows, "seq", split_axis=3, concat_axis=1, tiled=True)
    out_heads, lse = lax.map(partial(head_forward, False), (by_head, lengths))
    attended_rows = jax.tree.map(
        lambda part, own: part.astype(own.dtype),
        lax.all_to_all(as_sent(out_heads), "seq", split_axis=1, concat_axis=2, tiled=True),
        out_heads,
    )
    attended_rows = attended_rows.reshape(count, width)
    branch_path, narrow_proj = adapted(
        attended_rows, output_projection_weight, projection_bias, down_low[1], model_up_low[0]
    )
    middle = flat + branch_path
    normed_mid, unit_second, scaled_second = normalize(middle, gains[1], offsets[1])
    normed_mid = normed_mid.astype(jnp.bfloat16)
    before, narrow_expand = adapted(
        normed_mid, first_feedforward_weight, expand_bias_vector, down_low[2], hidden_up_low
    )
    activated, gelu_pull = jax.vjp(lambda value: jax.nn.gelu(value, approximate=True), before)
    activated = activated.astype(jnp.bfloat16)
    branch_out, narrow_contract = adapted(
        activated, second_feedforward_weight, contract_bias_vector, hidden_down_low, model_up_low[1]
    )
    output = (middle + branch_out).astype(jnp.bfloat16).reshape(rows, span, width)
    grad_out = cotangent.reshape(count, width).astype(jnp.float32) * keep
    grad_act, grad_down_contract, grad_up_contract = adapted_back(
        grad_out.astype(jnp.bfloat16),
        activated,
        second_feedforward_weight,
        hidden_down_low,
        model_up_low[1],
        narrow_contract,
    )
    grad_before = gelu_pull(grad_act)[0].astype(jnp.bfloat16)
    grad_norm_mid, grad_down_expand, grad_up_expand = adapted_back(
        grad_before, normed_mid, first_feedforward_weight, down_low[2], hidden_up_low, narrow_expand
    )
    grad_mid = grad_out + normalize_back(grad_norm_mid, unit_second, scaled_second, gains[1])
    grad_att, grad_down_proj, grad_up_proj = adapted_back(
        grad_mid.astype(jnp.bfloat16),
        attended_rows,
        output_projection_weight,
        down_low[1],
        model_up_low[0],
        narrow_proj,
    )
    grad_att = grad_att.astype(jnp.bfloat16).reshape(rows, span, HEADS, HEAD_DIM)
    grad_heads = lax.all_to_all(grad_att, "seq", split_axis=2, concat_axis=1, tiled=True)
    grad_triple = lax.map(partial(head_backward, False), (by_head, grad_heads, lse, lengths))
    grad_mixed = jax.tree.map(
        lambda part, own: part.astype(own.dtype),
        lax.all_to_all(as_sent(grad_triple), "seq", split_axis=1, concat_axis=3, tiled=True),
        grad_triple,
    )
    grad_mixed = grad_mixed.reshape(count, 3 * width)
    grad_normed, grad_down_qkv, grad_up_qkv = adapted_back(
        grad_mixed, normalized_rows, query_key_value_weight, down_low[0], qkv_up_low, narrow_qkv
    )
    input_grad = (
        (grad_mid + normalize_back(grad_normed, unit_first, scaled_first, gains[0]))
        .astype(jnp.bfloat16)
        .reshape(rows, span, width)
    )
    grads = lax.psum(
        (
            jnp.stack([grad_down_qkv, grad_down_proj, grad_down_expand]),
            grad_down_contract,
            grad_up_qkv,
            grad_up_expand,
            jnp.stack([grad_up_proj, grad_up_contract]),
        ),
        ("dp", "seq"),
    )
    grad_dm, grad_dh, grad_uq, grad_uh, grad_um = grads
    new_dm, row_dm, col_dm = factored(grad_dm, down_model, row_down_model, col_down_model)
    new_dh, row_dh, col_dh = factored(grad_dh, down_hidden, row_down_hidden, col_down_hidden)
    new_uq, row_uq, col_uq = factored(grad_uq, query_key_value_upward, row_up_qkv, col_up_qkv)
    new_uh, row_uh, col_uh = factored(grad_uh, hidden_adapter_upward, row_up_hidden, col_up_hidden)
    new_um, row_um, col_um = factored(grad_um, model_adapter_upward, row_up_model, col_up_model)
    return (
        output,
        input_grad,
        grad_dm,
        grad_dh,
        grad_uq,
        grad_uh,
        grad_um,
        new_dm,
        new_dh,
        new_uq,
        new_uh,
        new_um,
        row_dm,
        row_dh,
        row_uq,
        row_uh,
        row_um,
        col_dm,
        col_dh,
        col_uq,
        col_uh,
        col_um,
    )


def local_by_rows(
    pieces,
    copies,
    inputs,
    cotangent,
    lengths,
    norm_gain,
    norm_shift,
    query_key_value_weight,
    output_projection_weight,
    first_feedforward_weight,
    second_feedforward_weight,
    biases,
    down_model,
    down_hidden,
    query_key_value_upward,
    hidden_adapter_upward,
    model_adapter_upward,
    row_down_model,
    col_down_model,
    row_down_hidden,
    col_down_hidden,
    row_up_qkv,
    col_up_qkv,
    row_up_hidden,
    col_up_hidden,
    row_up_model,
    col_up_model,
):
    flip = lambda array: jnp.swapaxes(array, -1, -2)
    adapters = [
        flip(down_model),
        flip(down_hidden),
        query_key_value_upward,
        hidden_adapter_upward,
        model_adapter_upward,
    ]
    norms = [norm_gain, norm_shift]
    weights = [
        query_key_value_weight,
        output_projection_weight,
        first_feedforward_weight,
        second_feedforward_weight,
    ]
    output, input_grad, total = whole_block(
        pieces, copies, False, lengths, inputs, cotangent, [biases.reshape(1, -1)] + norms + adapters, weights
    )
    return update(
        total,
        output,
        input_grad,
        adapters,
        row_down_model,
        col_down_model,
        row_down_hidden,
        col_down_hidden,
        row_up_qkv,
        col_up_qkv,
        row_up_hidden,
        col_up_hidden,
        row_up_model,
        col_up_model,
    )


def local(pieces, copies, inputs, *others):
    if inputs.shape[0] == pieces and TILE % inputs.shape[1] == 0:
        return local_by_rows(pieces, copies, inputs, *others)
    return local_by_heads(inputs, *others)


def solution(mesh):
    placed = (
        P("dp", "seq", None),
        P("dp", "seq", None),
        P("dp"),
        P(),
        P(),
        P(),
        P(),
        P(),
        P(),
        P(),
        P(),
        P(),
        P(),
        P(),
        P(),
        P(),
        P(),
        P(),
        P(),
        P(),
        P(),
        P(),
        P(),
        P(),
        P(),
    )
    return jax.shard_map(
        partial(local, mesh.shape["seq"], mesh.shape["dp"]),
        mesh=mesh,
        in_specs=placed,
        out_specs=(
            P("dp", "seq", None),
            P("dp", "seq", None),
            P(),
            P(),
            P(),
            P(),
            P(),
            P(),
            P(),
            P(),
            P(),
            P(),
            P(),
            P(),
            P(),
            P(),
            P(),
            P(),
            P(),
            P(),
            P(),
            P(),
        ),
        check_vma=False,
    )
```

```python
from functools import partial

import jax
import jax.numpy as jnp
from jax import lax
from jax.experimental import pallas as pl
from jax.experimental.pallas import tpu as pltpu
from jax.sharding import PartitionSpec as P


HEADS = 16
HEAD_DIM = 64
STEP = 10


NORM_EPS = 1e-05
ADAPTER_SCALE = 8.0
STAT_EPS = 1e-30
CLIP_LEVEL = 1.0
RATE = 0.3
DECAY_WEIGHT = 0.01
MASKED = -1e30


def as_sent(array):

    def short(part):
        return part.astype(jnp.bfloat16) if part.dtype == jnp.float32 else part

    return jax.tree.map(short, array)


def normalize(values, gain, shift):
    centered = values - jnp.mean(values, axis=-1, keepdims=True)
    spread = jnp.mean(centered * centered, axis=-1, keepdims=True)
    scaled = lax.rsqrt(spread + NORM_EPS)
    unit = centered * scaled
    return (unit * gain + shift, unit, scaled)


def normalize_back(grad, unit, scaled, gain):
    gained = grad * gain
    return scaled * (
        gained
        - jnp.mean(gained, axis=-1, keepdims=True)
        - unit * jnp.mean(gained * unit, axis=-1, keepdims=True)
    )


def matrix_multiply(left, right):
    return jnp.dot(left, right, preferred_element_type=jnp.float32)


def inner_product(left, right):
    return jnp.einsum("tr,tc->rc", left, right, preferred_element_type=jnp.float32)


def compared_with(left, right):
    return jnp.einsum("tc,rc->tr", left, right, preferred_element_type=jnp.float32)


def adapted(source_rows, weight_matrix, bias_vector, down, upward_matrix):
    narrowed_rows = matrix_multiply(source_rows, down).astype(jnp.bfloat16)
    return (
        matrix_multiply(source_rows, weight_matrix)
        + bias_vector
        + ADAPTER_SCALE * matrix_multiply(narrowed_rows, upward_matrix),
        narrowed_rows,
    )


def adapted_back(gradient_lowrank, source_rows, weight_matrix, down, upward_matrix, narrowed_rows):
    gradient_upward = ADAPTER_SCALE * inner_product(narrowed_rows, gradient_lowrank)
    gradient_narrowed = (ADAPTER_SCALE * compared_with(gradient_lowrank, upward_matrix)).astype(
        jnp.bfloat16
    )
    grad_down = inner_product(source_rows, gradient_narrowed)
    grad_source = compared_with(gradient_lowrank, weight_matrix) + compared_with(
        gradient_narrowed, down
    )
    return (grad_source, grad_down, gradient_upward)


def score_block(operand):
    query, keys = operand
    return jnp.einsum("gqe,gke->gqk", query, keys, preferred_element_type=jnp.float32)


def mix_block(operand):
    weights, values = operand
    return jnp.einsum("gqk,gke->gqe", weights, values, preferred_element_type=jnp.float32)


def spread_block(operand):
    weights, queries = operand
    return jnp.einsum("gqk,gqe->gke", weights, queries, preferred_element_type=jnp.float32)


def masked_scores(query, keys, spots, length):
    total = keys.shape[1]
    size = min(512, total)
    reach = jnp.minimum(length, jnp.max(spots) + 1)
    places = jnp.arange(total)
    valid = (places[None, :] <= spots[:, None]) & (places[None, :] < length)
    pieces = []
    for begin in range(0, total, size):
        pieces.append(score_block((query, keys[:, begin : begin + size])))
    scores = jnp.concatenate(pieces, axis=-1) * query.shape[-1] ** (-0.5)
    return (jnp.where(valid[None], scores, MASKED), reach, size)


def attend(query, keys, values, spots, length):
    scores, reach, size = masked_scores(query, keys, spots, length)
    top = jnp.max(scores, axis=-1, keepdims=True)
    weights = jnp.exp(scores - top)
    summed = jnp.sum(weights, axis=-1, keepdims=True)
    probs = (weights / summed).astype(jnp.bfloat16)
    result = jnp.zeros(query.shape, jnp.float32)
    for begin in range(0, keys.shape[1], size):
        operand = (probs[:, :, begin : begin + size], values[:, begin : begin + size])
        result = result + mix_block(operand)
    return (result, (top + jnp.log(summed))[..., 0])


def attend_back(query, keys, values, spots, length, grad_rows, lse):
    scores, reach, size = masked_scores(query, keys, spots, length)
    probs = jnp.exp(scores - lse[..., None])
    pieces = []
    for begin in range(0, keys.shape[1], size):
        pieces.append(score_block((grad_rows, values[:, begin : begin + size])))
    dprob = jnp.concatenate(pieces, axis=-1)
    delta = jnp.sum(probs * dprob, axis=-1, keepdims=True)
    dscore = (probs * (dprob - delta)).astype(jnp.bfloat16)
    probs_low = probs.astype(jnp.bfloat16)
    scale = query.shape[-1] ** (-0.5)
    grad_query = jnp.zeros(query.shape, jnp.float32)
    key_parts = []
    value_parts = []
    for begin in range(0, keys.shape[1], size):
        grad_query = grad_query + mix_block(
            (dscore[:, :, begin : begin + size], keys[:, begin : begin + size])
        )
        key_parts.append(spread_block((dscore[:, :, begin : begin + size], query)))
        value_parts.append(spread_block((probs_low[:, :, begin : begin + size], grad_rows)))
    return (
        grad_query * scale,
        jnp.concatenate(key_parts, axis=1) * scale,
        jnp.concatenate(value_parts, axis=1),
    )


def heads_split(triple):
    return tuple((jnp.transpose(triple[:, index], (1, 0, 2)) for index in range(3)))


def head_forward(skip, item):
    triple, length = item
    spots = jnp.arange(triple.shape[0])
    query, keys, values = heads_split(triple)
    result, lse = attend(query, keys, values, spots, length)
    return (jnp.transpose(result, (1, 0, 2)).astype(jnp.bfloat16), lse)


def head_backward(skip, item):
    triple, grad_rows, lse, length = item
    spots = jnp.arange(triple.shape[0])
    query, keys, values = heads_split(triple)
    grads = attend_back(
        query, keys, values, spots, length, jnp.transpose(grad_rows, (1, 0, 2)), lse
    )
    return jnp.stack(grads, axis=0).transpose(2, 0, 1, 3).astype(jnp.bfloat16)


def factored(grad, weight_matrix, row, col):
    decay = 1.0 - STEP ** (-0.8)
    squares = grad * grad + STAT_EPS
    new_row = decay * row + (1.0 - decay) * jnp.mean(squares, axis=-1)
    new_col = decay * col + (1.0 - decay) * jnp.mean(squares, axis=-2)
    second = (
        new_row[..., :, None] * new_col[..., None, :] / jnp.mean(new_row, axis=-1)[..., None, None]
    )
    unit = grad * lax.rsqrt(second)
    level = jnp.sqrt(jnp.mean(unit * unit, axis=(-2, -1), keepdims=True))
    unit = unit / jnp.maximum(1.0, level / CLIP_LEVEL)
    rate = RATE * jnp.sqrt(jnp.mean(weight_matrix * weight_matrix, axis=(-2, -1), keepdims=True))
    return (weight_matrix - rate * (unit + DECAY_WEIGHT * weight_matrix), new_row, new_col)


LOG2E = 1.4426950408889634
NT = (((1,), (1,)), ((), ()))
TN = (((0,), (0,)), ((), ()))


def dotf(a, b, dims=(((1,), (0,)), ((), ()))):
    return lax.dot_general(a, b, dims, preferred_element_type=jnp.float32)


def triple(value):
    high = value.astype(jnp.bfloat16)
    rest = value - high.astype(jnp.float32)
    mid = rest.astype(jnp.bfloat16)
    low = (rest - mid.astype(jnp.float32)).astype(jnp.bfloat16)
    return high, mid, low


GELU_A = 0.7978845608028654
GELU_B = 0.7978845608028654 * 0.044715
RANK = 4


def norm_parts(values):
    centered = values - jnp.mean(values, axis=-1, keepdims=True)
    spread = jnp.mean(centered * centered, axis=-1, keepdims=True)
    scaled = lax.rsqrt(spread + NORM_EPS)
    return centered * scaled, scaled


def norm_back(grad, unit, scaled, gain):
    gained = grad * gain
    return scaled * (
        gained
        - jnp.mean(gained, axis=-1, keepdims=True)
        - unit * jnp.mean(gained * unit, axis=-1, keepdims=True)
    )


def low(value):
    return value.astype(jnp.bfloat16)


def wide(value):
    return value.astype(jnp.float32)


def gelu_pair(value):
    square = value * value
    half = 0.5 * value
    bent = jnp.tanh(value * (GELU_A + GELU_B * square))
    slope = (0.5 + 0.5 * bent) + half * (1.0 - bent * bent) * (GELU_A + 3.0 * GELU_B * square)
    return half + half * bent, slope


def peers_of(axis, size):
    me = lax.axis_index(axis)
    return me, [lax.rem(me + shift, size) for shift in range(1, size)]


def greet(axes):
    barrier = pltpu.get_barrier_semaphore()
    count = 0
    for axis, size in axes:
        _, peers = peers_of(axis, size)
        for peer in peers:
            pl.semaphore_signal(
                barrier, inc=1, device_id={axis: peer}, device_id_type=pl.DeviceIdType.MESH
            )
        count += len(peers)
    pl.semaphore_wait(barrier, count)


def send(source, target, sent, landed, axis, peer):
    return pltpu.make_async_remote_copy(
        src_ref=source,
        dst_ref=target,
        send_sem=sent,
        recv_sem=landed,
        device_id={axis: peer},
        device_id_type=pl.DeviceIdType.MESH,
    )


def sum_everywhere(
    splits, copies, part_ref, total_ref, dp_in, seq_in, own, piece, d_sent, d_land, s_sent, s_land, g_sent, g_land, e_sent, e_land
):
    size = part_ref.shape[1] // copies
    small = size // splits
    me, peers = peers_of("seq", splits)
    mine, others = peers_of("dp", copies)

    def columns(index):
        return pl.ds(pl.multiple_of(index * size, size), size)

    def narrow_columns(index, start=0):
        return pl.ds(pl.multiple_of(start + index * small, small), small)

    sent = []

    def start(copy):
        copy.start()
        sent.append(copy)

    for shift, peer in enumerate(others):
        start(send(part_ref.at[:, columns(peer)], dp_in.at[mine], d_sent.at[shift], d_land.at[mine], "dp", peer))
    dp_in[mine] = part_ref[:, columns(mine)]
    for peer in others:
        send(part_ref.at[:, columns(mine)], dp_in.at[peer], d_sent.at[0], d_land.at[peer], "dp", peer).wait_recv()
    summed = dp_in[0]
    for index in range(1, copies):
        summed = summed + dp_in[index]
    own[...] = summed
    for shift, peer in enumerate(peers):
        start(send(own.at[:, narrow_columns(peer)], seq_in.at[me], s_sent.at[shift], s_land.at[me], "seq", peer))
    seq_in[me] = own[:, narrow_columns(me)]
    for peer in peers:
        send(own.at[:, narrow_columns(me)], seq_in.at[peer], s_sent.at[0], s_land.at[peer], "seq", peer).wait_recv()
    summed = seq_in[0]
    for index in range(1, splits):
        summed = summed + seq_in[index]
    piece[...] = summed
    base = mine * size
    total_ref[:, narrow_columns(me, base)] = summed
    for shift, peer in enumerate(peers):
        start(send(piece, total_ref.at[:, narrow_columns(me, base)], g_sent.at[shift], g_land.at[me], "seq", peer))
    for peer in peers:
        send(piece, total_ref.at[:, narrow_columns(peer, base)], g_sent.at[0], g_land.at[peer], "seq", peer).wait_recv()
    for shift, peer in enumerate(others):
        part = total_ref.at[:, columns(mine)]
        start(send(part, part, e_sent.at[shift], e_land.at[mine], "dp", peer))
    for peer in others:
        part = total_ref.at[:, columns(peer)]
        send(part, part, e_sent.at[0], e_land.at[peer], "dp", peer).wait_recv()
    for copy in sent:
        copy.wait_send()


def sum_scratch(splits, copies, width):
    size = width // copies
    small = size // splits
    dma = pltpu.SemaphoreType.DMA
    return [
        pltpu.VMEM((copies, 8, size), jnp.float32),
        pltpu.VMEM((splits, 8, small), jnp.float32),
        pltpu.VMEM((8, size), jnp.float32),
        pltpu.VMEM((8, small), jnp.float32),
        dma((copies,)),
        dma((copies,)),
        dma((splits,)),
        dma((splits,)),
        dma((splits,)),
        dma((splits,)),
        dma((copies,)),
        dma((copies,)),
    ]


def across(column):
    count = column.shape[0]
    diagonal = lax.broadcasted_iota(jnp.int32, (count, count), 0) == lax.broadcasted_iota(
        jnp.int32, (count, count), 1
    )
    return jnp.sum(jnp.where(diagonal, jnp.broadcast_to(column, (count, count)), 0.0), axis=0, keepdims=True)


def upright(line):
    count = line.shape[1]
    diagonal = lax.broadcasted_iota(jnp.int32, (count, count), 0) == lax.broadcasted_iota(
        jnp.int32, (count, count), 1
    )
    return jnp.sum(jnp.where(diagonal, jnp.broadcast_to(line, (count, count)), 0.0), axis=1, keepdims=True)


def factored_step(grad, weight, short_line, long_line, rows_long):
    decay = 1.0 - STEP ** (-0.8)
    squares = grad * grad + STAT_EPS
    new_short = decay * upright(short_line) + (1.0 - decay) * jnp.mean(squares, axis=1, keepdims=True)
    new_long = decay * long_line + (1.0 - decay) * jnp.mean(squares, axis=0, keepdims=True)
    if rows_long:
        middle = jnp.mean(new_long, axis=1, keepdims=True)
    else:
        middle = jnp.mean(new_short, axis=0, keepdims=True)
    unit = grad * lax.rsqrt(new_short * new_long / middle)
    entries = grad.shape[0] * grad.shape[1]

    def mean_square(value):
        return jnp.sum(jnp.sum(value * value, axis=1, keepdims=True), axis=0, keepdims=True) / entries

    level = jnp.sqrt(mean_square(unit))
    unit = unit / jnp.maximum(1.0, level / CLIP_LEVEL)
    rate = RATE * jnp.sqrt(mean_square(weight))
    return weight - rate * (unit + DECAY_WEIGHT * weight), across(new_short), new_long


def update_kernel(
    total_ref, output_in, grad_in, dm, dh, uq, uh, um, row_dm, col_dm, row_dh, col_dh, row_uq, col_uq, row_uh, col_uh, row_um, col_um,
    output_out, grad_out, g_dm, g_dh, g_uq, g_uh, g_um, n_dm, n_dh, n_uq, n_uh, n_um,
    r_dm, r_dh, r_uq, r_uh, r_um, c_dm, c_dh, c_uq, c_uh, c_um, held_out, held_grad, sems,
):
    moves = [
        pltpu.make_async_copy(output_in, held_out, sems.at[0]),
        pltpu.make_async_copy(grad_in, held_grad, sems.at[1]),
    ]
    for move in moves:
        move.start()
    moves = [
        (moves[0], pltpu.make_async_copy(held_out, output_out, sems.at[0])),
        (moves[1], pltpu.make_async_copy(held_grad, grad_out, sems.at[1])),
    ]
    for move, onward in moves:
        move.wait()
        onward.start()
    width = dm.shape[2]
    hidden = dh.shape[1]
    for index in range(3):
        grad = total_ref[0:RANK, index * width : (index + 1) * width]
        g_dm[index] = grad
        n_dm[index], c_dm[index : index + 1, :], r_dm[index : index + 1, :] = factored_step(
            grad, dm[index], col_dm[index : index + 1, :], row_dm[index : index + 1, :], True
        )
    grad = total_ref[0:RANK, 3 * width : 6 * width]
    g_uq[...] = grad
    n_uq[...], r_uq[...], c_uq[...] = factored_step(grad, uq[...], row_uq[...], col_uq[...], False)
    for index in range(2):
        grad = total_ref[0:RANK, (6 + index) * width : (7 + index) * width]
        g_um[index] = grad
        n_um[index], r_um[index : index + 1, :], c_um[index : index + 1, :] = factored_step(
            grad, um[index], row_um[index : index + 1, :], col_um[index : index + 1, :], False
        )
    grad = total_ref[RANK : 2 * RANK, 0:hidden]
    g_dh[...] = grad
    n_dh[...], c_dh[...], r_dh[...] = factored_step(grad, dh[...], col_dh[...], row_dh[...], True)
    grad = total_ref[RANK : 2 * RANK, hidden : 2 * hidden]
    g_uh[...] = grad
    n_uh[...], r_uh[...], c_uh[...] = factored_step(grad, uh[...], row_uh[...], col_uh[...], False)
    for _, onward in moves:
        onward.wait()


def update(total, output, input_grad, adapters, row_dm, col_dm, row_dh, col_dh, row_uq, col_uq, row_uh, col_uh, row_um, col_um):
    flip = lambda array: jnp.swapaxes(array, -1, -2)
    line = lambda array: array.reshape(1, -1)
    given = [
        row_dm, col_dm, line(row_dh), line(col_dh), line(row_uq), line(col_uq), line(row_uh), line(col_uh), row_um, col_um,
    ]
    stats = given[0::2] + given[1::2]
    anyspace = pl.BlockSpec(memory_space=pl.ANY)
    vmem = pl.BlockSpec(memory_space=pltpu.VMEM)
    results = pl.pallas_call(
        update_kernel,
        out_shape=[jax.ShapeDtypeStruct(a.shape, a.dtype) for a in [output, input_grad] + adapters + adapters + stats],
        in_specs=[vmem, anyspace, anyspace] + [vmem] * 15,
        out_specs=[anyspace, anyspace] + [vmem] * 20,
        scratch_shapes=[
            pltpu.VMEM(output.shape, output.dtype),
            pltpu.VMEM(output.shape, output.dtype),
            pltpu.SemaphoreType.DMA((2,)),
        ],
        compiler_params=pltpu.CompilerParams(vmem_limit_bytes=60 * 2**20),
        name="factored_update",
    )(total, output, input_grad, *adapters, *given)
    results = list(results)
    for index in (2, 3, 7, 8):
        results[index] = flip(results[index])
    olds = (row_dm, row_dh, row_uq, row_uh, row_um, col_dm, col_dh, col_uq, col_uh, col_um)
    for index, old in zip(range(12, 22), olds):
        results[index] = results[index].reshape(old.shape)
    return tuple(results)


def fill_adapters(dm_ref, dh_ref, uq_ref, uh_ref, um_ref, aq, ap, a1, a2, bq, bp, b2, b1):
    for index, ref in enumerate((aq, ap, a1)):
        ref[...] = low(dm_ref[index])
    a2[...] = low(dh_ref[...])
    for ref, value in ((bq, uq_ref[...]), (bp, um_ref[0]), (b2, um_ref[1]), (b1, uh_ref[...])):
        ref[...] = low(ADAPTER_SCALE * wide(low(value)))


def adapter_scratch(width, hidden):
    sizes = [width, width, width, hidden, 3 * width, width, width, hidden]
    return [pltpu.VMEM((RANK, size), jnp.bfloat16) for size in sizes]


TILE = 256
GROUP = 4
LANES = 128


def peer_order(me, splits):
    half = splits // 2
    side, place = me // half, lax.rem(me, half)
    far = [(1 - side) * half + lax.rem(place + shift, half) for shift in range(half)]
    near = [side * half + lax.rem(place + shift, half) for shift in range(1, half)]
    return far, near


def block_kernel(
    splits, copies, solo,
    lengths_ref, inputs, cotangent, wqkv_hbm, wo_hbm, w1_hbm, w2_hbm,
    bias_ref, gain_ref, shift_ref, dm_ref, dh_ref, uq_ref, uh_ref, um_ref,
    output, dx_out, total_ref, cot_in, out_row, att_hbm, mid_hbm, act_hbm, slope_hbm,
    wqkv, wo, w1, w2, kx, vx, qx, dk, dv, xr, att, mid, act, slope, cot_t, outs, gx, dq, narrow, part,
    aq, ap, a1, a2, bq, bp, b2, b1,
    w_sem, s_sem, l_sem, own_sem, x_sent, x_land, c_sent, c_land, f_sent, f_land, b_sent, b_land,
    *sum_refs,
):
    me = 0 if solo else lax.axis_index("seq")
    span, width = xr.shape[1], xr.shape[2]
    hidden = w1.shape[1]
    total = splits * span
    tiles = total // TILE
    blocks = TILE // span
    heads = kx.shape[0]
    pairs = heads // 2
    half = LANES // 2
    length = lengths_ref[me]
    upper = me >= splits // 2

    loads = [
        pltpu.make_async_copy(source, target, w_sem.at[index])
        for index, (source, target) in enumerate(((wqkv_hbm, wqkv), (wo_hbm, wo), (w1_hbm, w1), (w2_hbm, w2)))
    ]
    own_x = pltpu.make_async_copy(inputs if solo else inputs.at[me], xr if solo else xr.at[me], own_sem.at[0])
    own_b = pltpu.make_async_copy(xr.at[me], dx_out.at[me], own_sem.at[1])

    own_f = pltpu.make_async_copy(out_row.at[me], output.at[me], own_sem.at[2])

    def saves(tile):
        rows = pl.ds(tile * TILE, TILE)
        moves = (
            (att, att_hbm.at[:, rows, :]),
            (mid, mid_hbm.at[rows, :]),
            (act, act_hbm.at[rows, :]),
            (slope, slope_hbm.at[rows, :]),
            (outs, out_row.at[pl.ds(tile * blocks, blocks)]),
        )
        return [pltpu.make_async_copy(a, b, s_sem.at[i]) for i, (a, b) in enumerate(moves)]

    def fetches(tile):
        rows = pl.ds(tile * TILE, TILE)
        moves = (
            (slope_hbm.at[rows, :], slope),
            (act_hbm.at[rows, :], act),
            (att_hbm.at[:, rows, :], att),
            (mid_hbm.at[rows, :], mid),
        )
        return [pltpu.make_async_copy(a, b, l_sem.at[i]) for i, (a, b) in enumerate(moves)]

    def x_copy(peer, slot):
        return send(inputs.at[peer], xr.at[me], x_sent.at[slot], x_land.at[me], "seq", peer)

    def c_copy(peer, slot):
        return send(cotangent.at[peer], cot_in.at[me], c_sent.at[slot], c_land.at[me], "seq", peer)

    def f_copy(block):
        return send(out_row.at[block], output.at[me], f_sent.at[block], f_land.at[me], "seq", block)

    def b_copy(block):
        return send(xr.at[block], dx_out.at[me], b_sent.at[block], b_land.at[me], "seq", block)

    def tile_blocks(tile):
        return range(tile * blocks, (tile + 1) * blocks)

    def cot_move(block, fetched):
        slot = cot_t.at[block % blocks]
        source = cotangent.at[me] if fetched else cot_in.at[block]
        return pltpu.make_async_copy(source, slot, l_sem.at[4 + block % blocks])

    def cot_fetch(tile):
        if solo:
            for block in tile_blocks(tile):
                cot_move(block, False).start()
            return
        for block in tile_blocks(tile):

            @pl.when(me == block)
            def _():
                cot_move(block, True).start()

            @pl.when(me != block)
            def _():
                send(cotangent.at[block], cot_in.at[block], c_sent.at[0], c_land.at[block], "seq", block).wait_recv()
                cot_move(block, False).start()

    def x_wait(tile):
        if solo:
            return
        for block in tile_blocks(tile):

            @pl.when(me != block)
            def _():
                send(inputs.at[block], xr.at[block], x_sent.at[0], x_land.at[block], "seq", block).wait_recv()

    def send_output(tile):
        if solo:
            return
        for block in tile_blocks(tile):

            @pl.when(me != block)
            def _():
                f_copy(block).start()

    if not solo:
        greet((("seq", splits), ("dp", copies)))
    own_x.start()
    loads[0].start()
    if not solo:
        far, near = peer_order(me, splits)
        early = lax.rem(me, splits // 2) < splits // 4
        lower_early = jnp.logical_and(early, jnp.logical_not(upper))
        lower_late = jnp.logical_and(jnp.logical_not(early), jnp.logical_not(upper))
        ways = list(enumerate(far + near))

        @pl.when(jnp.logical_not(lower_early))
        def _():
            for slot, peer in ways[len(far) :]:
                x_copy(peer, slot).start()

        @pl.when(jnp.logical_not(lower_late))
        def _():
            for slot, peer in ways[: len(far)]:
                x_copy(peer, slot).start()

    for load in loads[1:]:
        load.start()
    fill_adapters(dm_ref, dh_ref, uq_ref, uh_ref, um_ref, aq, ap, a1, a2, bq, bp, b2, b1)
    part[...] = jnp.zeros_like(part)

    lane = lax.broadcasted_iota(jnp.int32, (TILE, LANES), 1)
    row = lax.broadcasted_iota(jnp.int32, (TILE, TILE), 0)
    col = lax.broadcasted_iota(jnp.int32, (TILE, TILE), 1)
    zero = jnp.zeros((TILE, LANES), jnp.bfloat16)
    one = jnp.ones((TILE, LANES), jnp.bfloat16)
    scale = half ** (-0.5)
    owns = (lane < half, lane >= half)
    spares = (half, 0)

    def absorb(weight, down, up):
        rows, columns = weight.shape
        size = 1024

        def step(index, carry):
            span_rows = pl.ds(pl.multiple_of(index * TILE, TILE), TILE)
            left = down[:, span_rows]
            for start in range(0, columns, size):
                part_ref = weight.at[span_rows, pl.ds(start, size)]
                part_ref[...] = low(wide(part_ref[...]) + dotf(left, up[:, start : start + size], TN))
            return carry

        lax.fori_loop(0, rows // TILE, step, 0)

    def with_extra(own, spare, value, extra):
        high, middle, rest = triple(extra)
        return jnp.where(
            own,
            value,
            jnp.where(lane == spare, high, jnp.where(lane == spare + 1, middle, jnp.where(lane == spare + 2, rest, zero))),
        )

    def bias(start, size):
        return wide(bias_ref[0:1, start : start + size])

    def rows_of(tile):
        if isinstance(tile, int):
            return pl.ds(tile * TILE, TILE)
        return pl.ds(pl.multiple_of(tile * TILE, TILE), TILE)

    def project(tile):
        rows = rows_of(tile)
        x = wide(xr[pl.ds(tile * blocks, blocks)].reshape(TILE, width))
        unit, _ = norm_parts(x)
        normed = low(unit * wide(gain_ref[0:1, :]) + wide(shift_ref[0:1, :]))
        narrow_q = low(dotf(normed, aq[...], NT))
        narrow[rows, 0:RANK] = narrow_q
        spot = tile * TILE + lax.broadcasted_iota(jnp.int32, (TILE, LANES), 0)
        limit = jnp.where(spot < length, 0.0, MASKED).astype(jnp.bfloat16)
        size = 512
        for index in range(3):
            for start in range(0, width, size):
                column = index * width + start
                value = dotf(normed, wqkv[:, column : column + size])
                if index == 0:
                    value = value + bias(start, size)
                if index == 2:
                    value = value + bias(width + start, size)
                value = low(value)
                for pair in range(size // LANES):
                    piece = value[:, pair * LANES : (pair + 1) * LANES]
                    for parity in range(2):
                        head = 2 * (start // LANES + pair) + parity
                        own, spare = owns[parity], spares[parity]
                        if index == 0:
                            extra = jnp.where(lane == spare + 3, one, zero)
                            qx[head, rows, :] = jnp.where(own, piece * jnp.asarray(scale, jnp.bfloat16), extra)
                        elif index == 1:
                            extra = jnp.where(lane == spare + 3, limit, jnp.where(lane < spare + 3, one, zero))
                            kx[head, rows, :] = jnp.where(own, piece, extra)
                        else:
                            vx[head, rows, :] = jnp.where(own, piece, one)

    own_x.wait()
    loads[0].wait()
    absorb(wqkv, aq, bq)
    loads[1].wait()
    absorb(wo, ap, bp)
    if not solo:

        @pl.when(lower_early)
        def _():
            for slot, peer in ways[len(far) :]:
                x_copy(peer, slot).start()

    loads[2].wait()
    absorb(w1, a1, b1)
    if not solo:

        @pl.when(lower_late)
        def _():
            for slot, peer in ways[: len(far)]:
                x_copy(peer, slot).start()

    loads[3].wait()
    absorb(w2, a2, b2)
    if not solo:

        @pl.when(upper)
        def _():
            for tile in range(tiles // 2, tiles):
                x_wait(tile)
            lax.fori_loop(tiles // 2, tiles, lambda tile, carry: (project(tile), carry)[1], 0)

    for tile in range(tiles):
        begin, end = tile * TILE, (tile + 1) * TILE
        if tile < tiles // 2:
            x_wait(tile)
            project(tile)
        elif solo:
            project(tile)
        else:

            @pl.when(jnp.logical_not(upper))
            def _():
                x_wait(tile)
                project(tile)

        if not solo:
            last_tile = jnp.logical_and(upper, jnp.logical_not(early))
            ready = last_tile if tile == tiles // 2 - 1 else jnp.logical_not(last_tile)
            if tile == tiles // 2 - 1 or tile == tiles // 2:

                @pl.when(ready)
                def _():
                    for slot, peer in enumerate(far + near):
                        c_copy(peer, slot).start()

        if tile:
            saves(tile - 1)[0].wait()
        valid = begin + lax.broadcasted_iota(jnp.int32, (TILE, LANES), 0) < length
        causal = col <= row

        def attend(index, carry):
            def scores(unit):
                head = index * GROUP + unit
                return dotf(qx[head, begin:end, :], kx[head, 0:end, :], NT)

            def mix(unit, value):
                head = index * GROUP + unit
                last = jnp.where(causal, value[:, begin:], MASKED)
                value = jnp.concatenate([value[:, :begin], last], axis=1) if begin else last
                top = jnp.max(value, axis=-1, keepdims=True)
                weights = low(jnp.exp2((value - top) * LOG2E))
                mixed = dotf(weights, vx[head, 0:end, :])
                spare, own = spares[unit % 2], owns[unit % 2]
                summed = mixed[:, spare : spare + 1]
                back = jnp.where(valid, -(top + jnp.log(summed)), MASKED)
                qx[head, begin:end, :] = with_extra(own, spare, qx[head, begin:end, :], back)
                return mixed * (1.0 / summed)

            ahead = scores(0)
            results = []
            for unit in range(GROUP):
                value = ahead
                if unit + 1 < GROUP:
                    ahead = scores(unit + 1)
                results.append(mix(unit, value))
            for unit in range(0, GROUP, 2):
                att[index * (GROUP // 2) + unit // 2] = low(jnp.where(owns[0], results[unit], results[unit + 1]))
            return carry

        lax.fori_loop(0, heads // GROUP, attend, 0)
        if tile:
            for save in saves(tile - 1)[1:]:
                save.wait()
        attended = jnp.concatenate([att[index] for index in range(pairs)], axis=1)
        narrow_p = low(dotf(attended, ap[...], NT))
        middle = (
            wide(xr[tile * blocks : (tile + 1) * blocks].reshape(TILE, width))
            + dotf(attended, wo[...])
            + bias(2 * width, width)
        )
        mid[...] = middle
        unit, _ = norm_parts(middle)
        normed = low(unit * wide(gain_ref[1:2, :]) + wide(shift_ref[1:2, :]))
        narrow_1 = low(dotf(normed, a1[...], NT))
        size = 256

        def expand(start):
            return dotf(normed, w1[:, start : start + size]) + bias(3 * width + start, size)

        result = middle + bias(3 * width + hidden, width)
        narrow_2 = jnp.zeros((TILE, RANK), jnp.float32)
        ahead = expand(0)
        for start in range(0, hidden, size):
            stop = start + size
            before = ahead
            if stop < hidden:
                ahead = expand(stop)
            active, bend = gelu_pair(before)
            active = low(active)
            act[:, start:stop] = active
            slope[:, start:stop] = low(bend)
            result = result + dotf(active, w2[start:stop, :])
            narrow_2 = narrow_2 + dotf(active, a2[:, start:stop], NT)
        narrow_2 = low(narrow_2)
        outs[...] = low(result).reshape(blocks, span, width)
        narrow[begin:end, RANK : 2 * RANK] = narrow_p
        narrow[begin:end, 2 * RANK : 3 * RANK] = narrow_1
        narrow[begin:end, 3 * RANK : 4 * RANK] = narrow_2
        if tile < tiles - 1:
            for save in saves(tile):
                save.start()
        else:
            saves(tile)[4].start()

    def add_upper(start, value):
        part[0:RANK, start : start + value.shape[1]] += value

    def add_lower(start, value):
        part[RANK : 2 * RANK, start : start + value.shape[1]] += value

    cot_fetch(tiles - 1)
    for tile in reversed(range(tiles)):
        begin, end = tile * TILE, (tile + 1) * TILE
        newest = tile == tiles - 1
        if newest:
            pass
        else:
            for fetch in fetches(tile)[0:3]:
                fetch.wait()
        for block in tile_blocks(tile):
            cot_move(block, False).wait()
        spot = begin + lax.broadcasted_iota(jnp.int32, (TILE, width), 0)
        given = cot_t[...].reshape(TILE, width)
        gout = jnp.where(spot < length, given, jnp.zeros_like(given))
        narrow_q = narrow[begin:end, 0:RANK]
        narrow_p = narrow[begin:end, RANK : 2 * RANK]
        narrow_1 = narrow[begin:end, 2 * RANK : 3 * RANK]
        narrow_2 = narrow[begin:end, 3 * RANK : 4 * RANK]
        gn2 = low(dotf(gout, b2[...], NT))
        add_upper(7 * width, dotf(narrow_2, gout, TN))
        size = 512

        def contract(start):
            return dotf(gout, w2[start : start + size, :], NT)

        gnorm = jnp.zeros((TILE, width), jnp.float32)
        gn1 = jnp.zeros((TILE, RANK), jnp.float32)
        ahead = contract(0)
        for start in range(0, hidden, size):
            stop = start + size
            gact = ahead
            if stop < hidden:
                ahead = contract(stop)
            gbefore = low(gact * wide(slope[:, start:stop]))
            add_lower(start, dotf(gn2, act[:, start:stop], TN))
            add_lower(hidden + start, dotf(narrow_1, gbefore, TN))
            gn1 = gn1 + dotf(gbefore, b1[:, start:stop], NT)
            gnorm = gnorm + dotf(gbefore, w1[:, start:stop], NT)
        gn1 = low(gn1)
        if not newest:
            fetches(tile)[3].wait()
        unit, scaled = norm_parts(mid[...])
        normed = low(unit * wide(gain_ref[1:2, :]) + wide(shift_ref[1:2, :]))
        add_upper(2 * width, dotf(gn1, normed, TN))
        grad = wide(gout) + norm_back(gnorm, unit, scaled, wide(gain_ref[1:2, :]))
        mid[...] = grad
        glow = low(grad)
        gnp = low(dotf(glow, bp[...], NT))
        add_upper(6 * width, dotf(narrow_p, glow, TN))
        gatt = low(dotf(glow, wo[...], NT))
        attended = jnp.concatenate([att[index] for index in range(pairs)], axis=1)
        add_upper(width, dotf(gnp, attended, TN))
        for index in range(pairs):
            piece = gatt[:, index * LANES : (index + 1) * LANES]
            product = wide(piece) * wide(att[index])
            for parity in range(2):
                own, spare = owns[parity], spares[parity]
                delta = -jnp.sum(jnp.where(own, product, 0.0), axis=-1, keepdims=True)
                gx[2 * index + parity] = with_extra(own, spare, piece, jnp.broadcast_to(delta, (TILE, LANES)))
        if tile:
            for fetch in fetches(tile - 1)[0:3]:
                fetch.start()
            cot_fetch(tile - 1)
        if newest:
            saves(tile)[4].wait()
            for done in range(tiles):
                send_output(done)
            if not solo:
                own_f.start()
        causal = row <= col

        def attend_back(index, carry):
            def products(unit):
                head = index * GROUP + unit
                return (
                    dotf(kx[head, 0:end, :], qx[head, begin:end, :], NT),
                    dotf(vx[head, 0:end, :], gx[head], NT),
                )

            def spread(unit, scores, dprob):
                head = index * GROUP + unit
                weights = jnp.exp2(scores * LOG2E)
                last = jnp.where(causal, weights[begin:], 0.0)
                weights = jnp.concatenate([weights[:begin], last], axis=0) if begin else last
                dscore = low(weights * dprob)
                return (
                    dotf(dscore, kx[head, 0:end, :], TN),
                    dotf(dscore, qx[head, begin:end, :]),
                    dotf(low(weights), gx[head]),
                )

            ahead = products(0)
            results = []
            for unit in range(GROUP):
                given = ahead
                if unit + 1 < GROUP:
                    ahead = products(unit + 1)
                results.append(spread(unit, *given))
            first_lanes = lax.broadcasted_iota(jnp.int32, (end, LANES), 1) < half
            for unit in range(0, GROUP, 2):
                pair = index * (GROUP // 2) + unit // 2
                even, odd = results[unit], results[unit + 1]
                dq[pair] = low(jnp.where(owns[0], even[0], odd[0]) * scale)
                more_k = jnp.where(first_lanes, even[1], odd[1])
                more_v = jnp.where(first_lanes, even[2], odd[2])
                if newest:
                    dk[pair] = more_k
                    dv[pair] = more_v
                else:
                    dk[pair, 0:end, :] += more_k
                    dv[pair, 0:end, :] += more_v
            return carry

        lax.fori_loop(0, heads // GROUP, attend_back, 0)
        values = [
            jnp.concatenate([dq[index] for index in range(pairs)], axis=1),
            jnp.concatenate([low(dk[index, begin:end, :]) for index in range(pairs)], axis=1),
            jnp.concatenate([low(dv[index, begin:end, :]) for index in range(pairs)], axis=1),
        ]
        gnq = jnp.zeros((TILE, RANK), jnp.float32)
        gnormed = jnp.zeros((TILE, width), jnp.float32)
        for index, value in enumerate(values):
            start, stop = index * width, (index + 1) * width
            gnq = gnq + dotf(value, bq[:, start:stop], NT)
            add_upper(3 * width + start, dotf(narrow_q, value, TN))
            gnormed = gnormed + dotf(value, wqkv[:, start:stop], NT)
        gnq = low(gnq)
        unit, scaled = norm_parts(wide(xr[tile * blocks : (tile + 1) * blocks].reshape(TILE, width)))
        normed = low(unit * wide(gain_ref[0:1, :]) + wide(shift_ref[0:1, :]))
        add_upper(0, dotf(gnq, normed, TN))
        dx = low(mid[...] + norm_back(gnormed, unit, scaled, wide(gain_ref[0:1, :])))
        if tile:
            fetches(tile - 1)[3].start()
        xr[tile * blocks : (tile + 1) * blocks] = dx.reshape(blocks, span, width)
        if not solo:
            for block in tile_blocks(tile):

                @pl.when(me != block)
                def _():
                    b_copy(block).start()

                @pl.when(me == block)
                def _():
                    own_b.start()

    part[0:RANK, 3 * width :] = ADAPTER_SCALE * part[0:RANK, 3 * width :]
    part[RANK : 2 * RANK, hidden:] = ADAPTER_SCALE * part[RANK : 2 * RANK, hidden:]
    if solo:
        total_ref[...] = part[...]
        return
    sum_everywhere(splits, copies, part, total_ref, *sum_refs)
    own_f.wait()
    own_b.wait()
    for slot, peer in enumerate(far + near):
        x_copy(peer, slot).wait_send()
        c_copy(peer, slot).wait_send()
        send(out_row.at[peer], output.at[peer], f_sent.at[peer], f_land.at[peer], "seq", peer).wait()
        send(xr.at[peer], dx_out.at[peer], b_sent.at[peer], b_land.at[peer], "seq", peer).wait()


def whole_block(splits, copies, solo, lengths, inputs, cotangent, small, weights):
    span, width = inputs.shape[1:]
    total = splits * span
    hidden = weights[2].shape[1]
    heads = 2 * width // LANES
    blocks = TILE // span
    anyspace = pl.BlockSpec(memory_space=pl.ANY)
    vmem = pl.BlockSpec(memory_space=pltpu.VMEM)
    bf, f32 = jnp.bfloat16, jnp.float32
    row = (splits, span, width)
    shapes = [
        (row, bf),
        (row, bf),
        ((2 * RANK, 8 * width), f32),
        (row, bf),
        (row, bf),
        ((heads // 2, total, LANES), bf),
        ((total, width), f32),
        ((total, hidden), bf),
        ((total, hidden), bf),
    ]
    dma = pltpu.SemaphoreType.DMA
    scratch = [
        *[pltpu.VMEM(w.shape, bf) for w in weights],
        pltpu.VMEM((heads, total, LANES), bf),
        pltpu.VMEM((heads, total, LANES), bf),
        pltpu.VMEM((heads, total, LANES), bf),
        pltpu.VMEM((heads // 2, total, LANES), f32),
        pltpu.VMEM((heads // 2, total, LANES), f32),
        pltpu.VMEM(row, bf),
        pltpu.VMEM((heads // 2, TILE, LANES), bf),
        pltpu.VMEM((TILE, width), f32),
        pltpu.VMEM((TILE, hidden), bf),
        pltpu.VMEM((TILE, hidden), bf),
        pltpu.VMEM((blocks, span, width), bf),
        pltpu.VMEM((blocks, span, width), bf),
        pltpu.VMEM((heads, TILE, LANES), bf),
        pltpu.VMEM((heads // 2, TILE, LANES), bf),
        pltpu.VMEM((total, LANES), bf),
        pltpu.VMEM((2 * RANK, 8 * width), f32),
        *adapter_scratch(width, hidden),
        dma((4,)),
        dma((5,)),
        dma((4 + blocks,)),
        dma((3,)),
        *[dma((splits,)) for _ in range(8)],
    ]
    if not solo:
        scratch += sum_scratch(splits, copies, 8 * width)
    return pl.pallas_call(
        lambda *refs: block_kernel(splits, copies, solo, *refs),
        out_shape=[jax.ShapeDtypeStruct(s, d) for s, d in shapes],
        in_specs=[pl.BlockSpec(memory_space=pltpu.SMEM)] + [anyspace] * 6 + [vmem] * len(small),
        out_specs=[anyspace, anyspace, vmem] + [anyspace] * 6,
        scratch_shapes=scratch,
        compiler_params=pltpu.CompilerParams(
            collective_id=None if solo else 4, has_side_effects=not solo, vmem_limit_bytes=64 * 2**20 - 2**18
        ),
        name="block",
    )(lengths, inputs, cotangent, *weights, *small)[:3]


def local_by_heads(
    inputs,
    cotangent,
    lengths,
    norm_gain,
    norm_shift,
    query_key_value_weight,
    output_projection_weight,
    first_feedforward_weight,
    second_feedforward_weight,
    biases,
    down_model,
    down_hidden,
    query_key_value_upward,
    hidden_adapter_upward,
    model_adapter_upward,
    row_down_model,
    col_down_model,
    row_down_hidden,
    col_down_hidden,
    row_up_qkv,
    col_up_qkv,
    row_up_hidden,
    col_up_hidden,
    row_up_model,
    col_up_model,
):
    rows, span, width = inputs.shape
    hidden_width = first_feedforward_weight.shape[1]
    count = rows * span
    spots = lax.axis_index("seq") * span + jnp.arange(span)
    keep = (spots[None, :] < lengths[:, None]).astype(jnp.float32).reshape(count, 1)
    flat = inputs.reshape(count, width).astype(jnp.float32)
    shifts = biases.astype(jnp.float32)
    query_bias = shifts[0:width]
    value_bias = shifts[width : 2 * width]
    projection_bias = shifts[2 * width : 3 * width]
    expand_bias_vector = shifts[3 * width : 3 * width + hidden_width]
    contract_bias_vector = shifts[3 * width + hidden_width : 4 * width + hidden_width]
    query_key_value_bias = jnp.concatenate([query_bias, jnp.zeros_like(query_bias), value_bias])
    gains = norm_gain.astype(jnp.float32)
    offsets = norm_shift.astype(jnp.float32)
    down_low = down_model.astype(jnp.bfloat16)
    hidden_down_low = down_hidden.astype(jnp.bfloat16)
    qkv_up_low = query_key_value_upward.astype(jnp.bfloat16)
    hidden_up_low = hidden_adapter_upward.astype(jnp.bfloat16)
    model_up_low = model_adapter_upward.astype(jnp.bfloat16)
    normalized_rows, unit_first, scaled_first = normalize(flat, gains[0], offsets[0])
    normalized_rows = normalized_rows.astype(jnp.bfloat16)
    mixed_rows, narrow_qkv = adapted(
        normalized_rows, query_key_value_weight, query_key_value_bias, down_low[0], qkv_up_low
    )
    mixed_rows = mixed_rows.astype(jnp.bfloat16).reshape(rows, span, 3, HEADS, HEAD_DIM)
    by_head = lax.all_to_all(mixed_rows, "seq", split_axis=3, concat_axis=1, tiled=True)
    out_heads, lse = lax.map(partial(head_forward, False), (by_head, lengths))
    attended_rows = jax.tree.map(
        lambda part, own: part.astype(own.dtype),
        lax.all_to_all(as_sent(out_heads), "seq", split_axis=1, concat_axis=2, tiled=True),
        out_heads,
    )
    attended_rows = attended_rows.reshape(count, width)
    branch_path, narrow_proj = adapted(
        attended_rows, output_projection_weight, projection_bias, down_low[1], model_up_low[0]
    )
    middle = flat + branch_path
    normed_mid, unit_second, scaled_second = normalize(middle, gains[1], offsets[1])
    normed_mid = normed_mid.astype(jnp.bfloat16)
    before, narrow_expand = adapted(
        normed_mid, first_feedforward_weight, expand_bias_vector, down_low[2], hidden_up_low
    )
    activated, gelu_pull = jax.vjp(lambda value: jax.nn.gelu(value, approximate=True), before)
    activated = activated.astype(jnp.bfloat16)
    branch_out, narrow_contract = adapted(
        activated, second_feedforward_weight, contract_bias_vector, hidden_down_low, model_up_low[1]
    )
    output = (middle + branch_out).astype(jnp.bfloat16).reshape(rows, span, width)
    grad_out = cotangent.reshape(count, width).astype(jnp.float32) * keep
    grad_act, grad_down_contract, grad_up_contract = adapted_back(
        grad_out.astype(jnp.bfloat16),
        activated,
        second_feedforward_weight,
        hidden_down_low,
        model_up_low[1],
        narrow_contract,
    )
    grad_before = gelu_pull(grad_act)[0].astype(jnp.bfloat16)
    grad_norm_mid, grad_down_expand, grad_up_expand = adapted_back(
        grad_before, normed_mid, first_feedforward_weight, down_low[2], hidden_up_low, narrow_expand
    )
    grad_mid = grad_out + normalize_back(grad_norm_mid, unit_second, scaled_second, gains[1])
    grad_att, grad_down_proj, grad_up_proj = adapted_back(
        grad_mid.astype(jnp.bfloat16),
        attended_rows,
        output_projection_weight,
        down_low[1],
        model_up_low[0],
        narrow_proj,
    )
    grad_att = grad_att.astype(jnp.bfloat16).reshape(rows, span, HEADS, HEAD_DIM)
    grad_heads = lax.all_to_all(grad_att, "seq", split_axis=2, concat_axis=1, tiled=True)
    grad_triple = lax.map(partial(head_backward, False), (by_head, grad_heads, lse, lengths))
    grad_mixed = jax.tree.map(
        lambda part, own: part.astype(own.dtype),
        lax.all_to_all(as_sent(grad_triple), "seq", split_axis=1, concat_axis=3, tiled=True),
        grad_triple,
    )
    grad_mixed = grad_mixed.reshape(count, 3 * width)
    grad_normed, grad_down_qkv, grad_up_qkv = adapted_back(
        grad_mixed, normalized_rows, query_key_value_weight, down_low[0], qkv_up_low, narrow_qkv
    )
    input_grad = (
        (grad_mid + normalize_back(grad_normed, unit_first, scaled_first, gains[0]))
        .astype(jnp.bfloat16)
        .reshape(rows, span, width)
    )
    grads = lax.psum(
        (
            jnp.stack([grad_down_qkv, grad_down_proj, grad_down_expand]),
            grad_down_contract,
            grad_up_qkv,
            grad_up_expand,
            jnp.stack([grad_up_proj, grad_up_contract]),
        ),
        ("dp", "seq"),
    )
    grad_dm, grad_dh, grad_uq, grad_uh, grad_um = grads
    new_dm, row_dm, col_dm = factored(grad_dm, down_model, row_down_model, col_down_model)
    new_dh, row_dh, col_dh = factored(grad_dh, down_hidden, row_down_hidden, col_down_hidden)
    new_uq, row_uq, col_uq = factored(grad_uq, query_key_value_upward, row_up_qkv, col_up_qkv)
    new_uh, row_uh, col_uh = factored(grad_uh, hidden_adapter_upward, row_up_hidden, col_up_hidden)
    new_um, row_um, col_um = factored(grad_um, model_adapter_upward, row_up_model, col_up_model)
    return (
        output,
        input_grad,
        grad_dm,
        grad_dh,
        grad_uq,
        grad_uh,
        grad_um,
        new_dm,
        new_dh,
        new_uq,
        new_uh,
        new_um,
        row_dm,
        row_dh,
        row_uq,
        row_uh,
        row_um,
        col_dm,
        col_dh,
        col_uq,
        col_uh,
        col_um,
    )


def local_by_rows(
    pieces,
    copies,
    inputs,
    cotangent,
    lengths,
    norm_gain,
    norm_shift,
    query_key_value_weight,
    output_projection_weight,
    first_feedforward_weight,
    second_feedforward_weight,
    biases,
    down_model,
    down_hidden,
    query_key_value_upward,
    hidden_adapter_upward,
    model_adapter_upward,
    row_down_model,
    col_down_model,
    row_down_hidden,
    col_down_hidden,
    row_up_qkv,
    col_up_qkv,
    row_up_hidden,
    col_up_hidden,
    row_up_model,
    col_up_model,
):
    flip = lambda array: jnp.swapaxes(array, -1, -2)
    adapters = [
        flip(down_model),
        flip(down_hidden),
        query_key_value_upward,
        hidden_adapter_upward,
        model_adapter_upward,
    ]
    norms = [norm_gain, norm_shift]
    weights = [
        query_key_value_weight,
        output_projection_weight,
        first_feedforward_weight,
        second_feedforward_weight,
    ]
    output, input_grad, total = whole_block(
        pieces, copies, False, lengths, inputs, cotangent, [biases.reshape(1, -1)] + norms + adapters, weights
    )
    return update(
        total,
        output,
        input_grad,
        adapters,
        row_down_model,
        col_down_model,
        row_down_hidden,
        col_down_hidden,
        row_up_qkv,
        col_up_qkv,
        row_up_hidden,
        col_up_hidden,
        row_up_model,
        col_up_model,
    )


def local(pieces, copies, inputs, *others):
    if inputs.shape[0] == pieces and TILE % inputs.shape[1] == 0:
        return local_by_rows(pieces, copies, inputs, *others)
    return local_by_heads(inputs, *others)


def solution(mesh):
    placed = (
        P("dp", "seq", None),
        P("dp", "seq", None),
        P("dp"),
        P(),
        P(),
        P(),
        P(),
        P(),
        P(),
        P(),
        P(),
        P(),
        P(),
        P(),
        P(),
        P(),
        P(),
        P(),
        P(),
        P(),
        P(),
        P(),
        P(),
        P(),
        P(),
    )
    return jax.shard_map(
        partial(local, mesh.shape["seq"], mesh.shape["dp"]),
        mesh=mesh,
        in_specs=placed,
        out_specs=(
            P("dp", "seq", None),
            P("dp", "seq", None),
            P(),
            P(),
            P(),
            P(),
            P(),
            P(),
            P(),
            P(),
            P(),
            P(),
            P(),
            P(),
            P(),
            P(),
            P(),
            P(),
            P(),
            P(),
            P(),
            P(),
        ),
        check_vma=False,
    )
```

```python
from functools import partial

import jax
import jax.numpy as jnp
from jax import lax
from jax.experimental import pallas as pl
from jax.experimental.pallas import tpu as pltpu
from jax.sharding import PartitionSpec as P


HEADS = 16
HEAD_DIM = 64
STEP = 10


NORM_EPS = 1e-05
ADAPTER_SCALE = 8.0
STAT_EPS = 1e-30
CLIP_LEVEL = 1.0
RATE = 0.3
DECAY_WEIGHT = 0.01
MASKED = -1e30


def as_sent(array):

    def short(part):
        return part.astype(jnp.bfloat16) if part.dtype == jnp.float32 else part

    return jax.tree.map(short, array)


def normalize(values, gain, shift):
    centered = values - jnp.mean(values, axis=-1, keepdims=True)
    spread = jnp.mean(centered * centered, axis=-1, keepdims=True)
    scaled = lax.rsqrt(spread + NORM_EPS)
    unit = centered * scaled
    return (unit * gain + shift, unit, scaled)


def normalize_back(grad, unit, scaled, gain):
    gained = grad * gain
    return scaled * (
        gained
        - jnp.mean(gained, axis=-1, keepdims=True)
        - unit * jnp.mean(gained * unit, axis=-1, keepdims=True)
    )


def matrix_multiply(left, right):
    return jnp.dot(left, right, preferred_element_type=jnp.float32)


def inner_product(left, right):
    return jnp.einsum("tr,tc->rc", left, right, preferred_element_type=jnp.float32)


def compared_with(left, right):
    return jnp.einsum("tc,rc->tr", left, right, preferred_element_type=jnp.float32)


def adapted(source_rows, weight_matrix, bias_vector, down, upward_matrix):
    narrowed_rows = matrix_multiply(source_rows, down).astype(jnp.bfloat16)
    return (
        matrix_multiply(source_rows, weight_matrix)
        + bias_vector
        + ADAPTER_SCALE * matrix_multiply(narrowed_rows, upward_matrix),
        narrowed_rows,
    )


def adapted_back(gradient_lowrank, source_rows, weight_matrix, down, upward_matrix, narrowed_rows):
    gradient_upward = ADAPTER_SCALE * inner_product(narrowed_rows, gradient_lowrank)
    gradient_narrowed = (ADAPTER_SCALE * compared_with(gradient_lowrank, upward_matrix)).astype(
        jnp.bfloat16
    )
    grad_down = inner_product(source_rows, gradient_narrowed)
    grad_source = compared_with(gradient_lowrank, weight_matrix) + compared_with(
        gradient_narrowed, down
    )
    return (grad_source, grad_down, gradient_upward)


def score_block(operand):
    query, keys = operand
    return jnp.einsum("gqe,gke->gqk", query, keys, preferred_element_type=jnp.float32)


def mix_block(operand):
    weights, values = operand
    return jnp.einsum("gqk,gke->gqe", weights, values, preferred_element_type=jnp.float32)


def spread_block(operand):
    weights, queries = operand
    return jnp.einsum("gqk,gqe->gke", weights, queries, preferred_element_type=jnp.float32)


def masked_scores(query, keys, spots, length):
    total = keys.shape[1]
    size = min(512, total)
    reach = jnp.minimum(length, jnp.max(spots) + 1)
    places = jnp.arange(total)
    valid = (places[None, :] <= spots[:, None]) & (places[None, :] < length)
    pieces = []
    for begin in range(0, total, size):
        pieces.append(score_block((query, keys[:, begin : begin + size])))
    scores = jnp.concatenate(pieces, axis=-1) * query.shape[-1] ** (-0.5)
    return (jnp.where(valid[None], scores, MASKED), reach, size)


def attend(query, keys, values, spots, length):
    scores, reach, size = masked_scores(query, keys, spots, length)
    top = jnp.max(scores, axis=-1, keepdims=True)
    weights = jnp.exp(scores - top)
    summed = jnp.sum(weights, axis=-1, keepdims=True)
    probs = (weights / summed).astype(jnp.bfloat16)
    result = jnp.zeros(query.shape, jnp.float32)
    for begin in range(0, keys.shape[1], size):
        operand = (probs[:, :, begin : begin + size], values[:, begin : begin + size])
        result = result + mix_block(operand)
    return (result, (top + jnp.log(summed))[..., 0])


def attend_back(query, keys, values, spots, length, grad_rows, lse):
    scores, reach, size = masked_scores(query, keys, spots, length)
    probs = jnp.exp(scores - lse[..., None])
    pieces = []
    for begin in range(0, keys.shape[1], size):
        pieces.append(score_block((grad_rows, values[:, begin : begin + size])))
    dprob = jnp.concatenate(pieces, axis=-1)
    delta = jnp.sum(probs * dprob, axis=-1, keepdims=True)
    dscore = (probs * (dprob - delta)).astype(jnp.bfloat16)
    probs_low = probs.astype(jnp.bfloat16)
    scale = query.shape[-1] ** (-0.5)
    grad_query = jnp.zeros(query.shape, jnp.float32)
    key_parts = []
    value_parts = []
    for begin in range(0, keys.shape[1], size):
        grad_query = grad_query + mix_block(
            (dscore[:, :, begin : begin + size], keys[:, begin : begin + size])
        )
        key_parts.append(spread_block((dscore[:, :, begin : begin + size], query)))
        value_parts.append(spread_block((probs_low[:, :, begin : begin + size], grad_rows)))
    return (
        grad_query * scale,
        jnp.concatenate(key_parts, axis=1) * scale,
        jnp.concatenate(value_parts, axis=1),
    )


def heads_split(triple):
    return tuple((jnp.transpose(triple[:, index], (1, 0, 2)) for index in range(3)))


def head_forward(skip, item):
    triple, length = item
    spots = jnp.arange(triple.shape[0])
    query, keys, values = heads_split(triple)
    result, lse = attend(query, keys, values, spots, length)
    return (jnp.transpose(result, (1, 0, 2)).astype(jnp.bfloat16), lse)


def head_backward(skip, item):
    triple, grad_rows, lse, length = item
    spots = jnp.arange(triple.shape[0])
    query, keys, values = heads_split(triple)
    grads = attend_back(
        query, keys, values, spots, length, jnp.transpose(grad_rows, (1, 0, 2)), lse
    )
    return jnp.stack(grads, axis=0).transpose(2, 0, 1, 3).astype(jnp.bfloat16)


def factored(grad, weight_matrix, row, col):
    decay = 1.0 - STEP ** (-0.8)
    squares = grad * grad + STAT_EPS
    new_row = decay * row + (1.0 - decay) * jnp.mean(squares, axis=-1)
    new_col = decay * col + (1.0 - decay) * jnp.mean(squares, axis=-2)
    second = (
        new_row[..., :, None] * new_col[..., None, :] / jnp.mean(new_row, axis=-1)[..., None, None]
    )
    unit = grad * lax.rsqrt(second)
    level = jnp.sqrt(jnp.mean(unit * unit, axis=(-2, -1), keepdims=True))
    unit = unit / jnp.maximum(1.0, level / CLIP_LEVEL)
    rate = RATE * jnp.sqrt(jnp.mean(weight_matrix * weight_matrix, axis=(-2, -1), keepdims=True))
    return (weight_matrix - rate * (unit + DECAY_WEIGHT * weight_matrix), new_row, new_col)


LOG2E = 1.4426950408889634
NT = (((1,), (1,)), ((), ()))
TN = (((0,), (0,)), ((), ()))


def dotf(a, b, dims=(((1,), (0,)), ((), ()))):
    return lax.dot_general(a, b, dims, preferred_element_type=jnp.float32)


def triple(value):
    high = value.astype(jnp.bfloat16)
    rest = value - high.astype(jnp.float32)
    mid = rest.astype(jnp.bfloat16)
    low = (rest - mid.astype(jnp.float32)).astype(jnp.bfloat16)
    return high, mid, low


GELU_A = 0.7978845608028654
GELU_B = 0.7978845608028654 * 0.044715
RANK = 4


def norm_parts(values):
    centered = values - jnp.mean(values, axis=-1, keepdims=True)
    spread = jnp.mean(centered * centered, axis=-1, keepdims=True)
    scaled = lax.rsqrt(spread + NORM_EPS)
    return centered * scaled, scaled


def norm_back(grad, unit, scaled, gain):
    gained = grad * gain
    return scaled * (
        gained
        - jnp.mean(gained, axis=-1, keepdims=True)
        - unit * jnp.mean(gained * unit, axis=-1, keepdims=True)
    )


def low(value):
    return value.astype(jnp.bfloat16)


def wide(value):
    return value.astype(jnp.float32)


def gelu_pair(value):
    square = value * value
    half = 0.5 * value
    bent = jnp.tanh(value * (GELU_A + GELU_B * square))
    slope = (0.5 + 0.5 * bent) + half * (1.0 - bent * bent) * (GELU_A + 3.0 * GELU_B * square)
    return half + half * bent, slope


def peers_of(axis, size):
    me = lax.axis_index(axis)
    return me, [lax.rem(me + shift, size) for shift in range(1, size)]


def greet(axes):
    barrier = pltpu.get_barrier_semaphore()
    count = 0
    for axis, size in axes:
        _, peers = peers_of(axis, size)
        for peer in peers:
            pl.semaphore_signal(
                barrier, inc=1, device_id={axis: peer}, device_id_type=pl.DeviceIdType.MESH
            )
        count += len(peers)
    pl.semaphore_wait(barrier, count)


def send(source, target, sent, landed, axis, peer):
    return pltpu.make_async_remote_copy(
        src_ref=source,
        dst_ref=target,
        send_sem=sent,
        recv_sem=landed,
        device_id={axis: peer},
        device_id_type=pl.DeviceIdType.MESH,
    )


def sum_everywhere(
    splits, copies, part_ref, total_ref, dp_in, seq_in, own, piece, d_sent, d_land, s_sent, s_land, g_sent, g_land, e_sent, e_land
):
    size = part_ref.shape[1] // copies
    small = size // splits
    me, peers = peers_of("seq", splits)
    mine, others = peers_of("dp", copies)

    def columns(index):
        return pl.ds(pl.multiple_of(index * size, size), size)

    def narrow_columns(index, start=0):
        return pl.ds(pl.multiple_of(start + index * small, small), small)

    sent = []

    def start(copy):
        copy.start()
        sent.append(copy)

    for shift, peer in enumerate(others):
        start(send(part_ref.at[:, columns(peer)], dp_in.at[mine], d_sent.at[shift], d_land.at[mine], "dp", peer))
    dp_in[mine] = part_ref[:, columns(mine)]
    for peer in others:
        send(part_ref.at[:, columns(mine)], dp_in.at[peer], d_sent.at[0], d_land.at[peer], "dp", peer).wait_recv()
    summed = dp_in[0]
    for index in range(1, copies):
        summed = summed + dp_in[index]
    own[...] = summed
    for shift, peer in enumerate(peers):
        start(send(own.at[:, narrow_columns(peer)], seq_in.at[me], s_sent.at[shift], s_land.at[me], "seq", peer))
    seq_in[me] = own[:, narrow_columns(me)]
    for peer in peers:
        send(own.at[:, narrow_columns(me)], seq_in.at[peer], s_sent.at[0], s_land.at[peer], "seq", peer).wait_recv()
    summed = seq_in[0]
    for index in range(1, splits):
        summed = summed + seq_in[index]
    piece[...] = summed
    base = mine * size
    total_ref[:, narrow_columns(me, base)] = summed
    for shift, peer in enumerate(peers):
        start(send(piece, total_ref.at[:, narrow_columns(me, base)], g_sent.at[shift], g_land.at[me], "seq", peer))
    for peer in peers:
        send(piece, total_ref.at[:, narrow_columns(peer, base)], g_sent.at[0], g_land.at[peer], "seq", peer).wait_recv()
    for shift, peer in enumerate(others):
        part = total_ref.at[:, columns(mine)]
        start(send(part, part, e_sent.at[shift], e_land.at[mine], "dp", peer))
    for peer in others:
        part = total_ref.at[:, columns(peer)]
        send(part, part, e_sent.at[0], e_land.at[peer], "dp", peer).wait_recv()
    for copy in sent:
        copy.wait_send()


def sum_scratch(splits, copies, width):
    size = width // copies
    small = size // splits
    dma = pltpu.SemaphoreType.DMA
    return [
        pltpu.VMEM((copies, 8, size), jnp.float32),
        pltpu.VMEM((splits, 8, small), jnp.float32),
        pltpu.VMEM((8, size), jnp.float32),
        pltpu.VMEM((8, small), jnp.float32),
        dma((copies,)),
        dma((copies,)),
        dma((splits,)),
        dma((splits,)),
        dma((splits,)),
        dma((splits,)),
        dma((copies,)),
        dma((copies,)),
    ]


def across(column):
    count = column.shape[0]
    diagonal = lax.broadcasted_iota(jnp.int32, (count, count), 0) == lax.broadcasted_iota(
        jnp.int32, (count, count), 1
    )
    return jnp.sum(jnp.where(diagonal, jnp.broadcast_to(column, (count, count)), 0.0), axis=0, keepdims=True)


def upright(line):
    count = line.shape[1]
    diagonal = lax.broadcasted_iota(jnp.int32, (count, count), 0) == lax.broadcasted_iota(
        jnp.int32, (count, count), 1
    )
    return jnp.sum(jnp.where(diagonal, jnp.broadcast_to(line, (count, count)), 0.0), axis=1, keepdims=True)


def factored_step(grad, weight, short_line, long_line, rows_long):
    decay = 1.0 - STEP ** (-0.8)
    squares = grad * grad + STAT_EPS
    new_short = decay * upright(short_line) + (1.0 - decay) * jnp.mean(squares, axis=1, keepdims=True)
    new_long = decay * long_line + (1.0 - decay) * jnp.mean(squares, axis=0, keepdims=True)
    if rows_long:
        middle = jnp.mean(new_long, axis=1, keepdims=True)
    else:
        middle = jnp.mean(new_short, axis=0, keepdims=True)
    unit = grad * lax.rsqrt(new_short * new_long / middle)
    entries = grad.shape[0] * grad.shape[1]

    def mean_square(value):
        return jnp.sum(jnp.sum(value * value, axis=1, keepdims=True), axis=0, keepdims=True) / entries

    level = jnp.sqrt(mean_square(unit))
    unit = unit / jnp.maximum(1.0, level / CLIP_LEVEL)
    rate = RATE * jnp.sqrt(mean_square(weight))
    return weight - rate * (unit + DECAY_WEIGHT * weight), across(new_short), new_long


def update_kernel(
    total_ref, output_in, grad_in, dm, dh, uq, uh, um, row_dm, col_dm, row_dh, col_dh, row_uq, col_uq, row_uh, col_uh, row_um, col_um,
    output_out, grad_out, g_dm, g_dh, g_uq, g_uh, g_um, n_dm, n_dh, n_uq, n_uh, n_um,
    r_dm, r_dh, r_uq, r_uh, r_um, c_dm, c_dh, c_uq, c_uh, c_um, held_out, held_grad, sems,
):
    moves = [
        pltpu.make_async_copy(output_in, held_out, sems.at[0]),
        pltpu.make_async_copy(grad_in, held_grad, sems.at[1]),
    ]
    for move in moves:
        move.start()
    moves = [
        (moves[0], pltpu.make_async_copy(held_out, output_out, sems.at[0])),
        (moves[1], pltpu.make_async_copy(held_grad, grad_out, sems.at[1])),
    ]
    for move, onward in moves:
        move.wait()
        onward.start()
    width = dm.shape[2]
    hidden = dh.shape[1]
    for index in range(3):
        grad = total_ref[0:RANK, index * width : (index + 1) * width]
        g_dm[index] = grad
        n_dm[index], c_dm[index : index + 1, :], r_dm[index : index + 1, :] = factored_step(
            grad, dm[index], col_dm[index : index + 1, :], row_dm[index : index + 1, :], True
        )
    grad = total_ref[0:RANK, 3 * width : 6 * width]
    g_uq[...] = grad
    n_uq[...], r_uq[...], c_uq[...] = factored_step(grad, uq[...], row_uq[...], col_uq[...], False)
    for index in range(2):
        grad = total_ref[0:RANK, (6 + index) * width : (7 + index) * width]
        g_um[index] = grad
        n_um[index], r_um[index : index + 1, :], c_um[index : index + 1, :] = factored_step(
            grad, um[index], row_um[index : index + 1, :], col_um[index : index + 1, :], False
        )
    grad = total_ref[RANK : 2 * RANK, 0:hidden]
    g_dh[...] = grad
    n_dh[...], c_dh[...], r_dh[...] = factored_step(grad, dh[...], col_dh[...], row_dh[...], True)
    grad = total_ref[RANK : 2 * RANK, hidden : 2 * hidden]
    g_uh[...] = grad
    n_uh[...], r_uh[...], c_uh[...] = factored_step(grad, uh[...], row_uh[...], col_uh[...], False)
    for _, onward in moves:
        onward.wait()


def update(total, output, input_grad, adapters, row_dm, col_dm, row_dh, col_dh, row_uq, col_uq, row_uh, col_uh, row_um, col_um):
    flip = lambda array: jnp.swapaxes(array, -1, -2)
    line = lambda array: array.reshape(1, -1)
    given = [
        row_dm, col_dm, line(row_dh), line(col_dh), line(row_uq), line(col_uq), line(row_uh), line(col_uh), row_um, col_um,
    ]
    stats = given[0::2] + given[1::2]
    anyspace = pl.BlockSpec(memory_space=pl.ANY)
    vmem = pl.BlockSpec(memory_space=pltpu.VMEM)
    results = pl.pallas_call(
        update_kernel,
        out_shape=[jax.ShapeDtypeStruct(a.shape, a.dtype) for a in [output, input_grad] + adapters + adapters + stats],
        in_specs=[vmem, anyspace, anyspace] + [vmem] * 15,
        out_specs=[anyspace, anyspace] + [vmem] * 20,
        scratch_shapes=[
            pltpu.VMEM(output.shape, output.dtype),
            pltpu.VMEM(output.shape, output.dtype),
            pltpu.SemaphoreType.DMA((2,)),
        ],
        compiler_params=pltpu.CompilerParams(vmem_limit_bytes=60 * 2**20),
        name="factored_update",
    )(total, output, input_grad, *adapters, *given)
    results = list(results)
    for index in (2, 3, 7, 8):
        results[index] = flip(results[index])
    olds = (row_dm, row_dh, row_uq, row_uh, row_um, col_dm, col_dh, col_uq, col_uh, col_um)
    for index, old in zip(range(12, 22), olds):
        results[index] = results[index].reshape(old.shape)
    return tuple(results)


def fill_adapters(dm_ref, dh_ref, uq_ref, uh_ref, um_ref, aq, ap, a1, a2, bq, bp, b2, b1):
    for index, ref in enumerate((aq, ap, a1)):
        ref[...] = low(dm_ref[index])
    a2[...] = low(dh_ref[...])
    for ref, value in ((bq, uq_ref[...]), (bp, um_ref[0]), (b2, um_ref[1]), (b1, uh_ref[...])):
        ref[...] = low(ADAPTER_SCALE * wide(low(value)))


def adapter_scratch(width, hidden):
    sizes = [width, width, width, hidden, 3 * width, width, width, hidden]
    return [pltpu.VMEM((RANK, size), jnp.bfloat16) for size in sizes]


TILE = 256
GROUP = 4
LANES = 128


def peer_order(me, splits):
    half = splits // 2
    side, place = me // half, lax.rem(me, half)
    far = [(1 - side) * half + lax.rem(place + shift, half) for shift in range(half)]
    near = [side * half + lax.rem(place + shift, half) for shift in range(1, half)]
    return far, near


def block_kernel(
    splits, copies, solo,
    lengths_ref, inputs, cotangent, wqkv_hbm, wo_hbm, w1_hbm, w2_hbm,
    bias_ref, gain_ref, shift_ref, dm_ref, dh_ref, uq_ref, uh_ref, um_ref,
    output, dx_out, total_ref, cot_in, out_row, att_hbm, mid_hbm, act_hbm, slope_hbm,
    wqkv, wo, w1, w2, kx, vx, qx, dk, dv, xr, att, mid, act, slope, cot_t, outs, gx, dq, narrow, part,
    aq, ap, a1, a2, bq, bp, b2, b1,
    w_sem, s_sem, l_sem, own_sem, x_sent, x_land, c_sent, c_land, f_sent, f_land, b_sent, b_land,
    *sum_refs,
):
    me = 0 if solo else lax.axis_index("seq")
    span, width = xr.shape[1], xr.shape[2]
    hidden = w1.shape[1]
    total = splits * span
    tiles = total // TILE
    blocks = TILE // span
    heads = kx.shape[0]
    pairs = heads // 2
    half = LANES // 2
    length = lengths_ref[me]
    upper = me >= splits // 2

    loads = [
        pltpu.make_async_copy(source, target, w_sem.at[index])
        for index, (source, target) in enumerate(((wqkv_hbm, wqkv), (wo_hbm, wo), (w1_hbm, w1), (w2_hbm, w2)))
    ]
    own_x = pltpu.make_async_copy(inputs if solo else inputs.at[me], xr if solo else xr.at[me], own_sem.at[0])
    own_b = pltpu.make_async_copy(xr.at[me], dx_out.at[me], own_sem.at[1])

    own_f = pltpu.make_async_copy(out_row.at[me], output.at[me], own_sem.at[2])

    def saves(tile):
        rows = pl.ds(tile * TILE, TILE)
        moves = (
            (att, att_hbm.at[:, rows, :]),
            (mid, mid_hbm.at[rows, :]),
            (act, act_hbm.at[rows, :]),
            (slope, slope_hbm.at[rows, :]),
            (outs, out_row.at[pl.ds(tile * blocks, blocks)]),
        )
        return [pltpu.make_async_copy(a, b, s_sem.at[i]) for i, (a, b) in enumerate(moves)]

    def fetches(tile):
        rows = pl.ds(tile * TILE, TILE)
        moves = (
            (slope_hbm.at[rows, :], slope),
            (act_hbm.at[rows, :], act),
            (att_hbm.at[:, rows, :], att),
            (mid_hbm.at[rows, :], mid),
        )
        return [pltpu.make_async_copy(a, b, l_sem.at[i]) for i, (a, b) in enumerate(moves)]

    def x_copy(peer, slot):
        return send(inputs.at[peer], xr.at[me], x_sent.at[slot], x_land.at[me], "seq", peer)

    def c_copy(peer, slot):
        return send(cotangent.at[peer], cot_in.at[me], c_sent.at[slot], c_land.at[me], "seq", peer)

    def f_copy(block):
        return send(out_row.at[block], output.at[me], f_sent.at[block], f_land.at[me], "seq", block)

    def b_copy(block):
        return send(xr.at[block], dx_out.at[me], b_sent.at[block], b_land.at[me], "seq", block)

    def tile_blocks(tile):
        return range(tile * blocks, (tile + 1) * blocks)

    def cot_move(block, fetched):
        slot = cot_t.at[block % blocks]
        source = cotangent.at[me] if fetched else cot_in.at[block]
        return pltpu.make_async_copy(source, slot, l_sem.at[4 + block % blocks])

    def cot_fetch(tile):
        if solo:
            for block in tile_blocks(tile):
                cot_move(block, False).start()
            return
        for block in tile_blocks(tile):

            @pl.when(me == block)
            def _():
                cot_move(block, True).start()

            @pl.when(me != block)
            def _():
                send(cotangent.at[block], cot_in.at[block], c_sent.at[0], c_land.at[block], "seq", block).wait_recv()
                cot_move(block, False).start()

    def x_wait(tile):
        if solo:
            return
        for block in tile_blocks(tile):

            @pl.when(me != block)
            def _():
                send(inputs.at[block], xr.at[block], x_sent.at[0], x_land.at[block], "seq", block).wait_recv()

    def send_output(tile):
        if solo:
            return
        for block in tile_blocks(tile):

            @pl.when(me != block)
            def _():
                f_copy(block).start()

    if not solo:
        greet((("seq", splits), ("dp", copies)))
    own_x.start()
    loads[0].start()
    if not solo:
        far, near = peer_order(me, splits)
        early = lax.rem(me, splits // 2) < splits // 4
        lower_early = jnp.logical_and(early, jnp.logical_not(upper))
        lower_late = jnp.logical_and(jnp.logical_not(early), jnp.logical_not(upper))
        ways = list(enumerate(far + near))

        @pl.when(jnp.logical_not(lower_early))
        def _():
            for slot, peer in ways[len(far) :]:
                x_copy(peer, slot).start()

        @pl.when(jnp.logical_not(lower_late))
        def _():
            for slot, peer in ways[: len(far)]:
                x_copy(peer, slot).start()

    for load in loads[1:]:
        load.start()
    fill_adapters(dm_ref, dh_ref, uq_ref, uh_ref, um_ref, aq, ap, a1, a2, bq, bp, b2, b1)
    part[...] = jnp.zeros_like(part)

    lane = lax.broadcasted_iota(jnp.int32, (TILE, LANES), 1)
    row = lax.broadcasted_iota(jnp.int32, (TILE, TILE), 0)
    col = lax.broadcasted_iota(jnp.int32, (TILE, TILE), 1)
    zero = jnp.zeros((TILE, LANES), jnp.bfloat16)
    one = jnp.ones((TILE, LANES), jnp.bfloat16)
    scale = half ** (-0.5)
    owns = (lane < half, lane >= half)
    spares = (half, 0)

    def absorb(weight, down, up):
        rows, columns = weight.shape
        size = 1024

        def step(index, carry):
            span_rows = pl.ds(pl.multiple_of(index * TILE, TILE), TILE)
            left = down[:, span_rows]
            for start in range(0, columns, size):
                part_ref = weight.at[span_rows, pl.ds(start, size)]
                part_ref[...] = low(wide(part_ref[...]) + dotf(left, up[:, start : start + size], TN))
            return carry

        lax.fori_loop(0, rows // TILE, step, 0)

    def with_extra(own, spare, value, extra):
        high, middle, rest = triple(extra)
        return jnp.where(
            own,
            value,
            jnp.where(lane == spare, high, jnp.where(lane == spare + 1, middle, jnp.where(lane == spare + 2, rest, zero))),
        )

    def bias(start, size):
        return wide(bias_ref[0:1, start : start + size])

    def rows_of(tile):
        if isinstance(tile, int):
            return pl.ds(tile * TILE, TILE)
        return pl.ds(pl.multiple_of(tile * TILE, TILE), TILE)

    def project(tile):
        rows = rows_of(tile)
        x = wide(xr[pl.ds(tile * blocks, blocks)].reshape(TILE, width))
        unit, _ = norm_parts(x)
        normed = low(unit * wide(gain_ref[0:1, :]) + wide(shift_ref[0:1, :]))
        narrow_q = low(dotf(normed, aq[...], NT))
        narrow[rows, 0:RANK] = narrow_q
        spot = tile * TILE + lax.broadcasted_iota(jnp.int32, (TILE, LANES), 0)
        limit = jnp.where(spot < length, 0.0, MASKED).astype(jnp.bfloat16)
        size = 512
        for index in range(3):
            for start in range(0, width, size):
                column = index * width + start
                value = dotf(normed, wqkv[:, column : column + size]) + dotf(narrow_q, bq[:, column : column + size])
                if index == 0:
                    value = value + bias(start, size)
                if index == 2:
                    value = value + bias(width + start, size)
                value = low(value)
                for pair in range(size // LANES):
                    piece = value[:, pair * LANES : (pair + 1) * LANES]
                    for parity in range(2):
                        head = 2 * (start // LANES + pair) + parity
                        own, spare = owns[parity], spares[parity]
                        if index == 0:
                            extra = jnp.where(lane == spare + 3, one, zero)
                            qx[head, rows, :] = jnp.where(own, piece * jnp.asarray(scale, jnp.bfloat16), extra)
                        elif index == 1:
                            extra = jnp.where(lane == spare + 3, limit, jnp.where(lane < spare + 3, one, zero))
                            kx[head, rows, :] = jnp.where(own, piece, extra)
                        else:
                            vx[head, rows, :] = jnp.where(own, piece, one)

    own_x.wait()
    loads[0].wait()
    loads[1].wait()
    absorb(wo, ap, bp)
    if not solo:

        @pl.when(lower_early)
        def _():
            for slot, peer in ways[len(far) :]:
                x_copy(peer, slot).start()

    loads[2].wait()
    absorb(w1, a1, b1)
    if not solo:

        @pl.when(lower_late)
        def _():
            for slot, peer in ways[: len(far)]:
                x_copy(peer, slot).start()

    loads[3].wait()
    absorb(w2, a2, b2)
    if not solo:

        @pl.when(upper)
        def _():
            for tile in range(tiles // 2, tiles):
                x_wait(tile)
            lax.fori_loop(tiles // 2, tiles, lambda tile, carry: (project(tile), carry)[1], 0)

    for tile in range(tiles):
        begin, end = tile * TILE, (tile + 1) * TILE
        if tile < tiles // 2:
            x_wait(tile)
            project(tile)
        elif solo:
            project(tile)
        else:

            @pl.when(jnp.logical_not(upper))
            def _():
                x_wait(tile)
                project(tile)

        if not solo:
            last_tile = jnp.logical_and(upper, jnp.logical_not(early))
            ready = last_tile if tile == tiles // 2 - 1 else jnp.logical_not(last_tile)
            if tile == tiles // 2 - 1 or tile == tiles // 2:

                @pl.when(ready)
                def _():
                    for slot, peer in enumerate(far + near):
                        c_copy(peer, slot).start()

        if tile:
            saves(tile - 1)[0].wait()
        valid = begin + lax.broadcasted_iota(jnp.int32, (TILE, LANES), 0) < length
        causal = col <= row

        def attend(index, carry):
            def scores(unit):
                head = index * GROUP + unit
                return dotf(qx[head, begin:end, :], kx[head, 0:end, :], NT)

            def mix(unit, value):
                head = index * GROUP + unit
                last = jnp.where(causal, value[:, begin:], MASKED)
                value = jnp.concatenate([value[:, :begin], last], axis=1) if begin else last
                top = jnp.max(value, axis=-1, keepdims=True)
                weights = low(jnp.exp2((value - top) * LOG2E))
                mixed = dotf(weights, vx[head, 0:end, :])
                spare, own = spares[unit % 2], owns[unit % 2]
                summed = mixed[:, spare : spare + 1]
                back = jnp.where(valid, -(top + jnp.log(summed)), MASKED)
                qx[head, begin:end, :] = with_extra(own, spare, qx[head, begin:end, :], back)
                return mixed * (1.0 / summed)

            ahead = scores(0)
            results = []
            for unit in range(GROUP):
                value = ahead
                if unit + 1 < GROUP:
                    ahead = scores(unit + 1)
                results.append(mix(unit, value))
            for unit in range(0, GROUP, 2):
                att[index * (GROUP // 2) + unit // 2] = low(jnp.where(owns[0], results[unit], results[unit + 1]))
            return carry

        lax.fori_loop(0, heads // GROUP, attend, 0)
        if tile:
            for save in saves(tile - 1)[1:]:
                save.wait()
        attended = jnp.concatenate([att[index] for index in range(pairs)], axis=1)
        narrow_p = low(dotf(attended, ap[...], NT))
        middle = (
            wide(xr[tile * blocks : (tile + 1) * blocks].reshape(TILE, width))
            + dotf(attended, wo[...])
            + bias(2 * width, width)
        )
        mid[...] = middle
        unit, _ = norm_parts(middle)
        normed = low(unit * wide(gain_ref[1:2, :]) + wide(shift_ref[1:2, :]))
        narrow_1 = low(dotf(normed, a1[...], NT))
        size = 256

        def expand(start):
            return dotf(normed, w1[:, start : start + size]) + bias(3 * width + start, size)

        result = middle + bias(3 * width + hidden, width)
        narrow_2 = jnp.zeros((TILE, RANK), jnp.float32)
        ahead = expand(0)
        for start in range(0, hidden, size):
            stop = start + size
            before = ahead
            if stop < hidden:
                ahead = expand(stop)
            active, bend = gelu_pair(before)
            active = low(active)
            act[:, start:stop] = active
            slope[:, start:stop] = low(bend)
            result = result + dotf(active, w2[start:stop, :])
            narrow_2 = narrow_2 + dotf(active, a2[:, start:stop], NT)
        narrow_2 = low(narrow_2)
        outs[...] = low(result).reshape(blocks, span, width)
        narrow[begin:end, RANK : 2 * RANK] = narrow_p
        narrow[begin:end, 2 * RANK : 3 * RANK] = narrow_1
        narrow[begin:end, 3 * RANK : 4 * RANK] = narrow_2
        if tile < tiles - 1:
            for save in saves(tile):
                save.start()
        else:
            saves(tile)[4].start()

    def add_upper(start, value):
        part[0:RANK, start : start + value.shape[1]] += value

    def add_lower(start, value):
        part[RANK : 2 * RANK, start : start + value.shape[1]] += value

    cot_fetch(tiles - 1)
    for tile in reversed(range(tiles)):
        begin, end = tile * TILE, (tile + 1) * TILE
        newest = tile == tiles - 1
        if newest:
            pass
        else:
            for fetch in fetches(tile)[0:3]:
                fetch.wait()
        for block in tile_blocks(tile):
            cot_move(block, False).wait()
        spot = begin + lax.broadcasted_iota(jnp.int32, (TILE, width), 0)
        given = cot_t[...].reshape(TILE, width)
        gout = jnp.where(spot < length, given, jnp.zeros_like(given))
        narrow_q = narrow[begin:end, 0:RANK]
        narrow_p = narrow[begin:end, RANK : 2 * RANK]
        narrow_1 = narrow[begin:end, 2 * RANK : 3 * RANK]
        narrow_2 = narrow[begin:end, 3 * RANK : 4 * RANK]
        gn2 = low(dotf(gout, b2[...], NT))
        add_upper(7 * width, dotf(narrow_2, gout, TN))
        size = 512

        def contract(start):
            return dotf(gout, w2[start : start + size, :], NT)

        gnorm = jnp.zeros((TILE, width), jnp.float32)
        gn1 = jnp.zeros((TILE, RANK), jnp.float32)
        ahead = contract(0)
        for start in range(0, hidden, size):
            stop = start + size
            gact = ahead
            if stop < hidden:
                ahead = contract(stop)
            gbefore = low(gact * wide(slope[:, start:stop]))
            add_lower(start, dotf(gn2, act[:, start:stop], TN))
            add_lower(hidden + start, dotf(narrow_1, gbefore, TN))
            gn1 = gn1 + dotf(gbefore, b1[:, start:stop], NT)
            gnorm = gnorm + dotf(gbefore, w1[:, start:stop], NT)
        gn1 = low(gn1)
        if not newest:
            fetches(tile)[3].wait()
        unit, scaled = norm_parts(mid[...])
        normed = low(unit * wide(gain_ref[1:2, :]) + wide(shift_ref[1:2, :]))
        add_upper(2 * width, dotf(gn1, normed, TN))
        grad = wide(gout) + norm_back(gnorm, unit, scaled, wide(gain_ref[1:2, :]))
        mid[...] = grad
        glow = low(grad)
        gnp = low(dotf(glow, bp[...], NT))
        add_upper(6 * width, dotf(narrow_p, glow, TN))
        gatt = low(dotf(glow, wo[...], NT))
        attended = jnp.concatenate([att[index] for index in range(pairs)], axis=1)
        add_upper(width, dotf(gnp, attended, TN))
        for index in range(pairs):
            piece = gatt[:, index * LANES : (index + 1) * LANES]
            product = wide(piece) * wide(att[index])
            for parity in range(2):
                own, spare = owns[parity], spares[parity]
                delta = -jnp.sum(jnp.where(own, product, 0.0), axis=-1, keepdims=True)
                gx[2 * index + parity] = with_extra(own, spare, piece, jnp.broadcast_to(delta, (TILE, LANES)))
        if tile:
            for fetch in fetches(tile - 1)[0:3]:
                fetch.start()
            cot_fetch(tile - 1)
        if newest:
            saves(tile)[4].wait()
            for done in range(tiles):
                send_output(done)
            if not solo:
                own_f.start()
        causal = row <= col

        def attend_back(index, carry):
            def products(unit):
                head = index * GROUP + unit
                return (
                    dotf(kx[head, 0:end, :], qx[head, begin:end, :], NT),
                    dotf(vx[head, 0:end, :], gx[head], NT),
                )

            def spread(unit, scores, dprob):
                head = index * GROUP + unit
                weights = jnp.exp2(scores * LOG2E)
                last = jnp.where(causal, weights[begin:], 0.0)
                weights = jnp.concatenate([weights[:begin], last], axis=0) if begin else last
                dscore = low(weights * dprob)
                return (
                    dotf(dscore, kx[head, 0:end, :], TN),
                    dotf(dscore, qx[head, begin:end, :]),
                    dotf(low(weights), gx[head]),
                )

            ahead = products(0)
            results = []
            for unit in range(GROUP):
                given = ahead
                if unit + 1 < GROUP:
                    ahead = products(unit + 1)
                results.append(spread(unit, *given))
            first_lanes = lax.broadcasted_iota(jnp.int32, (end, LANES), 1) < half
            for unit in range(0, GROUP, 2):
                pair = index * (GROUP // 2) + unit // 2
                even, odd = results[unit], results[unit + 1]
                dq[pair] = low(jnp.where(owns[0], even[0], odd[0]) * scale)
                more_k = jnp.where(first_lanes, even[1], odd[1])
                more_v = jnp.where(first_lanes, even[2], odd[2])
                if newest:
                    dk[pair] = more_k
                    dv[pair] = more_v
                else:
                    dk[pair, 0:end, :] += more_k
                    dv[pair, 0:end, :] += more_v
            return carry

        lax.fori_loop(0, heads // GROUP, attend_back, 0)
        values = [
            jnp.concatenate([dq[index] for index in range(pairs)], axis=1),
            jnp.concatenate([low(dk[index, begin:end, :]) for index in range(pairs)], axis=1),
            jnp.concatenate([low(dv[index, begin:end, :]) for index in range(pairs)], axis=1),
        ]
        gnq = jnp.zeros((TILE, RANK), jnp.float32)
        gnormed = jnp.zeros((TILE, width), jnp.float32)
        for index, value in enumerate(values):
            start, stop = index * width, (index + 1) * width
            gnq = gnq + dotf(value, bq[:, start:stop], NT)
            add_upper(3 * width + start, dotf(narrow_q, value, TN))
            gnormed = gnormed + dotf(value, wqkv[:, start:stop], NT)
        gnq = low(gnq)
        gnormed = gnormed + dotf(gnq, aq[...])
        unit, scaled = norm_parts(wide(xr[tile * blocks : (tile + 1) * blocks].reshape(TILE, width)))
        normed = low(unit * wide(gain_ref[0:1, :]) + wide(shift_ref[0:1, :]))
        add_upper(0, dotf(gnq, normed, TN))
        dx = low(mid[...] + norm_back(gnormed, unit, scaled, wide(gain_ref[0:1, :])))
        if tile:
            fetches(tile - 1)[3].start()
        xr[tile * blocks : (tile + 1) * blocks] = dx.reshape(blocks, span, width)
        if not solo:
            for block in tile_blocks(tile):

                @pl.when(me != block)
                def _():
                    b_copy(block).start()

                @pl.when(me == block)
                def _():
                    own_b.start()

    part[0:RANK, 3 * width :] = ADAPTER_SCALE * part[0:RANK, 3 * width :]
    part[RANK : 2 * RANK, hidden:] = ADAPTER_SCALE * part[RANK : 2 * RANK, hidden:]
    if solo:
        total_ref[...] = part[...]
        return
    sum_everywhere(splits, copies, part, total_ref, *sum_refs)
    own_f.wait()
    own_b.wait()
    for slot, peer in enumerate(far + near):
        x_copy(peer, slot).wait_send()
        c_copy(peer, slot).wait_send()
        send(out_row.at[peer], output.at[peer], f_sent.at[peer], f_land.at[peer], "seq", peer).wait()
        send(xr.at[peer], dx_out.at[peer], b_sent.at[peer], b_land.at[peer], "seq", peer).wait()


def whole_block(splits, copies, solo, lengths, inputs, cotangent, small, weights):
    span, width = inputs.shape[1:]
    total = splits * span
    hidden = weights[2].shape[1]
    heads = 2 * width // LANES
    blocks = TILE // span
    anyspace = pl.BlockSpec(memory_space=pl.ANY)
    vmem = pl.BlockSpec(memory_space=pltpu.VMEM)
    bf, f32 = jnp.bfloat16, jnp.float32
    row = (splits, span, width)
    shapes = [
        (row, bf),
        (row, bf),
        ((2 * RANK, 8 * width), f32),
        (row, bf),
        (row, bf),
        ((heads // 2, total, LANES), bf),
        ((total, width), f32),
        ((total, hidden), bf),
        ((total, hidden), bf),
    ]
    dma = pltpu.SemaphoreType.DMA
    scratch = [
        *[pltpu.VMEM(w.shape, bf) for w in weights],
        pltpu.VMEM((heads, total, LANES), bf),
        pltpu.VMEM((heads, total, LANES), bf),
        pltpu.VMEM((heads, total, LANES), bf),
        pltpu.VMEM((heads // 2, total, LANES), f32),
        pltpu.VMEM((heads // 2, total, LANES), f32),
        pltpu.VMEM(row, bf),
        pltpu.VMEM((heads // 2, TILE, LANES), bf),
        pltpu.VMEM((TILE, width), f32),
        pltpu.VMEM((TILE, hidden), bf),
        pltpu.VMEM((TILE, hidden), bf),
        pltpu.VMEM((blocks, span, width), bf),
        pltpu.VMEM((blocks, span, width), bf),
        pltpu.VMEM((heads, TILE, LANES), bf),
        pltpu.VMEM((heads // 2, TILE, LANES), bf),
        pltpu.VMEM((total, LANES), bf),
        pltpu.VMEM((2 * RANK, 8 * width), f32),
        *adapter_scratch(width, hidden),
        dma((4,)),
        dma((5,)),
        dma((4 + blocks,)),
        dma((3,)),
        *[dma((splits,)) for _ in range(8)],
    ]
    if not solo:
        scratch += sum_scratch(splits, copies, 8 * width)
    return pl.pallas_call(
        lambda *refs: block_kernel(splits, copies, solo, *refs),
        out_shape=[jax.ShapeDtypeStruct(s, d) for s, d in shapes],
        in_specs=[pl.BlockSpec(memory_space=pltpu.SMEM)] + [anyspace] * 6 + [vmem] * len(small),
        out_specs=[anyspace, anyspace, vmem] + [anyspace] * 6,
        scratch_shapes=scratch,
        compiler_params=pltpu.CompilerParams(
            collective_id=None if solo else 4, has_side_effects=not solo, vmem_limit_bytes=64 * 2**20 - 2**18
        ),
        name="block",
    )(lengths, inputs, cotangent, *weights, *small)[:3]


def local_by_heads(
    inputs,
    cotangent,
    lengths,
    norm_gain,
    norm_shift,
    query_key_value_weight,
    output_projection_weight,
    first_feedforward_weight,
    second_feedforward_weight,
    biases,
    down_model,
    down_hidden,
    query_key_value_upward,
    hidden_adapter_upward,
    model_adapter_upward,
    row_down_model,
    col_down_model,
    row_down_hidden,
    col_down_hidden,
    row_up_qkv,
    col_up_qkv,
    row_up_hidden,
    col_up_hidden,
    row_up_model,
    col_up_model,
):
    rows, span, width = inputs.shape
    hidden_width = first_feedforward_weight.shape[1]
    count = rows * span
    spots = lax.axis_index("seq") * span + jnp.arange(span)
    keep = (spots[None, :] < lengths[:, None]).astype(jnp.float32).reshape(count, 1)
    flat = inputs.reshape(count, width).astype(jnp.float32)
    shifts = biases.astype(jnp.float32)
    query_bias = shifts[0:width]
    value_bias = shifts[width : 2 * width]
    projection_bias = shifts[2 * width : 3 * width]
    expand_bias_vector = shifts[3 * width : 3 * width + hidden_width]
    contract_bias_vector = shifts[3 * width + hidden_width : 4 * width + hidden_width]
    query_key_value_bias = jnp.concatenate([query_bias, jnp.zeros_like(query_bias), value_bias])
    gains = norm_gain.astype(jnp.float32)
    offsets = norm_shift.astype(jnp.float32)
    down_low = down_model.astype(jnp.bfloat16)
    hidden_down_low = down_hidden.astype(jnp.bfloat16)
    qkv_up_low = query_key_value_upward.astype(jnp.bfloat16)
    hidden_up_low = hidden_adapter_upward.astype(jnp.bfloat16)
    model_up_low = model_adapter_upward.astype(jnp.bfloat16)
    normalized_rows, unit_first, scaled_first = normalize(flat, gains[0], offsets[0])
    normalized_rows = normalized_rows.astype(jnp.bfloat16)
    mixed_rows, narrow_qkv = adapted(
        normalized_rows, query_key_value_weight, query_key_value_bias, down_low[0], qkv_up_low
    )
    mixed_rows = mixed_rows.astype(jnp.bfloat16).reshape(rows, span, 3, HEADS, HEAD_DIM)
    by_head = lax.all_to_all(mixed_rows, "seq", split_axis=3, concat_axis=1, tiled=True)
    out_heads, lse = lax.map(partial(head_forward, False), (by_head, lengths))
    attended_rows = jax.tree.map(
        lambda part, own: part.astype(own.dtype),
        lax.all_to_all(as_sent(out_heads), "seq", split_axis=1, concat_axis=2, tiled=True),
        out_heads,
    )
    attended_rows = attended_rows.reshape(count, width)
    branch_path, narrow_proj = adapted(
        attended_rows, output_projection_weight, projection_bias, down_low[1], model_up_low[0]
    )
    middle = flat + branch_path
    normed_mid, unit_second, scaled_second = normalize(middle, gains[1], offsets[1])
    normed_mid = normed_mid.astype(jnp.bfloat16)
    before, narrow_expand = adapted(
        normed_mid, first_feedforward_weight, expand_bias_vector, down_low[2], hidden_up_low
    )
    activated, gelu_pull = jax.vjp(lambda value: jax.nn.gelu(value, approximate=True), before)
    activated = activated.astype(jnp.bfloat16)
    branch_out, narrow_contract = adapted(
        activated, second_feedforward_weight, contract_bias_vector, hidden_down_low, model_up_low[1]
    )
    output = (middle + branch_out).astype(jnp.bfloat16).reshape(rows, span, width)
    grad_out = cotangent.reshape(count, width).astype(jnp.float32) * keep
    grad_act, grad_down_contract, grad_up_contract = adapted_back(
        grad_out.astype(jnp.bfloat16),
        activated,
        second_feedforward_weight,
        hidden_down_low,
        model_up_low[1],
        narrow_contract,
    )
    grad_before = gelu_pull(grad_act)[0].astype(jnp.bfloat16)
    grad_norm_mid, grad_down_expand, grad_up_expand = adapted_back(
        grad_before, normed_mid, first_feedforward_weight, down_low[2], hidden_up_low, narrow_expand
    )
    grad_mid = grad_out + normalize_back(grad_norm_mid, unit_second, scaled_second, gains[1])
    grad_att, grad_down_proj, grad_up_proj = adapted_back(
        grad_mid.astype(jnp.bfloat16),
        attended_rows,
        output_projection_weight,
        down_low[1],
        model_up_low[0],
        narrow_proj,
    )
    grad_att = grad_att.astype(jnp.bfloat16).reshape(rows, span, HEADS, HEAD_DIM)
    grad_heads = lax.all_to_all(grad_att, "seq", split_axis=2, concat_axis=1, tiled=True)
    grad_triple = lax.map(partial(head_backward, False), (by_head, grad_heads, lse, lengths))
    grad_mixed = jax.tree.map(
        lambda part, own: part.astype(own.dtype),
        lax.all_to_all(as_sent(grad_triple), "seq", split_axis=1, concat_axis=3, tiled=True),
        grad_triple,
    )
    grad_mixed = grad_mixed.reshape(count, 3 * width)
    grad_normed, grad_down_qkv, grad_up_qkv = adapted_back(
        grad_mixed, normalized_rows, query_key_value_weight, down_low[0], qkv_up_low, narrow_qkv
    )
    input_grad = (
        (grad_mid + normalize_back(grad_normed, unit_first, scaled_first, gains[0]))
        .astype(jnp.bfloat16)
        .reshape(rows, span, width)
    )
    grads = lax.psum(
        (
            jnp.stack([grad_down_qkv, grad_down_proj, grad_down_expand]),
            grad_down_contract,
            grad_up_qkv,
            grad_up_expand,
            jnp.stack([grad_up_proj, grad_up_contract]),
        ),
        ("dp", "seq"),
    )
    grad_dm, grad_dh, grad_uq, grad_uh, grad_um = grads
    new_dm, row_dm, col_dm = factored(grad_dm, down_model, row_down_model, col_down_model)
    new_dh, row_dh, col_dh = factored(grad_dh, down_hidden, row_down_hidden, col_down_hidden)
    new_uq, row_uq, col_uq = factored(grad_uq, query_key_value_upward, row_up_qkv, col_up_qkv)
    new_uh, row_uh, col_uh = factored(grad_uh, hidden_adapter_upward, row_up_hidden, col_up_hidden)
    new_um, row_um, col_um = factored(grad_um, model_adapter_upward, row_up_model, col_up_model)
    return (
        output,
        input_grad,
        grad_dm,
        grad_dh,
        grad_uq,
        grad_uh,
        grad_um,
        new_dm,
        new_dh,
        new_uq,
        new_uh,
        new_um,
        row_dm,
        row_dh,
        row_uq,
        row_uh,
        row_um,
        col_dm,
        col_dh,
        col_uq,
        col_uh,
        col_um,
    )


def local_by_rows(
    pieces,
    copies,
    inputs,
    cotangent,
    lengths,
    norm_gain,
    norm_shift,
    query_key_value_weight,
    output_projection_weight,
    first_feedforward_weight,
    second_feedforward_weight,
    biases,
    down_model,
    down_hidden,
    query_key_value_upward,
    hidden_adapter_upward,
    model_adapter_upward,
    row_down_model,
    col_down_model,
    row_down_hidden,
    col_down_hidden,
    row_up_qkv,
    col_up_qkv,
    row_up_hidden,
    col_up_hidden,
    row_up_model,
    col_up_model,
):
    flip = lambda array: jnp.swapaxes(array, -1, -2)
    adapters = [
        flip(down_model),
        flip(down_hidden),
        query_key_value_upward,
        hidden_adapter_upward,
        model_adapter_upward,
    ]
    norms = [norm_gain, norm_shift]
    weights = [
        query_key_value_weight,
        output_projection_weight,
        first_feedforward_weight,
        second_feedforward_weight,
    ]
    output, input_grad, total = whole_block(
        pieces, copies, False, lengths, inputs, cotangent, [biases.reshape(1, -1)] + norms + adapters, weights
    )
    return update(
        total,
        output,
        input_grad,
        adapters,
        row_down_model,
        col_down_model,
        row_down_hidden,
        col_down_hidden,
        row_up_qkv,
        col_up_qkv,
        row_up_hidden,
        col_up_hidden,
        row_up_model,
        col_up_model,
    )


def local(pieces, copies, inputs, *others):
    if inputs.shape[0] == pieces and TILE % inputs.shape[1] == 0:
        return local_by_rows(pieces, copies, inputs, *others)
    return local_by_heads(inputs, *others)


def solution(mesh):
    placed = (
        P("dp", "seq", None),
        P("dp", "seq", None),
        P("dp"),
        P(),
        P(),
        P(),
        P(),
        P(),
        P(),
        P(),
        P(),
        P(),
        P(),
        P(),
        P(),
        P(),
        P(),
        P(),
        P(),
        P(),
        P(),
        P(),
        P(),
        P(),
        P(),
    )
    return jax.shard_map(
        partial(local, mesh.shape["seq"], mesh.shape["dp"]),
        mesh=mesh,
        in_specs=placed,
        out_specs=(
            P("dp", "seq", None),
            P("dp", "seq", None),
            P(),
            P(),
            P(),
            P(),
            P(),
            P(),
            P(),
            P(),
            P(),
            P(),
            P(),
            P(),
            P(),
            P(),
            P(),
            P(),
            P(),
            P(),
            P(),
            P(),
        ),
        check_vma=False,
    )
```

```python
from functools import partial

import jax
import jax.numpy as jnp
from jax import lax
from jax.experimental import pallas as pl
from jax.experimental.pallas import tpu as pltpu
from jax.sharding import PartitionSpec as P


HEADS = 16
HEAD_DIM = 64
STEP = 10


NORM_EPS = 1e-05
ADAPTER_SCALE = 8.0
STAT_EPS = 1e-30
CLIP_LEVEL = 1.0
RATE = 0.3
DECAY_WEIGHT = 0.01
MASKED = -1e30


def as_sent(array):

    def short(part):
        return part.astype(jnp.bfloat16) if part.dtype == jnp.float32 else part

    return jax.tree.map(short, array)


def normalize(values, gain, shift):
    centered = values - jnp.mean(values, axis=-1, keepdims=True)
    spread = jnp.mean(centered * centered, axis=-1, keepdims=True)
    scaled = lax.rsqrt(spread + NORM_EPS)
    unit = centered * scaled
    return (unit * gain + shift, unit, scaled)


def normalize_back(grad, unit, scaled, gain):
    gained = grad * gain
    return scaled * (
        gained
        - jnp.mean(gained, axis=-1, keepdims=True)
        - unit * jnp.mean(gained * unit, axis=-1, keepdims=True)
    )


def matrix_multiply(left, right):
    return jnp.dot(left, right, preferred_element_type=jnp.float32)


def inner_product(left, right):
    return jnp.einsum("tr,tc->rc", left, right, preferred_element_type=jnp.float32)


def compared_with(left, right):
    return jnp.einsum("tc,rc->tr", left, right, preferred_element_type=jnp.float32)


def adapted(source_rows, weight_matrix, bias_vector, down, upward_matrix):
    narrowed_rows = matrix_multiply(source_rows, down).astype(jnp.bfloat16)
    return (
        matrix_multiply(source_rows, weight_matrix)
        + bias_vector
        + ADAPTER_SCALE * matrix_multiply(narrowed_rows, upward_matrix),
        narrowed_rows,
    )


def adapted_back(gradient_lowrank, source_rows, weight_matrix, down, upward_matrix, narrowed_rows):
    gradient_upward = ADAPTER_SCALE * inner_product(narrowed_rows, gradient_lowrank)
    gradient_narrowed = (ADAPTER_SCALE * compared_with(gradient_lowrank, upward_matrix)).astype(
        jnp.bfloat16
    )
    grad_down = inner_product(source_rows, gradient_narrowed)
    grad_source = compared_with(gradient_lowrank, weight_matrix) + compared_with(
        gradient_narrowed, down
    )
    return (grad_source, grad_down, gradient_upward)


def score_block(operand):
    query, keys = operand
    return jnp.einsum("gqe,gke->gqk", query, keys, preferred_element_type=jnp.float32)


def mix_block(operand):
    weights, values = operand
    return jnp.einsum("gqk,gke->gqe", weights, values, preferred_element_type=jnp.float32)


def spread_block(operand):
    weights, queries = operand
    return jnp.einsum("gqk,gqe->gke", weights, queries, preferred_element_type=jnp.float32)


def masked_scores(query, keys, spots, length):
    total = keys.shape[1]
    size = min(512, total)
    reach = jnp.minimum(length, jnp.max(spots) + 1)
    places = jnp.arange(total)
    valid = (places[None, :] <= spots[:, None]) & (places[None, :] < length)
    pieces = []
    for begin in range(0, total, size):
        pieces.append(score_block((query, keys[:, begin : begin + size])))
    scores = jnp.concatenate(pieces, axis=-1) * query.shape[-1] ** (-0.5)
    return (jnp.where(valid[None], scores, MASKED), reach, size)


def attend(query, keys, values, spots, length):
    scores, reach, size = masked_scores(query, keys, spots, length)
    top = jnp.max(scores, axis=-1, keepdims=True)
    weights = jnp.exp(scores - top)
    summed = jnp.sum(weights, axis=-1, keepdims=True)
    probs = (weights / summed).astype(jnp.bfloat16)
    result = jnp.zeros(query.shape, jnp.float32)
    for begin in range(0, keys.shape[1], size):
        operand = (probs[:, :, begin : begin + size], values[:, begin : begin + size])
        result = result + mix_block(operand)
    return (result, (top + jnp.log(summed))[..., 0])


def attend_back(query, keys, values, spots, length, grad_rows, lse):
    scores, reach, size = masked_scores(query, keys, spots, length)
    probs = jnp.exp(scores - lse[..., None])
    pieces = []
    for begin in range(0, keys.shape[1], size):
        pieces.append(score_block((grad_rows, values[:, begin : begin + size])))
    dprob = jnp.concatenate(pieces, axis=-1)
    delta = jnp.sum(probs * dprob, axis=-1, keepdims=True)
    dscore = (probs * (dprob - delta)).astype(jnp.bfloat16)
    probs_low = probs.astype(jnp.bfloat16)
    scale = query.shape[-1] ** (-0.5)
    grad_query = jnp.zeros(query.shape, jnp.float32)
    key_parts = []
    value_parts = []
    for begin in range(0, keys.shape[1], size):
        grad_query = grad_query + mix_block(
            (dscore[:, :, begin : begin + size], keys[:, begin : begin + size])
        )
        key_parts.append(spread_block((dscore[:, :, begin : begin + size], query)))
        value_parts.append(spread_block((probs_low[:, :, begin : begin + size], grad_rows)))
    return (
        grad_query * scale,
        jnp.concatenate(key_parts, axis=1) * scale,
        jnp.concatenate(value_parts, axis=1),
    )


def heads_split(triple):
    return tuple((jnp.transpose(triple[:, index], (1, 0, 2)) for index in range(3)))


def head_forward(skip, item):
    triple, length = item
    spots = jnp.arange(triple.shape[0])
    query, keys, values = heads_split(triple)
    result, lse = attend(query, keys, values, spots, length)
    return (jnp.transpose(result, (1, 0, 2)).astype(jnp.bfloat16), lse)


def head_backward(skip, item):
    triple, grad_rows, lse, length = item
    spots = jnp.arange(triple.shape[0])
    query, keys, values = heads_split(triple)
    grads = attend_back(
        query, keys, values, spots, length, jnp.transpose(grad_rows, (1, 0, 2)), lse
    )
    return jnp.stack(grads, axis=0).transpose(2, 0, 1, 3).astype(jnp.bfloat16)


def factored(grad, weight_matrix, row, col):
    decay = 1.0 - STEP ** (-0.8)
    squares = grad * grad + STAT_EPS
    new_row = decay * row + (1.0 - decay) * jnp.mean(squares, axis=-1)
    new_col = decay * col + (1.0 - decay) * jnp.mean(squares, axis=-2)
    second = (
        new_row[..., :, None] * new_col[..., None, :] / jnp.mean(new_row, axis=-1)[..., None, None]
    )
    unit = grad * lax.rsqrt(second)
    level = jnp.sqrt(jnp.mean(unit * unit, axis=(-2, -1), keepdims=True))
    unit = unit / jnp.maximum(1.0, level / CLIP_LEVEL)
    rate = RATE * jnp.sqrt(jnp.mean(weight_matrix * weight_matrix, axis=(-2, -1), keepdims=True))
    return (weight_matrix - rate * (unit + DECAY_WEIGHT * weight_matrix), new_row, new_col)


LOG2E = 1.4426950408889634
NT = (((1,), (1,)), ((), ()))
TN = (((0,), (0,)), ((), ()))


def dotf(a, b, dims=(((1,), (0,)), ((), ()))):
    return lax.dot_general(a, b, dims, preferred_element_type=jnp.float32)


def triple(value):
    high = value.astype(jnp.bfloat16)
    rest = value - high.astype(jnp.float32)
    mid = rest.astype(jnp.bfloat16)
    low = (rest - mid.astype(jnp.float32)).astype(jnp.bfloat16)
    return high, mid, low


GELU_A = 0.7978845608028654
GELU_B = 0.7978845608028654 * 0.044715
RANK = 4


def norm_parts(values):
    centered = values - jnp.mean(values, axis=-1, keepdims=True)
    spread = jnp.mean(centered * centered, axis=-1, keepdims=True)
    scaled = lax.rsqrt(spread + NORM_EPS)
    return centered * scaled, scaled


def norm_back(grad, unit, scaled, gain):
    gained = grad * gain
    return scaled * (
        gained
        - jnp.mean(gained, axis=-1, keepdims=True)
        - unit * jnp.mean(gained * unit, axis=-1, keepdims=True)
    )


def low(value):
    return value.astype(jnp.bfloat16)


def wide(value):
    return value.astype(jnp.float32)


def gelu_pair(value):
    square = value * value
    half = 0.5 * value
    bent = jnp.tanh(value * (GELU_A + GELU_B * square))
    slope = (0.5 + 0.5 * bent) + half * (1.0 - bent * bent) * (GELU_A + 3.0 * GELU_B * square)
    return half + half * bent, slope


def peers_of(axis, size):
    me = lax.axis_index(axis)
    return me, [lax.rem(me + shift, size) for shift in range(1, size)]


def greet(axes):
    barrier = pltpu.get_barrier_semaphore()
    count = 0
    for axis, size in axes:
        _, peers = peers_of(axis, size)
        for peer in peers:
            pl.semaphore_signal(
                barrier, inc=1, device_id={axis: peer}, device_id_type=pl.DeviceIdType.MESH
            )
        count += len(peers)
    pl.semaphore_wait(barrier, count)


def send(source, target, sent, landed, axis, peer):
    return pltpu.make_async_remote_copy(
        src_ref=source,
        dst_ref=target,
        send_sem=sent,
        recv_sem=landed,
        device_id={axis: peer},
        device_id_type=pl.DeviceIdType.MESH,
    )


def sum_everywhere(
    splits, copies, part_ref, total_ref, dp_in, seq_in, own, piece, d_sent, d_land, s_sent, s_land, g_sent, g_land, e_sent, e_land
):
    size = part_ref.shape[1] // copies
    small = size // splits
    me, peers = peers_of("seq", splits)
    mine, others = peers_of("dp", copies)

    def columns(index):
        return pl.ds(pl.multiple_of(index * size, size), size)

    def narrow_columns(index, start=0):
        return pl.ds(pl.multiple_of(start + index * small, small), small)

    sent = []

    def start(copy):
        copy.start()
        sent.append(copy)

    for shift, peer in enumerate(others):
        start(send(part_ref.at[:, columns(peer)], dp_in.at[mine], d_sent.at[shift], d_land.at[mine], "dp", peer))
    dp_in[mine] = part_ref[:, columns(mine)]
    for peer in others:
        send(part_ref.at[:, columns(mine)], dp_in.at[peer], d_sent.at[0], d_land.at[peer], "dp", peer).wait_recv()
    summed = dp_in[0]
    for index in range(1, copies):
        summed = summed + dp_in[index]
    own[...] = summed
    for shift, peer in enumerate(peers):
        start(send(own.at[:, narrow_columns(peer)], seq_in.at[me], s_sent.at[shift], s_land.at[me], "seq", peer))
    seq_in[me] = own[:, narrow_columns(me)]
    for peer in peers:
        send(own.at[:, narrow_columns(me)], seq_in.at[peer], s_sent.at[0], s_land.at[peer], "seq", peer).wait_recv()
    summed = seq_in[0]
    for index in range(1, splits):
        summed = summed + seq_in[index]
    piece[...] = summed
    base = mine * size
    total_ref[:, narrow_columns(me, base)] = summed
    for shift, peer in enumerate(peers):
        start(send(piece, total_ref.at[:, narrow_columns(me, base)], g_sent.at[shift], g_land.at[me], "seq", peer))
    for peer in peers:
        send(piece, total_ref.at[:, narrow_columns(peer, base)], g_sent.at[0], g_land.at[peer], "seq", peer).wait_recv()
    for shift, peer in enumerate(others):
        part = total_ref.at[:, columns(mine)]
        start(send(part, part, e_sent.at[shift], e_land.at[mine], "dp", peer))
    for peer in others:
        part = total_ref.at[:, columns(peer)]
        send(part, part, e_sent.at[0], e_land.at[peer], "dp", peer).wait_recv()
    for copy in sent:
        copy.wait_send()


def sum_scratch(splits, copies, width):
    size = width // copies
    small = size // splits
    dma = pltpu.SemaphoreType.DMA
    return [
        pltpu.VMEM((copies, 8, size), jnp.float32),
        pltpu.VMEM((splits, 8, small), jnp.float32),
        pltpu.VMEM((8, size), jnp.float32),
        pltpu.VMEM((8, small), jnp.float32),
        dma((copies,)),
        dma((copies,)),
        dma((splits,)),
        dma((splits,)),
        dma((splits,)),
        dma((splits,)),
        dma((copies,)),
        dma((copies,)),
    ]


def across(column):
    count = column.shape[0]
    diagonal = lax.broadcasted_iota(jnp.int32, (count, count), 0) == lax.broadcasted_iota(
        jnp.int32, (count, count), 1
    )
    return jnp.sum(jnp.where(diagonal, jnp.broadcast_to(column, (count, count)), 0.0), axis=0, keepdims=True)


def upright(line):
    count = line.shape[1]
    diagonal = lax.broadcasted_iota(jnp.int32, (count, count), 0) == lax.broadcasted_iota(
        jnp.int32, (count, count), 1
    )
    return jnp.sum(jnp.where(diagonal, jnp.broadcast_to(line, (count, count)), 0.0), axis=1, keepdims=True)


def factored_step(grad, weight, short_line, long_line, rows_long):
    decay = 1.0 - STEP ** (-0.8)
    squares = grad * grad + STAT_EPS
    new_short = decay * upright(short_line) + (1.0 - decay) * jnp.mean(squares, axis=1, keepdims=True)
    new_long = decay * long_line + (1.0 - decay) * jnp.mean(squares, axis=0, keepdims=True)
    if rows_long:
        middle = jnp.mean(new_long, axis=1, keepdims=True)
    else:
        middle = jnp.mean(new_short, axis=0, keepdims=True)
    unit = grad * lax.rsqrt(new_short * new_long / middle)
    entries = grad.shape[0] * grad.shape[1]

    def mean_square(value):
        return jnp.sum(jnp.sum(value * value, axis=1, keepdims=True), axis=0, keepdims=True) / entries

    level = jnp.sqrt(mean_square(unit))
    unit = unit / jnp.maximum(1.0, level / CLIP_LEVEL)
    rate = RATE * jnp.sqrt(mean_square(weight))
    return weight - rate * (unit + DECAY_WEIGHT * weight), across(new_short), new_long


def update_kernel(
    total_ref, output_in, grad_in, dm, dh, uq, uh, um, row_dm, col_dm, row_dh, col_dh, row_uq, col_uq, row_uh, col_uh, row_um, col_um,
    output_out, grad_out, g_dm, g_dh, g_uq, g_uh, g_um, n_dm, n_dh, n_uq, n_uh, n_um,
    r_dm, r_dh, r_uq, r_uh, r_um, c_dm, c_dh, c_uq, c_uh, c_um, held_out, held_grad, sems,
):
    moves = []
    for index in range(output_in.shape[0]):
        for place, (source, held, target) in enumerate(
            ((output_in, held_out, output_out), (grad_in, held_grad, grad_out))
        ):
            moves.append(
                (
                    pltpu.make_async_copy(source.at[index], held.at[index], sems.at[place, index]),
                    pltpu.make_async_copy(held.at[index], target.at[index], sems.at[place, index]),
                )
            )
    for move, _ in moves:
        move.start()
    for move, onward in moves:
        move.wait()
        onward.start()
    width = dm.shape[2]
    hidden = dh.shape[1]
    for index in range(3):
        grad = total_ref[0:RANK, index * width : (index + 1) * width]
        g_dm[index] = grad
        n_dm[index], c_dm[index : index + 1, :], r_dm[index : index + 1, :] = factored_step(
            grad, dm[index], col_dm[index : index + 1, :], row_dm[index : index + 1, :], True
        )
    grad = total_ref[0:RANK, 3 * width : 6 * width]
    g_uq[...] = grad
    n_uq[...], r_uq[...], c_uq[...] = factored_step(grad, uq[...], row_uq[...], col_uq[...], False)
    for index in range(2):
        grad = total_ref[0:RANK, (6 + index) * width : (7 + index) * width]
        g_um[index] = grad
        n_um[index], r_um[index : index + 1, :], c_um[index : index + 1, :] = factored_step(
            grad, um[index], row_um[index : index + 1, :], col_um[index : index + 1, :], False
        )
    grad = total_ref[RANK : 2 * RANK, 0:hidden]
    g_dh[...] = grad
    n_dh[...], c_dh[...], r_dh[...] = factored_step(grad, dh[...], col_dh[...], row_dh[...], True)
    grad = total_ref[RANK : 2 * RANK, hidden : 2 * hidden]
    g_uh[...] = grad
    n_uh[...], r_uh[...], c_uh[...] = factored_step(grad, uh[...], row_uh[...], col_uh[...], False)
    for _, onward in moves:
        onward.wait()


def update(total, output, input_grad, adapters, row_dm, col_dm, row_dh, col_dh, row_uq, col_uq, row_uh, col_uh, row_um, col_um):
    flip = lambda array: jnp.swapaxes(array, -1, -2)
    line = lambda array: array.reshape(1, -1)
    given = [
        row_dm, col_dm, line(row_dh), line(col_dh), line(row_uq), line(col_uq), line(row_uh), line(col_uh), row_um, col_um,
    ]
    stats = given[0::2] + given[1::2]
    anyspace = pl.BlockSpec(memory_space=pl.ANY)
    vmem = pl.BlockSpec(memory_space=pltpu.VMEM)
    results = pl.pallas_call(
        update_kernel,
        out_shape=[jax.ShapeDtypeStruct(a.shape, a.dtype) for a in [output, input_grad] + adapters + adapters + stats],
        in_specs=[vmem, anyspace, anyspace] + [vmem] * 15,
        out_specs=[anyspace, anyspace] + [vmem] * 20,
        scratch_shapes=[
            pltpu.VMEM(output.shape, output.dtype),
            pltpu.VMEM(output.shape, output.dtype),
            pltpu.SemaphoreType.DMA((2, output.shape[0])),
        ],
        compiler_params=pltpu.CompilerParams(vmem_limit_bytes=60 * 2**20),
        name="factored_update",
    )(total, output, input_grad, *adapters, *given)
    results = list(results)
    for index in (2, 3, 7, 8):
        results[index] = flip(results[index])
    olds = (row_dm, row_dh, row_uq, row_uh, row_um, col_dm, col_dh, col_uq, col_uh, col_um)
    for index, old in zip(range(12, 22), olds):
        results[index] = results[index].reshape(old.shape)
    return tuple(results)


def fill_adapters(dm_ref, dh_ref, uq_ref, uh_ref, um_ref, aq, ap, a1, a2, bq, bp, b2, b1):
    for index, ref in enumerate((aq, ap, a1)):
        ref[...] = low(dm_ref[index])
    a2[...] = low(dh_ref[...])
    for ref, value in ((bq, uq_ref[...]), (bp, um_ref[0]), (b2, um_ref[1]), (b1, uh_ref[...])):
        ref[...] = low(ADAPTER_SCALE * wide(low(value)))


def adapter_scratch(width, hidden):
    sizes = [width, width, width, hidden, 3 * width, width, width, hidden]
    return [pltpu.VMEM((RANK, size), jnp.bfloat16) for size in sizes]


TILE = 256
GROUP = 4
LANES = 128


def peer_order(me, splits):
    half = splits // 2
    side, place = me // half, lax.rem(me, half)
    far = [(1 - side) * half + lax.rem(place + shift, half) for shift in range(half)]
    near = [side * half + lax.rem(place + shift, half) for shift in range(1, half)]
    return far, near


def block_kernel(
    splits, copies, solo,
    lengths_ref, inputs, cotangent, wqkv_hbm, wo_hbm, w1_hbm, w2_hbm,
    bias_ref, gain_ref, shift_ref, dm_ref, dh_ref, uq_ref, uh_ref, um_ref,
    output, dx_out, total_ref, cot_in, out_row, att_hbm, mid_hbm, act_hbm, slope_hbm,
    wqkv, wo, w1, w2, kx, vx, qx, dk, dv, xr, att, mid, act, slope, cot_t, outs, gx, dq, narrow, part,
    bias_row, aq, ap, a1, a2, bq, bp, b2, b1,
    w_sem, s_sem, l_sem, own_sem, x_sent, x_land, c_sent, c_land, f_sent, f_land, b_sent, b_land,
    *sum_refs,
):
    me = 0 if solo else lax.axis_index("seq")
    span, width = xr.shape[1], xr.shape[2]
    hidden = w1.shape[1]
    total = splits * span
    tiles = total // TILE
    blocks = TILE // span
    heads = kx.shape[0]
    pairs = heads // 2
    half = LANES // 2
    length = lengths_ref[me]
    upper = me >= splits // 2

    loads = [
        pltpu.make_async_copy(source, target, w_sem.at[index])
        for index, (source, target) in enumerate(((wqkv_hbm, wqkv), (wo_hbm, wo), (w1_hbm, w1), (w2_hbm, w2)))
    ]
    own_x = pltpu.make_async_copy(inputs if solo else inputs.at[me], xr if solo else xr.at[me], own_sem.at[0])
    own_b = pltpu.make_async_copy(xr.at[me], dx_out.at[me], own_sem.at[1])

    own_f = pltpu.make_async_copy(out_row.at[me], output.at[me], own_sem.at[2])

    def saves(tile):
        rows = pl.ds(tile * TILE, TILE)
        moves = (
            (att, att_hbm.at[:, rows, :]),
            (mid, mid_hbm.at[rows, :]),
            (act, act_hbm.at[rows, :]),
            (slope, slope_hbm.at[rows, :]),
            (outs, out_row.at[pl.ds(tile * blocks, blocks)]),
        )
        return [pltpu.make_async_copy(a, b, s_sem.at[i]) for i, (a, b) in enumerate(moves)]

    def fetches(tile):
        rows = pl.ds(tile * TILE, TILE)
        moves = (
            (slope_hbm.at[rows, :], slope),
            (act_hbm.at[rows, :], act),
            (att_hbm.at[:, rows, :], att),
            (mid_hbm.at[rows, :], mid),
        )
        return [pltpu.make_async_copy(a, b, l_sem.at[i]) for i, (a, b) in enumerate(moves)]

    def x_copy(peer, slot):
        return send(inputs.at[peer], xr.at[me], x_sent.at[slot], x_land.at[me], "seq", peer)

    def c_copy(peer, slot):
        return send(cotangent.at[peer], cot_in.at[me], c_sent.at[slot], c_land.at[me], "seq", peer)

    def f_copy(block):
        return send(out_row.at[block], output.at[me], f_sent.at[block], f_land.at[me], "seq", block)

    def b_copy(block):
        return send(xr.at[block], dx_out.at[me], b_sent.at[block], b_land.at[me], "seq", block)

    def tile_blocks(tile):
        return range(tile * blocks, (tile + 1) * blocks)

    def cot_move(block, fetched):
        slot = cot_t.at[block % blocks]
        source = cotangent.at[me] if fetched else cot_in.at[block]
        return pltpu.make_async_copy(source, slot, l_sem.at[4 + block % blocks])

    def cot_fetch(tile):
        if solo:
            for block in tile_blocks(tile):
                cot_move(block, False).start()
            return
        for block in tile_blocks(tile):

            @pl.when(me == block)
            def _():
                cot_move(block, True).start()

            @pl.when(me != block)
            def _():
                send(cotangent.at[block], cot_in.at[block], c_sent.at[0], c_land.at[block], "seq", block).wait_recv()
                cot_move(block, False).start()

    def x_wait(tile):
        if solo:
            return
        for block in tile_blocks(tile):

            @pl.when(me != block)
            def _():
                send(inputs.at[block], xr.at[block], x_sent.at[0], x_land.at[block], "seq", block).wait_recv()

    def send_output(tile):
        if solo:
            return
        for block in tile_blocks(tile):

            @pl.when(me != block)
            def _():
                f_copy(block).start()

    if not solo:
        greet((("seq", splits), ("dp", copies)))
    own_x.start()
    loads[0].start()
    if not solo:
        far, near = peer_order(me, splits)
        early = lax.rem(me, splits // 2) < splits // 4
        lower_early = jnp.logical_and(early, jnp.logical_not(upper))
        lower_late = jnp.logical_and(jnp.logical_not(early), jnp.logical_not(upper))
        ways = list(enumerate(far + near))

        @pl.when(jnp.logical_not(lower_early))
        def _():
            for slot, peer in ways[len(far) :]:
                x_copy(peer, slot).start()

        @pl.when(jnp.logical_not(lower_late))
        def _():
            for slot, peer in ways[: len(far)]:
                x_copy(peer, slot).start()

    for load in loads[1:]:
        load.start()
    fill_adapters(dm_ref, dh_ref, uq_ref, uh_ref, um_ref, aq, ap, a1, a2, bq, bp, b2, b1)
    part[...] = jnp.zeros_like(part)
    bias_lines = wide(bias_ref[...])
    for index in range(bias_ref.shape[0]):
        bias_row[0:1, index * LANES : (index + 1) * LANES] = bias_lines[index : index + 1, :]

    lane = lax.broadcasted_iota(jnp.int32, (TILE, LANES), 1)
    row = lax.broadcasted_iota(jnp.int32, (TILE, TILE), 0)
    col = lax.broadcasted_iota(jnp.int32, (TILE, TILE), 1)
    zero = jnp.zeros((TILE, LANES), jnp.bfloat16)
    one = jnp.ones((TILE, LANES), jnp.bfloat16)
    scale = half ** (-0.5)
    owns = (lane < half, lane >= half)
    spares = (half, 0)

    def absorb(weight, down, up):
        rows, columns = weight.shape
        size = 1024

        def step(index, carry):
            span_rows = pl.ds(pl.multiple_of(index * TILE, TILE), TILE)
            left = down[:, span_rows]
            for start in range(0, columns, size):
                part_ref = weight.at[span_rows, pl.ds(start, size)]
                part_ref[...] = low(wide(part_ref[...]) + dotf(left, up[:, start : start + size], TN))
            return carry

        lax.fori_loop(0, rows // TILE, step, 0)

    def with_extra(own, spare, value, extra):
        high, middle, rest = triple(extra)
        return jnp.where(
            own,
            value,
            jnp.where(lane == spare, high, jnp.where(lane == spare + 1, middle, jnp.where(lane == spare + 2, rest, zero))),
        )

    def bias(start, size):
        return bias_row[0:1, start : start + size]

    def rows_of(tile):
        if isinstance(tile, int):
            return pl.ds(tile * TILE, TILE)
        return pl.ds(pl.multiple_of(tile * TILE, TILE), TILE)

    def project(tile):
        rows = rows_of(tile)
        x = wide(xr[pl.ds(tile * blocks, blocks)].reshape(TILE, width))
        unit, _ = norm_parts(x)
        normed = low(unit * wide(gain_ref[0:1, :]) + wide(shift_ref[0:1, :]))
        narrow_q = low(dotf(normed, aq[...], NT))
        narrow[rows, 0:RANK] = narrow_q
        spot = tile * TILE + lax.broadcasted_iota(jnp.int32, (TILE, LANES), 0)
        limit = jnp.where(spot < length, 0.0, MASKED).astype(jnp.bfloat16)
        size = 512
        for index in range(3):
            for start in range(0, width, size):
                column = index * width + start
                value = dotf(normed, wqkv[:, column : column + size])
                if index == 0:
                    value = value + bias(start, size)
                if index == 2:
                    value = value + bias(width + start, size)
                value = low(value)
                for pair in range(size // LANES):
                    piece = value[:, pair * LANES : (pair + 1) * LANES]
                    for parity in range(2):
                        head = 2 * (start // LANES + pair) + parity
                        own, spare = owns[parity], spares[parity]
                        if index == 0:
                            extra = jnp.where(lane == spare + 3, one, zero)
                            qx[head, rows, :] = jnp.where(own, piece * jnp.asarray(scale, jnp.bfloat16), extra)
                        elif index == 1:
                            extra = jnp.where(lane == spare + 3, limit, jnp.where(lane < spare + 3, one, zero))
                            kx[head, rows, :] = jnp.where(own, piece, extra)
                        else:
                            vx[head, rows, :] = jnp.where(own, piece, one)

    own_x.wait()
    loads[0].wait()
    absorb(wqkv, aq, bq)
    loads[1].wait()
    absorb(wo, ap, bp)
    if not solo:

        @pl.when(lower_early)
        def _():
            for slot, peer in ways[len(far) :]:
                x_copy(peer, slot).start()

    loads[2].wait()
    absorb(w1, a1, b1)
    if not solo:

        @pl.when(lower_late)
        def _():
            for slot, peer in ways[: len(far)]:
                x_copy(peer, slot).start()

    loads[3].wait()
    absorb(w2, a2, b2)
    if not solo:

        @pl.when(upper)
        def _():
            for tile in range(tiles // 2, tiles):
                x_wait(tile)
            lax.fori_loop(tiles // 2, tiles, lambda tile, carry: (project(tile), carry)[1], 0)

    for tile in range(tiles):
        begin, end = tile * TILE, (tile + 1) * TILE
        if tile < tiles // 2:
            x_wait(tile)
            project(tile)
        elif solo:
            project(tile)
        else:

            @pl.when(jnp.logical_not(upper))
            def _():
                x_wait(tile)
                project(tile)

        if not solo:
            last_tile = jnp.logical_and(upper, jnp.logical_not(early))
            ready = last_tile if tile == tiles // 2 - 1 else jnp.logical_not(last_tile)
            if tile == tiles // 2 - 1 or tile == tiles // 2:

                @pl.when(ready)
                def _():
                    for slot, peer in enumerate(far + near):
                        c_copy(peer, slot).start()

        if tile:
            saves(tile - 1)[0].wait()
        valid = begin + lax.broadcasted_iota(jnp.int32, (TILE, LANES), 0) < length
        causal = col <= row

        def attend(index, carry):
            def scores(unit):
                head = index * GROUP + unit
                return dotf(qx[head, begin:end, :], kx[head, 0:end, :], NT)

            def mix(unit, value):
                head = index * GROUP + unit
                last = jnp.where(causal, value[:, begin:], MASKED)
                value = jnp.concatenate([value[:, :begin], last], axis=1) if begin else last
                top = jnp.max(value, axis=-1, keepdims=True)
                weights = low(jnp.exp2((value - top) * LOG2E))
                mixed = dotf(weights, vx[head, 0:end, :])
                spare, own = spares[unit % 2], owns[unit % 2]
                summed = mixed[:, spare : spare + 1]
                back = jnp.where(valid, -(top + jnp.log(summed)), MASKED)
                qx[head, begin:end, :] = with_extra(own, spare, qx[head, begin:end, :], back)
                return mixed * (1.0 / summed)

            ahead = scores(0)
            results = []
            for unit in range(GROUP):
                value = ahead
                if unit + 1 < GROUP:
                    ahead = scores(unit + 1)
                results.append(mix(unit, value))
            for unit in range(0, GROUP, 2):
                att[index * (GROUP // 2) + unit // 2] = low(jnp.where(owns[0], results[unit], results[unit + 1]))
            return carry

        lax.fori_loop(0, heads // GROUP, attend, 0)
        if tile:
            for save in saves(tile - 1)[1:]:
                save.wait()
        attended = jnp.concatenate([att[index] for index in range(pairs)], axis=1)
        narrow_p = low(dotf(attended, ap[...], NT))
        middle = (
            wide(xr[tile * blocks : (tile + 1) * blocks].reshape(TILE, width))
            + dotf(attended, wo[...])
            + bias(2 * width, width)
        )
        mid[...] = middle
        unit, _ = norm_parts(middle)
        normed = low(unit * wide(gain_ref[1:2, :]) + wide(shift_ref[1:2, :]))
        narrow_1 = low(dotf(normed, a1[...], NT))
        size = 256

        def expand(start):
            return dotf(normed, w1[:, start : start + size]) + bias(3 * width + start, size)

        result = middle + bias(3 * width + hidden, width)
        narrow_2 = jnp.zeros((TILE, RANK), jnp.float32)
        ahead = expand(0)
        for start in range(0, hidden, size):
            stop = start + size
            before = ahead
            if stop < hidden:
                ahead = expand(stop)
            active, bend = gelu_pair(before)
            active = low(active)
            act[:, start:stop] = active
            slope[:, start:stop] = low(bend)
            result = result + dotf(active, w2[start:stop, :])
            narrow_2 = narrow_2 + dotf(active, a2[:, start:stop], NT)
        narrow_2 = low(narrow_2)
        outs[...] = low(result).reshape(blocks, span, width)
        narrow[begin:end, RANK : 2 * RANK] = narrow_p
        narrow[begin:end, 2 * RANK : 3 * RANK] = narrow_1
        narrow[begin:end, 3 * RANK : 4 * RANK] = narrow_2
        if tile < tiles - 1:
            for save in saves(tile):
                save.start()
        else:
            saves(tile)[4].start()

    def add_upper(start, value):
        part[0:RANK, start : start + value.shape[1]] += value

    def add_lower(start, value):
        part[RANK : 2 * RANK, start : start + value.shape[1]] += value

    cot_fetch(tiles - 1)
    for tile in reversed(range(tiles)):
        begin, end = tile * TILE, (tile + 1) * TILE
        newest = tile == tiles - 1
        if newest:
            pass
        else:
            for fetch in fetches(tile)[0:3]:
                fetch.wait()
        for block in tile_blocks(tile):
            cot_move(block, False).wait()
        spot = begin + lax.broadcasted_iota(jnp.int32, (TILE, width), 0)
        given = cot_t[...].reshape(TILE, width)
        gout = jnp.where(spot < length, given, jnp.zeros_like(given))
        narrow_q = narrow[begin:end, 0:RANK]
        narrow_p = narrow[begin:end, RANK : 2 * RANK]
        narrow_1 = narrow[begin:end, 2 * RANK : 3 * RANK]
        narrow_2 = narrow[begin:end, 3 * RANK : 4 * RANK]
        gn2 = low(dotf(gout, b2[...], NT))
        add_upper(7 * width, dotf(narrow_2, gout, TN))
        size = 512

        def contract(start):
            return dotf(gout, w2[start : start + size, :], NT)

        gnorm = jnp.zeros((TILE, width), jnp.float32)
        gn1 = jnp.zeros((TILE, RANK), jnp.float32)
        ahead = contract(0)
        for start in range(0, hidden, size):
            stop = start + size
            gact = ahead
            if stop < hidden:
                ahead = contract(stop)
            gbefore = low(gact * wide(slope[:, start:stop]))
            add_lower(start, dotf(gn2, act[:, start:stop], TN))
            add_lower(hidden + start, dotf(narrow_1, gbefore, TN))
            gn1 = gn1 + dotf(gbefore, b1[:, start:stop], NT)
            gnorm = gnorm + dotf(gbefore, w1[:, start:stop], NT)
        gn1 = low(gn1)
        if not newest:
            fetches(tile)[3].wait()
        unit, scaled = norm_parts(mid[...])
        normed = low(unit * wide(gain_ref[1:2, :]) + wide(shift_ref[1:2, :]))
        add_upper(2 * width, dotf(gn1, normed, TN))
        grad = wide(gout) + norm_back(gnorm, unit, scaled, wide(gain_ref[1:2, :]))
        mid[...] = grad
        glow = low(grad)
        gnp = low(dotf(glow, bp[...], NT))
        add_upper(6 * width, dotf(narrow_p, glow, TN))
        gatt = low(dotf(glow, wo[...], NT))
        attended = jnp.concatenate([att[index] for index in range(pairs)], axis=1)
        add_upper(width, dotf(gnp, attended, TN))
        for index in range(pairs):
            piece = gatt[:, index * LANES : (index + 1) * LANES]
            product = wide(piece) * wide(att[index])
            for parity in range(2):
                own, spare = owns[parity], spares[parity]
                delta = -jnp.sum(jnp.where(own, product, 0.0), axis=-1, keepdims=True)
                gx[2 * index + parity] = with_extra(own, spare, piece, jnp.broadcast_to(delta, (TILE, LANES)))
        if tile:
            for fetch in fetches(tile - 1)[0:3]:
                fetch.start()
            cot_fetch(tile - 1)
        if newest:
            saves(tile)[4].wait()
            for done in range(tiles):
                send_output(done)
            if not solo:
                own_f.start()
        causal = row <= col

        def attend_back(index, carry):
            def products(unit):
                head = index * GROUP + unit
                return (
                    dotf(kx[head, 0:end, :], qx[head, begin:end, :], NT),
                    dotf(vx[head, 0:end, :], gx[head], NT),
                )

            def spread(unit, scores, dprob):
                head = index * GROUP + unit
                weights = jnp.exp2(scores * LOG2E)
                last = jnp.where(causal, weights[begin:], 0.0)
                weights = jnp.concatenate([weights[:begin], last], axis=0) if begin else last
                dscore = low(weights * dprob)
                return (
                    dotf(dscore, kx[head, 0:end, :], TN),
                    dotf(dscore, qx[head, begin:end, :]),
                    dotf(low(weights), gx[head]),
                )

            ahead = products(0)
            results = []
            for unit in range(GROUP):
                given = ahead
                if unit + 1 < GROUP:
                    ahead = products(unit + 1)
                results.append(spread(unit, *given))
            first_lanes = lax.broadcasted_iota(jnp.int32, (end, LANES), 1) < half
            for unit in range(0, GROUP, 2):
                pair = index * (GROUP // 2) + unit // 2
                even, odd = results[unit], results[unit + 1]
                dq[pair] = low(jnp.where(owns[0], even[0], odd[0]) * scale)
                more_k = jnp.where(first_lanes, even[1], odd[1])
                more_v = jnp.where(first_lanes, even[2], odd[2])
                if newest:
                    dk[pair] = more_k
                    dv[pair] = more_v
                else:
                    dk[pair, 0:end, :] += more_k
                    dv[pair, 0:end, :] += more_v
            return carry

        lax.fori_loop(0, heads // GROUP, attend_back, 0)
        values = [
            jnp.concatenate([dq[index] for index in range(pairs)], axis=1),
            jnp.concatenate([low(dk[index, begin:end, :]) for index in range(pairs)], axis=1),
            jnp.concatenate([low(dv[index, begin:end, :]) for index in range(pairs)], axis=1),
        ]
        gnq = jnp.zeros((TILE, RANK), jnp.float32)
        gnormed = jnp.zeros((TILE, width), jnp.float32)
        for index, value in enumerate(values):
            start, stop = index * width, (index + 1) * width
            gnq = gnq + dotf(value, bq[:, start:stop], NT)
            add_upper(3 * width + start, dotf(narrow_q, value, TN))
            gnormed = gnormed + dotf(value, wqkv[:, start:stop], NT)
        gnq = low(gnq)
        unit, scaled = norm_parts(wide(xr[tile * blocks : (tile + 1) * blocks].reshape(TILE, width)))
        normed = low(unit * wide(gain_ref[0:1, :]) + wide(shift_ref[0:1, :]))
        add_upper(0, dotf(gnq, normed, TN))
        dx = low(mid[...] + norm_back(gnormed, unit, scaled, wide(gain_ref[0:1, :])))
        if tile:
            fetches(tile - 1)[3].start()
        xr[tile * blocks : (tile + 1) * blocks] = dx.reshape(blocks, span, width)
        if not solo:
            for block in tile_blocks(tile):

                @pl.when(me != block)
                def _():
                    b_copy(block).start()

                @pl.when(me == block)
                def _():
                    own_b.start()

    part[0:RANK, 3 * width :] = ADAPTER_SCALE * part[0:RANK, 3 * width :]
    part[RANK : 2 * RANK, hidden:] = ADAPTER_SCALE * part[RANK : 2 * RANK, hidden:]
    if solo:
        total_ref[...] = part[...]
        return
    sum_everywhere(splits, copies, part, total_ref, *sum_refs)
    own_f.wait()
    own_b.wait()
    for slot, peer in enumerate(far + near):
        x_copy(peer, slot).wait_send()
        c_copy(peer, slot).wait_send()
        send(out_row.at[peer], output.at[peer], f_sent.at[peer], f_land.at[peer], "seq", peer).wait()
        send(xr.at[peer], dx_out.at[peer], b_sent.at[peer], b_land.at[peer], "seq", peer).wait()


def whole_block(splits, copies, solo, lengths, inputs, cotangent, small, weights):
    span, width = inputs.shape[1:]
    total = splits * span
    hidden = weights[2].shape[1]
    heads = 2 * width // LANES
    blocks = TILE // span
    anyspace = pl.BlockSpec(memory_space=pl.ANY)
    vmem = pl.BlockSpec(memory_space=pltpu.VMEM)
    bf, f32 = jnp.bfloat16, jnp.float32
    row = (splits, span, width)
    shapes = [
        (row, bf),
        (row, bf),
        ((2 * RANK, 8 * width), f32),
        (row, bf),
        (row, bf),
        ((heads // 2, total, LANES), bf),
        ((total, width), f32),
        ((total, hidden), bf),
        ((total, hidden), bf),
    ]
    dma = pltpu.SemaphoreType.DMA
    scratch = [
        *[pltpu.VMEM(w.shape, bf) for w in weights],
        pltpu.VMEM((heads, total, LANES), bf),
        pltpu.VMEM((heads, total, LANES), bf),
        pltpu.VMEM((heads, total, LANES), bf),
        pltpu.VMEM((heads // 2, total, LANES), f32),
        pltpu.VMEM((heads // 2, total, LANES), f32),
        pltpu.VMEM(row, bf),
        pltpu.VMEM((heads // 2, TILE, LANES), bf),
        pltpu.VMEM((TILE, width), f32),
        pltpu.VMEM((TILE, hidden), bf),
        pltpu.VMEM((TILE, hidden), bf),
        pltpu.VMEM((blocks, span, width), bf),
        pltpu.VMEM((blocks, span, width), bf),
        pltpu.VMEM((heads, TILE, LANES), bf),
        pltpu.VMEM((heads // 2, TILE, LANES), bf),
        pltpu.VMEM((total, LANES), bf),
        pltpu.VMEM((2 * RANK, 8 * width), f32),
        pltpu.VMEM((1, small[0].size), f32),
        *adapter_scratch(width, hidden),
        dma((4,)),
        dma((5,)),
        dma((4 + blocks,)),
        dma((3,)),
        *[dma((splits,)) for _ in range(8)],
    ]
    if not solo:
        scratch += sum_scratch(splits, copies, 8 * width)
    return pl.pallas_call(
        lambda *refs: block_kernel(splits, copies, solo, *refs),
        out_shape=[jax.ShapeDtypeStruct(s, d) for s, d in shapes],
        in_specs=[pl.BlockSpec(memory_space=pltpu.SMEM)] + [anyspace] * 6 + [vmem] * len(small),
        out_specs=[anyspace, anyspace, vmem] + [anyspace] * 6,
        scratch_shapes=scratch,
        compiler_params=pltpu.CompilerParams(
            collective_id=None if solo else 4, has_side_effects=not solo, vmem_limit_bytes=64 * 2**20 - 2**18
        ),
        name="block",
    )(lengths, inputs, cotangent, *weights, *small)[:3]


def local_by_heads(
    inputs,
    cotangent,
    lengths,
    norm_gain,
    norm_shift,
    query_key_value_weight,
    output_projection_weight,
    first_feedforward_weight,
    second_feedforward_weight,
    biases,
    down_model,
    down_hidden,
    query_key_value_upward,
    hidden_adapter_upward,
    model_adapter_upward,
    row_down_model,
    col_down_model,
    row_down_hidden,
    col_down_hidden,
    row_up_qkv,
    col_up_qkv,
    row_up_hidden,
    col_up_hidden,
    row_up_model,
    col_up_model,
):
    rows, span, width = inputs.shape
    hidden_width = first_feedforward_weight.shape[1]
    count = rows * span
    spots = lax.axis_index("seq") * span + jnp.arange(span)
    keep = (spots[None, :] < lengths[:, None]).astype(jnp.float32).reshape(count, 1)
    flat = inputs.reshape(count, width).astype(jnp.float32)
    shifts = biases.astype(jnp.float32)
    query_bias = shifts[0:width]
    value_bias = shifts[width : 2 * width]
    projection_bias = shifts[2 * width : 3 * width]
    expand_bias_vector = shifts[3 * width : 3 * width + hidden_width]
    contract_bias_vector = shifts[3 * width + hidden_width : 4 * width + hidden_width]
    query_key_value_bias = jnp.concatenate([query_bias, jnp.zeros_like(query_bias), value_bias])
    gains = norm_gain.astype(jnp.float32)
    offsets = norm_shift.astype(jnp.float32)
    down_low = down_model.astype(jnp.bfloat16)
    hidden_down_low = down_hidden.astype(jnp.bfloat16)
    qkv_up_low = query_key_value_upward.astype(jnp.bfloat16)
    hidden_up_low = hidden_adapter_upward.astype(jnp.bfloat16)
    model_up_low = model_adapter_upward.astype(jnp.bfloat16)
    normalized_rows, unit_first, scaled_first = normalize(flat, gains[0], offsets[0])
    normalized_rows = normalized_rows.astype(jnp.bfloat16)
    mixed_rows, narrow_qkv = adapted(
        normalized_rows, query_key_value_weight, query_key_value_bias, down_low[0], qkv_up_low
    )
    mixed_rows = mixed_rows.astype(jnp.bfloat16).reshape(rows, span, 3, HEADS, HEAD_DIM)
    by_head = lax.all_to_all(mixed_rows, "seq", split_axis=3, concat_axis=1, tiled=True)
    out_heads, lse = lax.map(partial(head_forward, False), (by_head, lengths))
    attended_rows = jax.tree.map(
        lambda part, own: part.astype(own.dtype),
        lax.all_to_all(as_sent(out_heads), "seq", split_axis=1, concat_axis=2, tiled=True),
        out_heads,
    )
    attended_rows = attended_rows.reshape(count, width)
    branch_path, narrow_proj = adapted(
        attended_rows, output_projection_weight, projection_bias, down_low[1], model_up_low[0]
    )
    middle = flat + branch_path
    normed_mid, unit_second, scaled_second = normalize(middle, gains[1], offsets[1])
    normed_mid = normed_mid.astype(jnp.bfloat16)
    before, narrow_expand = adapted(
        normed_mid, first_feedforward_weight, expand_bias_vector, down_low[2], hidden_up_low
    )
    activated, gelu_pull = jax.vjp(lambda value: jax.nn.gelu(value, approximate=True), before)
    activated = activated.astype(jnp.bfloat16)
    branch_out, narrow_contract = adapted(
        activated, second_feedforward_weight, contract_bias_vector, hidden_down_low, model_up_low[1]
    )
    output = (middle + branch_out).astype(jnp.bfloat16).reshape(rows, span, width)
    grad_out = cotangent.reshape(count, width).astype(jnp.float32) * keep
    grad_act, grad_down_contract, grad_up_contract = adapted_back(
        grad_out.astype(jnp.bfloat16),
        activated,
        second_feedforward_weight,
        hidden_down_low,
        model_up_low[1],
        narrow_contract,
    )
    grad_before = gelu_pull(grad_act)[0].astype(jnp.bfloat16)
    grad_norm_mid, grad_down_expand, grad_up_expand = adapted_back(
        grad_before, normed_mid, first_feedforward_weight, down_low[2], hidden_up_low, narrow_expand
    )
    grad_mid = grad_out + normalize_back(grad_norm_mid, unit_second, scaled_second, gains[1])
    grad_att, grad_down_proj, grad_up_proj = adapted_back(
        grad_mid.astype(jnp.bfloat16),
        attended_rows,
        output_projection_weight,
        down_low[1],
        model_up_low[0],
        narrow_proj,
    )
    grad_att = grad_att.astype(jnp.bfloat16).reshape(rows, span, HEADS, HEAD_DIM)
    grad_heads = lax.all_to_all(grad_att, "seq", split_axis=2, concat_axis=1, tiled=True)
    grad_triple = lax.map(partial(head_backward, False), (by_head, grad_heads, lse, lengths))
    grad_mixed = jax.tree.map(
        lambda part, own: part.astype(own.dtype),
        lax.all_to_all(as_sent(grad_triple), "seq", split_axis=1, concat_axis=3, tiled=True),
        grad_triple,
    )
    grad_mixed = grad_mixed.reshape(count, 3 * width)
    grad_normed, grad_down_qkv, grad_up_qkv = adapted_back(
        grad_mixed, normalized_rows, query_key_value_weight, down_low[0], qkv_up_low, narrow_qkv
    )
    input_grad = (
        (grad_mid + normalize_back(grad_normed, unit_first, scaled_first, gains[0]))
        .astype(jnp.bfloat16)
        .reshape(rows, span, width)
    )
    grads = lax.psum(
        (
            jnp.stack([grad_down_qkv, grad_down_proj, grad_down_expand]),
            grad_down_contract,
            grad_up_qkv,
            grad_up_expand,
            jnp.stack([grad_up_proj, grad_up_contract]),
        ),
        ("dp", "seq"),
    )
    grad_dm, grad_dh, grad_uq, grad_uh, grad_um = grads
    new_dm, row_dm, col_dm = factored(grad_dm, down_model, row_down_model, col_down_model)
    new_dh, row_dh, col_dh = factored(grad_dh, down_hidden, row_down_hidden, col_down_hidden)
    new_uq, row_uq, col_uq = factored(grad_uq, query_key_value_upward, row_up_qkv, col_up_qkv)
    new_uh, row_uh, col_uh = factored(grad_uh, hidden_adapter_upward, row_up_hidden, col_up_hidden)
    new_um, row_um, col_um = factored(grad_um, model_adapter_upward, row_up_model, col_up_model)
    return (
        output,
        input_grad,
        grad_dm,
        grad_dh,
        grad_uq,
        grad_uh,
        grad_um,
        new_dm,
        new_dh,
        new_uq,
        new_uh,
        new_um,
        row_dm,
        row_dh,
        row_uq,
        row_uh,
        row_um,
        col_dm,
        col_dh,
        col_uq,
        col_uh,
        col_um,
    )


def local_by_rows(
    pieces,
    copies,
    inputs,
    cotangent,
    lengths,
    norm_gain,
    norm_shift,
    query_key_value_weight,
    output_projection_weight,
    first_feedforward_weight,
    second_feedforward_weight,
    biases,
    down_model,
    down_hidden,
    query_key_value_upward,
    hidden_adapter_upward,
    model_adapter_upward,
    row_down_model,
    col_down_model,
    row_down_hidden,
    col_down_hidden,
    row_up_qkv,
    col_up_qkv,
    row_up_hidden,
    col_up_hidden,
    row_up_model,
    col_up_model,
):
    flip = lambda array: jnp.swapaxes(array, -1, -2)
    adapters = [
        flip(down_model),
        flip(down_hidden),
        query_key_value_upward,
        hidden_adapter_upward,
        model_adapter_upward,
    ]
    norms = [norm_gain, norm_shift]
    weights = [
        query_key_value_weight,
        output_projection_weight,
        first_feedforward_weight,
        second_feedforward_weight,
    ]
    output, input_grad, total = whole_block(
        pieces, copies, False, lengths, inputs, cotangent, [biases.reshape(-1, LANES)] + norms + adapters, weights
    )
    return update(
        total,
        output,
        input_grad,
        adapters,
        row_down_model,
        col_down_model,
        row_down_hidden,
        col_down_hidden,
        row_up_qkv,
        col_up_qkv,
        row_up_hidden,
        col_up_hidden,
        row_up_model,
        col_up_model,
    )


def local(pieces, copies, inputs, *others):
    if inputs.shape[0] == pieces and TILE % inputs.shape[1] == 0:
        return local_by_rows(pieces, copies, inputs, *others)
    return local_by_heads(inputs, *others)


def solution(mesh):
    placed = (
        P("dp", "seq", None),
        P("dp", "seq", None),
        P("dp"),
        P(),
        P(),
        P(),
        P(),
        P(),
        P(),
        P(),
        P(),
        P(),
        P(),
        P(),
        P(),
        P(),
        P(),
        P(),
        P(),
        P(),
        P(),
        P(),
        P(),
        P(),
        P(),
    )
    return jax.shard_map(
        partial(local, mesh.shape["seq"], mesh.shape["dp"]),
        mesh=mesh,
        in_specs=placed,
        out_specs=(
            P("dp", "seq", None),
            P("dp", "seq", None),
            P(),
            P(),
            P(),
            P(),
            P(),
            P(),
            P(),
            P(),
            P(),
            P(),
            P(),
            P(),
            P(),
            P(),
            P(),
            P(),
            P(),
            P(),
            P(),
            P(),
        ),
        check_vma=False,
    )
```
